128 devices in a mesh: head: 8 (over y, core), blk: 16 (over z, x).
Axes of the slice: x: 4, y: 4, z: 4, core: 2. Of those that a mesh axis runs over, the one named last changes fastest.
Arguments:
- tokens: bfloat16 [2, 8192, 2048], P(None, ('blk', 'head')), may hold values from -6 to 6
- cotangent: bfloat16 [2, 8192, 2048], P(None, ('blk', 'head')), may hold values from -6 to 6
- doc_lengths: int32 [2, 4], replicated, may hold values from 1 to 8189, as said below
- adapter_index: int32 [2, 1], replicated, may hold values from 0 to 1
- attn_gain: float32 [2048], replicated, may hold values from 0.25 to 1.75
- ffn_gain: float32 [2048], replicated, may hold values from 0.25 to 1.75
- w_qkv: bfloat16 [2048, 4096], P('blk', 'head'), may hold values from -0.125 to 0.125
- w_out: bfloat16 [2048, 2048], P('head', 'blk'), may hold values from -0.5 to 0.5
- w_gate: bfloat16 [2048, 8192], P('blk', 'head'), may hold values from -0.125 to 0.125
- w_up: bfloat16 [2048, 8192], P('blk', 'head'), may hold values from -0.125 to 0.125
- w_down: bfloat16 [8192, 2048], P('head', 'blk'), may hold values from -0.0625 to 0.0625
- qkv_in: bfloat16 [2, 2048, 16], replicated, may hold values from -0.125 to 0.125
- qkv_out: bfloat16 [2, 16, 4096], replicated, may hold values from -1 to 1
- attn_in: bfloat16 [2, 2048, 16], replicated, may hold values from -0.5 to 0.5
- attn_out: bfloat16 [2, 16, 2048], replicated, may hold values from -1 to 1
- gate_in: bfloat16 [2, 2048, 16], replicated, may hold values from -0.125 to 0.125
- gate_out: bfloat16 [2, 16, 8192], replicated, may hold values from -1 to 1
- up_in: bfloat16 [2, 2048, 16], replicated, may hold values from -0.125 to 0.125
- up_out: bfloat16 [2, 16, 8192], replicated, may hold values from -1 to 1
- down_in: bfloat16 [2, 8192, 16], replicated, may hold values from -0.0625 to 0.0625
- down_out: bfloat16 [2, 16, 2048], replicated, may hold values from -1 to 1
Outputs:
- result: float32 [2, 8192, 2048], P(None, ('blk', 'head'))
- input_grad: float32 [2, 8192, 2048], P(None, ('blk', 'head'))
- qkv_in_grad: float32 [2, 2048, 16], replicated
- qkv_out_grad: float32 [2, 16, 4096], replicated
- attn_in_grad: float32 [2, 2048, 16], replicated
- attn_out_grad: float32 [2, 16, 2048], replicated
- gate_in_grad: float32 [2, 2048, 16], replicated
- gate_out_grad: float32 [2, 16, 8192], replicated
- up_in_grad: float32 [2, 2048, 16], replicated
- up_out_grad: float32 [2, 16, 8192], replicated
- down_in_grad: float32 [2, 8192, 16], replicated
- down_out_grad: float32 [2, 16, 2048], replicated
The draws below stay inside these ranges and needn't reach their ends.
Inputs may be any that keep to these rules, and one draw needn't show every extreme that they name: `doc_lengths`: each row sums to 8192. `adapter_index`: every adapter is named by some sequence.
All inputs are finite; a program needn't handle non-finite values.
Results may differ from the reference program's by a relative error of at most 0.025.
Values may be sent and summed in bfloat16 or wider, within the bound.
A program may use at most 192 MiB of HBM per device.

```python
from functools import partial
import jax
import jax.numpy as jnp
from jax import lax

D = 2048
QUERY_HEADS = 16
KEY_VALUE_HEADS = 8
HEAD_SIZE = 128
FF = 8192
RANK = 16
NADAPT = 2
SEQS = 2
SEQUENCE_LENGTH = 8192
ATTENTION_WINDOW = 1024
NDOC = 4
QKV = 4096
QD = 2048


def draw_doc_lengths(key, part):
    key = jax.random.fold_in(key, 11)
    first_key, second_key = jax.random.split(key)
    share = jax.random.randint(first_key, (SEQS, NDOC), 1, 9)
    spare = SEQUENCE_LENGTH - NDOC
    base_weight = share * spare // jnp.sum(share, axis=1, keepdims=True)
    rest = spare - jnp.sum(base_weight, axis=1, keepdims=True)
    ending = (jnp.arange(NDOC) == NDOC - 1).astype(jnp.int32)
    lengths = 1 + base_weight + rest * ending[None, :]
    chosen = jax.random.randint(second_key, (), 0, SEQS)
    special = 1 + spare * (jnp.arange(NDOC) == 0).astype(jnp.int32)
    picked = jnp.arange(SEQS)[:, None] == chosen
    return jnp.where(picked, special[None, :], lengths).astype(jnp.int32)


def block_scale(rng, extent, cuts, low, largest):
    level, own = 1.0, jax.random.fold_in(rng, 6)
    for axis_at, blocks in cuts:
        steps = jnp.exp(jax.random.uniform(jax.random.fold_in(own, axis_at), (blocks,), jnp.float32, low / len(cuts), largest / len(cuts)))
        level = level * jnp.repeat(steps, extent[axis_at] // blocks).reshape([-1 if axis == axis_at else 1 for axis in range(len(extent))])
    return level


def choose_distinct(stream_key, rows, count, top, lift):
    ranking = jax.random.permutation(jax.random.fold_in(stream_key, 1), count)
    favour = ranking
    for power in range(3):
        favour = favour * favour // count
    favour = favour * lift // count
    chance = jax.random.randint(jax.random.fold_in(stream_key, 2), (rows, count), 0, 4096) + favour
    sure = jax.random.permutation(jax.random.fold_in(stream_key, 3), rows)[jnp.arange(count) % rows]
    chance = jnp.where(jnp.arange(rows)[:, None] == sure[None, :], 1 << 14, chance)
    merit = chance * count + jnp.arange(count)
    return lax.top_k(merit.astype(jnp.int32), top)[1].astype(jnp.int32)


def bell_draw(rng, shape, spread, bound, shards=(), kind=jnp.bfloat16):
    array = jax.random.normal(rng, shape, jnp.float32) * spread
    if len(shards) > 0:
        array = block_scale(rng, shape, shards, -0.22, 0.18) * array
    return jnp.clip(array, min=-bound, max=bound).astype(kind)


def setup_inputs(seed: int = 0) -> dict:
    streams_of = jax.random.split(jax.random.key(seed), 22)
    return {
        "tokens": bell_draw(streams_of[0], (SEQS, SEQUENCE_LENGTH, D), 1.0, 6.0, ((1, 128),)),
        "cotangent": bell_draw(streams_of[1], (SEQS, SEQUENCE_LENGTH, D), 1.0, 6.0, ((1, 128),)),
        "doc_lengths": draw_doc_lengths(jax.random.fold_in(streams_of[21], 71), 0),
        "adapter_index": choose_distinct(streams_of[3], SEQS, NADAPT, 1, 0),
        "attn_gain": jnp.clip(1.0 + 0.15 * jax.random.normal(streams_of[4], (D,), jnp.float32), 0.25, 1.75),
        "ffn_gain": jnp.clip(1.0 + 0.15 * jax.random.normal(streams_of[5], (D,), jnp.float32), 0.25, 1.75),
        "w_qkv": bell_draw(streams_of[6], (D, QKV), D ** -0.5, 0.125, ((0, 16), (1, 8))),
        "w_out": bell_draw(streams_of[7], (QD, D), (QD // 16) ** -0.5, 0.5, ((0, 8), (1, 16))),
        "w_gate": bell_draw(streams_of[8], (D, FF), D ** -0.5, 0.125, ((0, 16), (1, 8))),
        "w_up": bell_draw(streams_of[9], (D, FF), D ** -0.5, 0.125, ((0, 16), (1, 8))),
        "w_down": bell_draw(streams_of[10], (FF, D), FF ** -0.5, 0.0625, ((0, 8), (1, 16))),
        "qkv_in": bell_draw(streams_of[11], (NADAPT, D, RANK), D ** -0.5, 0.125),
        "qkv_out": bell_draw(streams_of[12], (NADAPT, RANK, QKV), (2 * RANK) ** -0.5, 1.0),
        "attn_in": bell_draw(streams_of[13], (NADAPT, QD, RANK), (QD // 16) ** -0.5, 0.5),
        "attn_out": bell_draw(streams_of[14], (NADAPT, RANK, D), (2 * RANK) ** -0.5, 1.0),
        "gate_in": bell_draw(streams_of[15], (NADAPT, D, RANK), D ** -0.5, 0.125),
        "gate_out": bell_draw(streams_of[16], (NADAPT, RANK, FF), (2 * RANK) ** -0.5, 1.0),
        "up_in": bell_draw(streams_of[17], (NADAPT, D, RANK), D ** -0.5, 0.125),
        "up_out": bell_draw(streams_of[18], (NADAPT, RANK, FF), (2 * RANK) ** -0.5, 1.0),
        "down_in": bell_draw(streams_of[19], (NADAPT, FF, RANK), FF ** -0.5, 0.0625),
        "down_out": bell_draw(streams_of[20], (NADAPT, RANK, D), (2 * RANK) ** -0.5, 1.0),
    }


EPS = 1e-05
THETA = 1000000.0
HIGH_PRECISION = lax.Precision.HIGHEST

@jax.custom_vjp
def low(v):
    return lax.optimization_barrier(v.astype(jnp.bfloat16)).astype(jnp.float32)

@jax.custom_vjp
def low_back(v):
    return v

def low_keep(v):
    return (low(v), None)

def low_pass(kept, gradient_value):
    return (gradient_value,)

def back_keep(v):
    return (v, None)

def back_low(kept, gradient_value):
    return (low(gradient_value),)
low.defvjp(low_keep, low_pass)
low_back.defvjp(back_keep, back_low)

def matmul(left, right):
    return jnp.dot(left, right, precision=HIGH_PRECISION)

def rms_scale(value_rows, gain):
    return value_rows * lax.rsqrt(lax.optimization_barrier(jnp.mean(value_rows * value_rows, axis=-1, keepdims=True)) + EPS) * gain

def rotate(value_rows, where):
    half = value_rows.shape[-1] // 2
    inverse = THETA ** (-(jnp.arange(half, dtype=jnp.float32) * 2.0 / value_rows.shape[-1]))
    angle = where[..., None] * inverse
    cosine = jnp.concatenate([jnp.cos(angle), jnp.cos(angle)], axis=-1)
    sine = jnp.concatenate([jnp.sin(angle), jnp.sin(angle)], axis=-1)
    turned = jnp.concatenate([-value_rows[..., half:], value_rows[..., :half]], axis=-1)
    return value_rows * cosine + turned * sine

def doc_place(lengths, where):
    ends = jnp.cumsum(lengths, axis=-1)
    after = where[..., :, None] >= ends[..., None, :]
    number = lax.optimization_barrier(jnp.sum(after.astype(jnp.int32), axis=-1))
    start = lax.optimization_barrier(jnp.sum(jnp.where(after, lengths[..., None, :], 0), axis=-1))
    return (number, start)

def attend(queries, key_rows, value_rows, doc, lengths_row):
    block = min(512, SEQUENCE_LENGTH)
    query_groups = QUERY_HEADS // KEY_VALUE_HEADS
    key_padded_rows = jnp.concatenate([jnp.zeros((ATTENTION_WINDOW, KEY_VALUE_HEADS, HEAD_SIZE), jnp.float32), key_rows], axis=0)
    value_padded_rows = jnp.concatenate([jnp.zeros((ATTENTION_WINDOW, KEY_VALUE_HEADS, HEAD_SIZE), jnp.float32), value_rows], axis=0)

    def one_block(first):
        query_part = lax.dynamic_slice_in_dim(queries, first, block, 0)
        key_part = lax.dynamic_slice_in_dim(key_padded_rows, first, ATTENTION_WINDOW + block, 0)
        value_part = lax.dynamic_slice_in_dim(value_padded_rows, first, ATTENTION_WINDOW + block, 0)
        query_pos = first + jnp.arange(block, dtype=jnp.int32)
        key_pos = first - ATTENTION_WINDOW + jnp.arange(ATTENTION_WINDOW + block, dtype=jnp.int32)
        query_doc = lax.dynamic_slice_in_dim(doc, first, block, 0)
        key_doc, unused = doc_place(lengths_row, key_pos)
        gap = query_pos[:, None] - key_pos[None, :]
        allowed = (gap >= 0) & (gap < ATTENTION_WINDOW) & (key_pos[None, :] >= 0) & (query_doc[:, None] == key_doc[None, :])
        scores = low_back(jnp.einsum('qkgh,jkh->kgqj', query_part, key_part, precision=HIGH_PRECISION))
        scores = jnp.where(allowed[None, None], scores, -jnp.inf)
        top = lax.optimization_barrier(jnp.max(scores, axis=-1, keepdims=True))
        expo = jnp.exp(scores - top)
        probs = low(expo / lax.optimization_barrier(jnp.sum(expo, axis=-1, keepdims=True)))
        return jnp.einsum('kgqj,jkh->qkgh', probs, value_part, precision=HIGH_PRECISION)
    starts = jnp.arange(SEQUENCE_LENGTH // block, dtype=jnp.int32) * block
    output_rows = lax.map(jax.checkpoint(one_block), starts)
    return output_rows.reshape(SEQUENCE_LENGTH, KEY_VALUE_HEADS * query_groups * HEAD_SIZE)

def seq_layer(row, lengths_row, hot, adapters, frozen):
    attn_gain, ffn_gain, w_qkv, w_out, w_gate, w_up, w_down = frozen
    picked = [jnp.tensordot(hot, table, axes=1, precision=HIGH_PRECISION) for table in adapters]
    qkv_in, qkv_out, attn_in, attn_out, gate_in, gate_out, up_in, up_out, down_in, down_out = picked
    query_groups = QUERY_HEADS // KEY_VALUE_HEADS
    scale = HEAD_SIZE ** (-0.5)
    normed = low(rms_scale(row, attn_gain))
    unscaled_input = low_back(matmul(normed, w_qkv) + matmul(matmul(normed, qkv_in), qkv_out))
    reshaped_rows = unscaled_input.reshape(SEQUENCE_LENGTH, KEY_VALUE_HEADS, query_groups + 2, HEAD_SIZE)
    place = jnp.arange(SEQUENCE_LENGTH, dtype=jnp.int32)
    doc, start = doc_place(lengths_row, place)
    inside = (place - start).astype(jnp.float32)
    queries = low(rotate(reshaped_rows[:, :, :query_groups], inside[:, None, None]) * scale)
    key_rows = low(rotate(reshaped_rows[:, :, query_groups], inside[:, None]))
    value_rows = low(reshaped_rows[:, :, query_groups + 1])
    attn = low(low_back(attend(queries, key_rows, value_rows, doc, lengths_row)))
    middle = row + low_back(matmul(attn, w_out) + matmul(matmul(attn, attn_in), attn_out))
    mid_normed = low(rms_scale(middle, ffn_gain))
    gate = low_back(matmul(mid_normed, w_gate) + matmul(matmul(mid_normed, gate_in), gate_out))
    up = low_back(matmul(mid_normed, w_up) + matmul(matmul(mid_normed, up_in), up_out))
    hidden = low(gate * jax.nn.sigmoid(gate) * up)
    return middle + low_back(matmul(hidden, w_down) + matmul(matmul(hidden, down_in), down_out))

def reference(tokens, cotangent, doc_lengths, adapter_index, attn_gain, ffn_gain, w_qkv, w_out, w_gate, w_up, w_down, qkv_in, qkv_out, attn_in, attn_out, gate_in, gate_out, up_in, up_out, down_in, down_out):
    frozen = (attn_gain.astype(jnp.float32), ffn_gain.astype(jnp.float32)) + tuple((table.astype(jnp.float32) for table in (w_qkv, w_out, w_gate, w_up, w_down)))
    adapters = tuple((table.astype(jnp.float32) for table in (qkv_in, qkv_out, attn_in, attn_out, gate_in, gate_out, up_in, up_out, down_in, down_out)))
    onehot = (adapter_index[:, 0:1] == jnp.arange(NADAPT, dtype=jnp.int32)[None, :]).astype(jnp.float32)
    layer = jax.checkpoint(partial(seq_layer, frozen=frozen))

    def forward(input_rows, tables):

        def advance(carry, item):
            row, lengths_row, hot = item
            return (carry, layer(row, lengths_row, hot, tables))
        unused, output_rows = lax.scan(advance, jnp.zeros((), jnp.float32), (input_rows, doc_lengths, onehot))
        return output_rows
    result, pullback = jax.vjp(forward, tokens.astype(jnp.float32), adapters)
    input_grad, table_grads = pullback(cotangent.astype(jnp.float32))
    return (result, input_grad, table_grads[0], table_grads[1], table_grads[2], table_grads[3], table_grads[4], table_grads[5], table_grads[6], table_grads[7], table_grads[8], table_grads[9])
```

```python
from functools import partial

import jax
import jax.numpy as jnp
from jax import lax
from jax.experimental import pallas as pl
from jax.experimental.pallas import tpu as pltpu
from jax.sharding import PartitionSpec as P

MESH = pl.DeviceIdType.MESH
BF = jnp.bfloat16
F32 = jnp.float32
D = 2048
EXT = 128
CW = D + EXT
RANK = 16
WINDOW = 1024
EPS = 1e-05
THETA = 1000000.0
Y, CORES, Z, X = 4, 2, 4, 4
TOK = 64
SPAN = 512
SCALE = 128 ** (-0.5)


def mm(a, b):
    return jnp.dot(a, b, preferred_element_type=F32)


def mm_nt(a, b):
    return lax.dot_general(a, b, (((1,), (1,)), ((), ())), preferred_element_type=F32)


def mm_tn(a, b):
    return lax.dot_general(a, b, (((0,), (0,)), ((), ())), preferred_element_type=F32)


class Place:
    def __init__(self):
        h = lax.axis_index("head")
        b = lax.axis_index("blk")
        self.h, self.b = h, b
        self.y, self.c = h // 2, h % 2
        self.z, self.x = b // 4, b % 4
        y, c, z, x = self.y, self.c, self.z, self.x
        self.yu, self.yd, self.yo = (y + 1) % 4, (y + 3) % 4, (y + 2) % 4
        self.xu, self.xd = (x + 1) % 4, (x + 3) % 4
        self.zu, self.zd = (z + 1) % 4, (z + 3) % 4
        self.sib = (y * 2 + (1 - c), b)
        self.yp, self.ym = (self.yu * 2 + c, b), (self.yd * 2 + c, b)
        self.xp, self.xm = (h, z * 4 + self.xu), (h, z * 4 + self.xd)
        self.zp, self.zm = (h, self.zu * 4 + x), (h, self.zd * 4 + x)
        self.next1, self.next2 = (h, (b + 1) % 16), (h, (b + 2) % 16)
        self.prev1, self.prev2 = (h, (b + 15) % 16), (h, (b + 14) % 16)

    def greet(self, peers):
        barrier = pltpu.get_barrier_semaphore()
        for peer in peers:
            pl.semaphore_signal(barrier, inc=1, device_id=peer, device_id_type=MESH)
        pl.semaphore_wait(barrier, len(peers))


class Net:
    def __init__(self, send, recv):
        self.send, self.recv, self.count, self.copies = send, recv, 0, []

    def push(self, src, dst, peer):
        i = self.count
        self.count += 1
        copy = pltpu.make_async_remote_copy(
            src_ref=src,
            dst_ref=dst,
            send_sem=self.send.at[i],
            recv_sem=self.recv.at[i],
            device_id=peer,
            device_id_type=MESH,
        )
        copy.start()
        self.copies.append(copy)
        return copy

    def settle(self, copies):
        for copy in copies:
            copy.wait_send()
            self.copies = [other for other in self.copies if other is not copy]

    def drain(self):
        self.settle(list(self.copies))


class Gather:
    def __init__(self, net, at, buf, s):
        self.net, self.at, self.buf, self.s = net, at, buf, s
        own = buf.at[s, at.h]
        self.up = net.push(own, own, at.yp)
        self.down = net.push(own, own, at.ym)
        self.side = [net.push(own, own, at.sib)]

    def relay(self):
        at, net = self.at, self.net
        below = self.buf.at[self.s, at.yd * 2 + at.c]
        above = self.buf.at[self.s, at.yu * 2 + at.c]
        self.up.wait_recv()
        part = below.at[pl.ds(0, TOK // 2)]
        self.far_a = net.push(part, part, at.yp)
        self.side.append(net.push(below, below, at.sib))
        self.down.wait_recv()
        part = above.at[pl.ds(TOK // 2, TOK // 2)]
        self.far_b = net.push(part, part, at.ym)
        self.side.append(net.push(above, above, at.sib))

    def last(self):
        at, net = self.at, self.net
        far = self.buf.at[self.s, at.yo * 2 + at.c]
        self.far_a.wait_recv()
        part = far.at[pl.ds(0, TOK // 2)]
        self.side.append(net.push(part, part, at.sib))
        self.far_b.wait_recv()
        part = far.at[pl.ds(TOK // 2, TOK // 2)]
        self.side.append(net.push(part, part, at.sib))

    def done(self):
        for copy in self.side:
            copy.wait_recv()

    def settle(self):
        self.net.settle([self.up, self.down, self.far_a, self.far_b] + self.side)


class Scatter:
    def __init__(self, net, at, part, s, bufs):
        self.net, self.at, self.part, self.s = net, at, part, s
        self.sibr, self.ra, self.rb, self.fp, self.fm = bufs
        self.side = net.push(part.at[s, :, 1 - at.c], self.sibr.at[s], at.sib)

    def _merge(self, y):
        at, s = self.at, self.s
        self.part[s, y, at.c] = (
            self.part[s, y, at.c].astype(F32) + self.sibr[s, y].astype(F32)
        ).astype(BF)

    def merge(self):
        at, net, s = self.at, self.net, self.s
        self.side.wait_recv()
        self._merge(at.yo)
        far = self.part.at[s, at.yo, at.c]
        self.a = net.push(far.at[pl.ds(0, TOK // 2)], self.ra.at[s], at.yp)
        self.b = net.push(far.at[pl.ds(TOK // 2, TOK // 2)], self.rb.at[s], at.ym)
        self._merge(at.yu)
        self._merge(at.yd)

    def relay(self):
        at, net, s = self.at, self.net, self.s
        self.a.wait_recv()
        half = pl.ds(0, TOK // 2)
        self.part[s, at.yu, at.c, half] = (
            self.part[s, at.yu, at.c, half].astype(F32) + self.ra[s].astype(F32)
        ).astype(BF)
        self.up = net.push(self.part.at[s, at.yu, at.c], self.fp.at[s], at.yp)
        self.b.wait_recv()
        half = pl.ds(TOK // 2, TOK // 2)
        self.part[s, at.yd, at.c, half] = (
            self.part[s, at.yd, at.c, half].astype(F32) + self.rb[s].astype(F32)
        ).astype(BF)
        self.down = net.push(self.part.at[s, at.yd, at.c], self.fm.at[s], at.ym)

    def done(self):
        at, s = self.at, self.s
        self.up.wait_recv()
        self.down.wait_recv()
        self.net.settle([self.side, self.a, self.b, self.up, self.down])
        return (
            self.part[s, at.y, at.c].astype(F32) + self.sibr[s, at.y].astype(F32)
        ) + (self.fp[s].astype(F32) + self.fm[s].astype(F32))


class Weight:
    def __init__(self, net, at, ref, by_row):
        self.net, self.at, self.ref, self.by_row = net, at, ref, by_row
        self.rows, self.cols = ref.shape[1], ref.shape[2]
        self.state = [{}, {}]

    def sub(self, half, z, x, part):
        at = pl.ds(pl.multiple_of(x * 128, 128), 128)
        if self.by_row:
            width = self.cols // 2
            cols = pl.ds(half * width, width)
            if part is None:
                return self.ref.at[z, at, cols]
            return self.ref.at[z, pl.ds(pl.multiple_of(x * 128 + part * 64, 64), 64), cols]
        height = self.rows // 2
        if part is None:
            rows = pl.ds(half * height, height)
        else:
            rows = pl.ds(half * height + part * (height // 2), height // 2)
        return self.ref.at[z, rows, at]

    def block(self, half, index, part):
        if half == 0:
            if self.by_row:
                cols = pl.ds(0, self.cols // 2)
                rows = pl.ds(0, 512) if part is None else pl.ds(part * 256, 256)
                return self.ref.at[index, rows, cols]
            height = self.rows // 2
            rows = (
                pl.ds(0, height) if part is None else pl.ds(part * (height // 2), height // 2)
            )
            return self.ref.at[index, rows, pl.ds(0, 512)]
        zs = pl.ds(0, 4) if part is None else pl.ds(part * 2, 2)
        at = pl.ds(pl.multiple_of(index * 128, 128), 128)
        if self.by_row:
            return self.ref.at[zs, at, pl.ds(self.cols // 2, self.cols // 2)]
        return self.ref.at[zs, pl.ds(self.rows // 2, self.rows // 2), at]

    def _near(self, half, off, part):
        at = self.at
        if half == 0:
            return self.sub(0, at.z, (at.x + off) % 4, part)
        return self.sub(1, (at.z + off) % 4, at.x, part)

    def _far(self, half, off, part):
        at = self.at
        return self.block(half, ((at.z if half == 0 else at.x) + off) % 4, part)

    def _peers(self, half, first):
        at = self.at
        return (at.xp, at.xm) if (half == 0) == first else (at.zp, at.zm)

    def _round(self, k):
        for half in (0, 1):
            st = self.state[half]
            up, down = self._peers(half, k <= 2)
            if k == 1:
                ref = self._near(half, 0, None)
                st["u"], st["d"] = self.net.push(ref, ref, up), self.net.push(ref, ref, down)
            elif k == 2:
                st["u"].wait_recv()
                ref = self._near(half, 3, 0)
                st["fu"] = self.net.push(ref, ref, up)
                st["d"].wait_recv()
                ref = self._near(half, 1, 1)
                st["fd"] = self.net.push(ref, ref, down)
            elif k == 3:
                st["fu"].wait_recv()
                st["fd"].wait_recv()
                ref = self._far(half, 0, None)
                st["u"], st["d"] = self.net.push(ref, ref, up), self.net.push(ref, ref, down)
            elif k == 4:
                st["u"].wait_recv()
                ref = self._far(half, 3, 0)
                st["fu"] = self.net.push(ref, ref, up)
                st["d"].wait_recv()
                ref = self._far(half, 1, 1)
                st["fd"] = self.net.push(ref, ref, down)
            else:
                st["fu"].wait_recv()
                st["fd"].wait_recv()

    def step(self, k):
        self._round(k)


def rows_of(m):
    return pl.ds(pl.multiple_of(m * 256, 256), 256)


def cols_of(n):
    return pl.ds(pl.multiple_of(n * 512, 512), 512)


def heads_of(buf, s, m):
    return buf[s, pl.ds(m * 4, 4)].reshape(256, buf.shape[-1])


def rms(v, gain):
    return v * lax.rsqrt(jnp.mean(v * v, axis=-1, keepdims=True) + EPS) * gain


def rms_back(v, gain, grad):
    scale = lax.rsqrt(jnp.mean(v * v, axis=-1, keepdims=True) + EPS)
    scaled = gain * grad
    return scaled * scale - v * (
        jnp.mean(v * scaled, axis=-1, keepdims=True) * scale * scale * scale
    )


def put_part(part, s, m, z, value):
    part[s, pl.ds(m * 2, 2), :, :, cols_of(z)] = value.astype(BF).reshape(2, 2, TOK, 512)


def put_ext(part, s, pieces):
    part[s, :, :, :, D:] = jnp.zeros((4, 2, TOK, EXT), BF)
    for i, piece in enumerate(pieces):
        part[s, :, :, :, D + i * RANK : D + (i + 1) * RANK] = piece.astype(BF).reshape(
            4, 2, TOK, RANK
        )


def put_rows(buf, s, h, value, pieces):
    buf[s, h, :, :D] = value
    buf[s, h, :, D:] = jnp.zeros((TOK, EXT), BF)
    for i, piece in enumerate(pieces):
        buf[s, h, :, D + i * RANK : D + (i + 1) * RANK] = piece.astype(BF)


def grid_loop(m_count, n_count, body):
    def step(i, carry):
        body(i // n_count, i % n_count)
        return carry

    lax.fori_loop(0, m_count * n_count, step, 0)


def front(
    index_ref, length_ref,
    tok, cot, again, fgain, inv,
    wq, wo, wg, wu, wd,
    qin, gin, uin, aout, dout, ain, din, qout, gout, uout,
    result_o, mgrad_o, bgrad_o, q_o, kv_o, attn_o, lse_o, cos_o, sin_o, start_o, wq_o, wo_o,
    normed_o, next_o, g_go_o, g_uo_o, g_di_o, g_gi_o, g_ui_o, g_ao_o, g_do_o,
    w_q, w_o, w_g, w_u, w_d,
    nb, cb, part1, part2, sib1, sib2, ra1, rb1, fp1, fm1, ra2, rb2, fp2, fm2,
    gate, up, hidden, qb, kvb, attn, lse, cosb, sinb, startb,
    midf, normed, midn, inner_a, bgrad, mgrad, result, next_s,
    a_b, d_b, q_b, g_b, u_b,
    g_go, g_uo, g_di, g_gi, g_ui, g_ao, g_do,
    send, recv, local,
):
    at = Place()
    net = Net(send, recv)
    pick = [index_ref[0, 0], index_ref[1, 0]]
    h, b = at.h, at.b

    here = pl.ds(pl.multiple_of(at.x * 128, 128), 128)
    loads = []

    def load(src, dst):
        copy = pltpu.make_async_copy(src, dst, local.at[len(loads)])
        copy.start()
        loads.append(copy)
        return copy

    load(wq, w_q.at[at.z, here, :])
    load(wo, w_o.at[at.z, :, here])
    load(wg, w_g.at[at.z, here, :])
    load(wu, w_u.at[at.z, here, :])
    load(wd, w_d.at[at.z, :, here])
    load(ain.at[:, :, pl.ds(pl.multiple_of(h * 256, 256), 256)], a_b)
    load(din.at[:, :, pl.ds(pl.multiple_of(h * 1024, 1024), 1024)], d_b)
    load(qout.at[:, :, pl.ds(pl.multiple_of(h * 512, 512), 512)], q_b)
    load(gout.at[:, :, pl.ds(pl.multiple_of(h * 1024, 1024), 1024)], g_b)
    load(uout.at[:, :, pl.ds(pl.multiple_of(h * 1024, 1024), 1024)], u_b)

    at.greet(
        [at.sib, at.yp, at.ym, at.xp, at.xm, at.zp, at.zm]
        + [at.next1, at.next2, at.prev1, at.prev2]
    )
    for copy in loads:
        copy.wait()
    W_Q = Weight(net, at, w_q, True)
    W_O = Weight(net, at, w_o, False)
    W_G = Weight(net, at, w_g, True)
    W_U = Weight(net, at, w_u, True)
    W_D = Weight(net, at, w_d, False)

    W_Q.step(1)
    W_O.step(1)

    g_n = []
    for s in (0, 1):
        n = rms(tok[s].astype(F32), again[...]).astype(BF)
        normed[s] = n
        put_rows(nb, s, h, n, [mm_nt(n, qin[pick[s]])])
        g_n.append(Gather(net, at, nb, s))
    W_Q.step(2)
    W_O.step(2)
    W_G.step(1)

    sign = jnp.where(lax.broadcasted_iota(jnp.int32, (1, 128), 1) < 64, -1.0, 1.0)

    def table(s, m):
        rows = pl.ds(pl.multiple_of(m * 64, 64), 64)
        pos = b * SPAN + m * 64 + lax.broadcasted_iota(jnp.int32, (64, 1), 0)
        start = jnp.zeros((64, 1), jnp.int32)
        end = 0
        for d in range(4):
            length = length_ref[s, d]
            end = end + length
            start = start + jnp.where(pos >= end, length, 0)
        startb[s, rows] = start
        angle = (pos - start).astype(F32) * inv[...]
        cosb[s, rows] = jnp.cos(angle)
        sinb[s, rows] = jnp.sin(angle) * sign

    grid_loop(2, 8, table)
    g_n[0].relay()
    g_n[1].relay()
    W_Q.step(3)
    W_G.step(2)

    for s in (0, 1):
        put_rows(cb, s, h, cot[s], [mm_nt(cot[s], dout[pick[s]])])
    g_n[0].last()
    g_n[1].last()
    W_Q.step(4)
    W_O.step(3)
    g_c = [Gather(net, at, cb, s) for s in (0, 1)]
    g_n[0].done()
    g_n[1].done()
    W_Q.step(5)
    W_G.step(3)

    halos = []
    for s in (0, 1):

        def qkv(m, unused, s=s):
            x = heads_of(nb, s, m)
            r = mm(x[:, :D], w_q[...].reshape(D, 512)) + mm(x[:, D : D + RANK], q_b[pick[s]])
            rows = rows_of(m)
            c, sn = cosb[s, rows], sinb[s, rows]

            def rot(v):
                return v * c + pltpu.roll(v, 64, 1) * sn

            for j in (0, 1):
                qb[s, j, rows] = (rot(r[:, j * 128 : (j + 1) * 128]) * SCALE).astype(BF)
            own = pl.ds(pl.multiple_of(1024 + m * 256, 256), 256)
            kvb[s, 0, own] = rot(r[:, 256:384]).astype(BF)
            kvb[s, 1, own] = r[:, 384:512].astype(BF)

        grid_loop(2, 1, qkv)
        own = kvb.at[s, :, pl.ds(1024, 512)]
        halos.append(net.push(own, kvb.at[s, :, pl.ds(512, 512)], at.next1))
        halos.append(net.push(own, kvb.at[s, :, pl.ds(0, 512)], at.next2))
    next_s[...] = nb[:, :, :, D:]
    W_O.step(4)
    W_U.step(1)
    g_c[0].relay()
    g_c[1].relay()
    W_U.step(2)
    W_O.step(5)

    g_n[0].settle()
    g_n[1].settle()

    row = lax.broadcasted_iota(jnp.int32, (256, 1280), 0)
    col = lax.broadcasted_iota(jnp.int32, (256, 1280), 1)
    scat1 = []
    for s in (0, 1):
        halos[2 * s].wait_recv()
        halos[2 * s + 1].wait_recv()

        def attend(g, m, s=s):
            rows = rows_of(m)
            keys = pl.ds(pl.multiple_of(m * 256, 256), 1280)
            sc = mm_nt(qb[s, g, rows], kvb[s, 0, keys])
            low = startb[s, rows] - (b * SPAN - WINDOW + m * 256)
            gap = row - col + WINDOW
            ok = (gap >= 0) & (gap < WINDOW) & (col >= low)
            sc = jnp.where(ok, sc, -1e30)
            top = jnp.max(sc, axis=-1, keepdims=True)
            e = jnp.exp(sc - top)
            total = jnp.sum(e, axis=-1, keepdims=True)
            p = (e * (1.0 / total)).astype(BF)
            o = mm(p, kvb[s, 1, keys])
            attn[s, rows, pl.ds(pl.multiple_of(g * 128, 128), 128)] = o.astype(BF)
            lse[s, g, rows] = top + jnp.log(total)

        grid_loop(2, 2, attend)
        if s == 0:
            g_c[0].last()
            g_c[1].last()
            W_G.step(4)

        def out_proj(m, z, s=s):
            put_part(part1, s, m, z, mm(attn[s, rows_of(m)], w_o[z]))

        grid_loop(2, 4, out_proj)
        put_ext(part1, s, [mm_nt(attn[s], a_b[pick[s]])])
        scat1.append(Scatter(net, at, part1, s, (sib1, ra1, rb1, fp1, fm1)))
        if s == 0:
            W_U.step(3)
    g_c[0].done()
    g_c[1].done()
    scat1[0].merge()
    scat1[1].merge()
    scat1[0].relay()
    scat1[1].relay()
    W_G.step(5)
    W_D.step(1)

    g_m = []
    for s in (0, 1):
        t = scat1[s].done()
        inn = t[:, D : D + RANK]
        inner_a[s] = inn
        mid = tok[s].astype(F32) + t[:, :D] + mm(inn.astype(BF), aout[pick[s]])
        midf[s] = mid
        n = rms(mid, fgain[...]).astype(BF)
        midn[s] = n
        put_rows(nb, s, h, n, [mm_nt(n, gin[pick[s]]), mm_nt(n, uin[pick[s]])])
        g_m.append(Gather(net, at, nb, s))
    W_U.step(4)
    W_D.step(2)
    g_m[0].relay()
    g_m[1].relay()
    W_D.step(3)
    g_m[0].last()
    g_m[1].last()
    W_U.step(5)
    g_m[0].done()
    g_m[1].done()
    W_D.step(4)

    for s in (0, 1):

        def ffn(m, n, s=s):
            x = heads_of(nb, s, m)
            rows, cols = rows_of(m), cols_of(n)
            g = mm(x[:, :D], w_g[:, :, cols].reshape(D, 512))
            g = g + mm(x[:, D : D + RANK], g_b[pick[s], :, cols])
            u = mm(x[:, :D], w_u[:, :, cols].reshape(D, 512))
            u = u + mm(x[:, D + RANK : D + 2 * RANK], u_b[pick[s], :, cols])
            gate[s, rows, cols] = g.astype(BF)
            up[s, rows, cols] = u.astype(BF)
            hidden[s, rows, cols] = (g * jax.nn.sigmoid(g) * u).astype(BF)

        grid_loop(2, 2, ffn)
    W_D.step(5)

    scat3 = []
    for s in (0, 1):

        def hid_back(m, n, s=s):
            x = heads_of(cb, s, m)
            rows, cols = rows_of(m), cols_of(n)
            hb = mm(x[:, D : D + RANK], d_b[pick[s], :, cols])
            for z in range(4):
                hb = hb + mm_nt(x[:, z * 512 : (z + 1) * 512], w_d[z, cols, :])
            g = gate[s, rows, cols].astype(F32)
            u = up[s, rows, cols].astype(F32)
            sg = jax.nn.sigmoid(g)
            gate[s, rows, cols] = (hb * u * sg * (1.0 + g * (1.0 - sg))).astype(BF)
            up[s, rows, cols] = (hb * g * sg).astype(BF)

        grid_loop(2, 2, hid_back)

        def mid_back(m, z, s=s):
            rows = rows_of(m)
            r = mm_nt(gate[s, rows], w_g[z]) + mm_nt(up[s, rows], w_u[z])
            put_part(part1, s, m, z, r)

        grid_loop(2, 4, mid_back)
        put_ext(part1, s, [mm_nt(gate[s], g_b[pick[s]]), mm_nt(up[s], u_b[pick[s]])])
        scat3.append(Scatter(net, at, part1, s, (sib1, ra1, rb1, fp1, fm1)))

    scat2 = []
    for s in (0, 1):

        def down(m, z, s=s):
            put_part(part2, s, m, z, mm(hidden[s, rows_of(m)], w_d[z]))

        scat3[s].merge()
        grid_loop(2, 4, down)
        put_ext(part2, s, [mm_nt(hidden[s], d_b[pick[s]])])
        scat2.append(Scatter(net, at, part2, s, (sib2, ra2, rb2, fp2, fm2)))
    scat3[0].relay()
    scat3[1].relay()
    for s in (0, 1):
        e = nb[s, :, :, D:].reshape(SPAN, EXT)
        g_go[s] = mm_tn(e, gate[s])[:RANK]
        g_uo[s] = mm_tn(e, up[s])[RANK : 2 * RANK]
        e = cb[s, :, :, D:].reshape(SPAN, EXT)
        g_di[s] = mm_tn(e, hidden[s])[:RANK]
    scat2[0].merge()
    scat2[1].merge()

    for s in (0, 1):
        t = scat3[s].done()
        pg, pu = t[:, D : D + RANK].astype(BF), t[:, D + RANK : D + 2 * RANK].astype(BF)
        back = t[:, :D] + mm(pg, gin[pick[s]]) + mm(pu, uin[pick[s]])
        mg = cot[s].astype(F32) + rms_back(midf[s], fgain[...], back)
        mgrad[s] = mg
        bg = mg.astype(BF)
        bgrad[s] = bg
        g_gi[s] = mm_tn(pg, midn[s])
        g_ui[s] = mm_tn(pu, midn[s])
        g_ao[s] = mm_tn(inner_a[s].astype(BF), bg)
    scat2[0].relay()
    scat2[1].relay()
    for s in (0, 1):
        t = scat2[s].done()
        inn = t[:, D : D + RANK].astype(BF)
        result[s] = midf[s] + t[:, :D] + mm(inn, dout[pick[s]])
        g_do[s] = mm_tn(inn, cot[s])
    net.drain()
    outs = [
        (result, result_o), (mgrad, mgrad_o), (bgrad, bgrad_o), (qb, q_o), (kvb, kv_o),
        (attn, attn_o), (lse, lse_o), (cosb, cos_o), (sinb, sin_o), (startb, start_o),
        (w_q, wq_o), (w_o, wo_o), (normed, normed_o), (next_s, next_o), (g_go, g_go_o),
        (g_uo, g_uo_o), (g_di, g_di_o), (g_gi, g_gi_o), (g_ui, g_ui_o), (g_ao, g_ao_o),
        (g_do, g_do_o),
    ]
    copies = [pltpu.make_async_copy(src, dst, local.at[i]) for i, (src, dst) in enumerate(outs)]
    for copy in copies:
        copy.start()
    for copy in copies:
        copy.wait()


def call_front(args):
    vm = lambda *shape, t=BF: pltpu.VMEM(shape, t)
    rs = lambda: [vm(2, TOK // 2, CW), vm(2, TOK // 2, CW), vm(2, TOK, CW), vm(2, TOK, CW)]
    outs = [
        ((2, TOK, D), F32), ((2, TOK, D), F32), ((2, TOK, D), BF),
        ((2, 2, SPAN, 128), BF), ((2, 2, 1536, 128), BF), ((2, SPAN, 256), BF),
        ((2, 2, SPAN, 1), F32), ((2, SPAN, 128), F32), ((2, SPAN, 128), F32),
        ((2, SPAN, 1), jnp.int32), ((4, 512, 512), BF), ((4, 256, 512), BF),
        ((2, TOK, D), BF), ((2, 8, TOK, EXT), BF),
        ((2, RANK, 1024), F32), ((2, RANK, 1024), F32), ((2, RANK, 1024), F32),
        ((2, RANK, D), F32), ((2, RANK, D), F32), ((2, RANK, D), F32), ((2, RANK, D), F32),
    ]
    scratch = (
        [vm(4, 512, 512), vm(4, 256, 512), vm(4, 512, 1024), vm(4, 512, 1024), vm(4, 1024, 512)]
        + [vm(2, 8, TOK, CW), vm(2, 8, TOK, CW), vm(2, 4, 2, TOK, CW), vm(2, 4, 2, TOK, CW)]
        + [vm(2, 4, TOK, CW), vm(2, 4, TOK, CW)]
        + rs() + rs()
        + [vm(2, SPAN, 1024)] * 3
        + [vm(2, 2, SPAN, 128), vm(2, 2, 1536, 128), vm(2, SPAN, 256), vm(2, 2, SPAN, 1, t=F32)]
        + [vm(2, SPAN, 128, t=F32)] * 2
        + [vm(2, SPAN, 1, t=jnp.int32)]
        + [vm(2, TOK, D, t=F32), vm(2, TOK, D), vm(2, TOK, D), vm(2, TOK, RANK, t=F32)]
        + [vm(2, TOK, D), vm(2, TOK, D, t=F32), vm(2, TOK, D, t=F32), vm(2, 8, TOK, EXT)]
        + [vm(2, RANK, 256), vm(2, RANK, 1024), vm(2, RANK, 512), vm(2, RANK, 1024), vm(2, RANK, 1024)]
        + [vm(2, RANK, 1024, t=F32)] * 3
        + [vm(2, RANK, D, t=F32)] * 4
        + [pltpu.SemaphoreType.DMA((170,)), pltpu.SemaphoreType.DMA((170,)), pltpu.SemaphoreType.DMA((24,))]
    )
    smem = pl.BlockSpec(memory_space=pltpu.SMEM)
    vmem = pl.BlockSpec(memory_space=pltpu.VMEM)
    hbm = pl.BlockSpec(memory_space=pl.ANY)
    return pl.pallas_call(
        front,
        out_shape=[jax.ShapeDtypeStruct(shape, kind) for shape, kind in outs],
        in_specs=[smem] * 2 + [vmem] * 5 + [hbm] * 5 + [vmem] * 5 + [hbm] * 5,
        out_specs=[hbm] * len(outs),
        scratch_shapes=scratch,
        compiler_params=pltpu.CompilerParams(
            collective_id=0, has_side_effects=True, vmem_limit_bytes=63 * 2**20
        ),
        cost_estimate=pl.CostEstimate(
            flops=26 * 10**9, bytes_accessed=30 * 10**6, transcendentals=5 * 10**6
        ),
    )(*args)


def rotate_back(g, cosine, signed):
    return g * cosine - jnp.roll(g, 64, axis=-1) * signed


def project_back(gradient_value, weight_matrix, low_in, high_out):
    wide = gradient_value.astype(F32)
    p = jnp.einsum("slc,src->slr", wide, high_out.astype(F32), precision=lax.Precision.HIGHEST)
    back = jnp.einsum("tfp,np->tfn", gradient_value, weight_matrix, preferred_element_type=F32)
    return back, p


def from_behind(value, axis, steps):
    count = lax.axis_size(axis)
    first, last = (max(0, -steps), min(count, count - steps))
    return lax.ppermute(value, axis, [(source, source + steps) for source in range(first, last)])


def body(
    tokens, cotangent, doc_lengths, adapter_index, attn_gain, ffn_gain,
    w_qkv, w_out, w_gate, w_up, w_down,
    qkv_in, qkv_out, attn_in, attn_out, gate_in, gate_out, up_in, up_out, down_in, down_out,
):
    flip = lambda g: jnp.swapaxes(g, 1, 2)
    half = jnp.arange(64, dtype=F32)
    inverse = THETA ** (-(half * 2.0 / 128))
    inv = jnp.concatenate([inverse, inverse])[None]
    head_at = lax.axis_index("head")
    block_at = lax.axis_index("blk")
    (
        result, mgrad, bgrad, q, kv, attn, lse, cosb, sinb, startb, wq, wo, normed, next_s,
        g_go, g_uo, g_di, g_gi, g_ui, g_ao, g_do,
    ) = call_front((
        adapter_index, doc_lengths, tokens, cotangent, attn_gain[None], ffn_gain[None], inv,
        w_qkv, w_out, w_gate, w_up, w_down,
        flip(qkv_in), flip(gate_in), flip(up_in), attn_out, down_out, flip(attn_in), flip(down_in),
        qkv_out, gate_out, up_out,
    ))
    pick = adapter_index[:, 0]
    sel = lambda t: jnp.take(t, pick, axis=0)
    own = lambda t, n, ax: lax.dynamic_slice_in_dim(t, head_at * n, n, ax)
    qkv_w = wq.reshape(D, 512)
    out_w = jnp.transpose(wo, (1, 0, 2)).reshape(256, D)
    grad_all = lax.all_gather(bgrad, "head", axis=1, tiled=True)
    a_in = sel(own(attn_in, 256, 1))
    back, p_attn = project_back(grad_all, out_w, a_in, sel(attn_out))
    back = back + jnp.einsum("slr,scr->slc", p_attn.astype(BF), a_in, preferred_element_type=F32)
    grad_attn_in = jnp.einsum("slr,slc->src", p_attn.astype(BF), attn, preferred_element_type=F32)
    dout = back.astype(BF).reshape(2, SPAN, 2, 128)
    keys, values = kv[:, 0], kv[:, 1]
    scores = jnp.einsum("sgqh,sjh->sgqj", q, keys, preferred_element_type=F32)
    qpos = block_at * SPAN + jnp.arange(SPAN)
    kpos = (block_at - 2) * SPAN + jnp.arange(3 * SPAN)
    gap = qpos[:, None] - kpos[None]
    ok = ((gap >= 0) & (gap < WINDOW))[None] & (kpos[None, None] >= startb)
    probs = jnp.where(ok[:, None], jnp.exp(scores - lse), 0.0)
    vgp = jnp.einsum("sqgh,sjh->sgqj", dout, values, preferred_element_type=F32)
    delta = jnp.sum(probs * vgp, axis=-1, keepdims=True)
    sgrad = (probs * (vgp - delta)).astype(BF)
    dq = jnp.einsum("sgqj,sjh->sgqh", sgrad, keys, preferred_element_type=F32)
    dk = jnp.einsum("sgqj,sgqh->sjh", sgrad, q, preferred_element_type=F32)
    dv = jnp.einsum("sgqj,sqgh->sjh", probs.astype(BF), dout, preferred_element_type=F32)
    pairs = jnp.stack([dk, dv], axis=1)
    mine = pairs[:, :, 1024:]
    for hop in (1, 2):
        part = pairs[:, :, (2 - hop) * SPAN : (3 - hop) * SPAN].astype(BF)
        mine = mine + from_behind(part, "blk", -hop).astype(F32)
    raw = jnp.concatenate(
        [rotate_back(dq[:, 0] * SCALE, cosb, sinb), rotate_back(dq[:, 1] * SCALE, cosb, sinb),
         rotate_back(mine[:, 0], cosb, sinb), mine[:, 1]], axis=-1).astype(BF)
    q_out = sel(own(qkv_out, 512, 2))
    back, p_qkv = project_back(raw, qkv_w, None, q_out)
    nin = jnp.transpose(next_s[..., :RANK], (0, 1, 2, 3)).reshape(2, SPAN, RANK)
    grad_qkv_out = jnp.einsum("slr,slc->src", nin, raw, preferred_element_type=F32)
    first = lax.psum_scatter(back.astype(BF), "head", scatter_dimension=1, tiled=True).astype(F32)
    p_own = lax.psum_scatter(p_qkv, "head", scatter_dimension=1, tiled=True)
    first = first + jnp.einsum("slr,scr->slc", p_own.astype(BF), sel(qkv_in), preferred_element_type=F32)
    grad_qkv_in = jnp.einsum("slr,slc->src", p_own.astype(BF), normed, preferred_element_type=F32)
    input_grad = mgrad + rms_back(tokens.astype(F32), attn_gain, first)

    swap = pick[0] == 1

    def by_adapter(g):
        return jnp.where(swap, g[::-1], g).astype(BF)

    def place(g, full):
        empty = jnp.zeros((2, RANK, full), BF)
        return lax.dynamic_update_slice_in_dim(empty, by_adapter(g), head_at * g.shape[2], 2)

    summed = lax.psum((
        by_adapter(grad_qkv_in), place(grad_qkv_out, 4096), place(grad_attn_in, D), by_adapter(g_ao),
        by_adapter(g_gi), place(g_go, 8192), by_adapter(g_ui), place(g_uo, 8192),
        place(g_di, 8192), by_adapter(g_do),
    ), ("head", "blk"))
    fin = [g.astype(F32) for g in summed]
    return (
        result, input_grad, flip(fin[0]), fin[1], flip(fin[2]), fin[3], flip(fin[4]), fin[5],
        flip(fin[6]), fin[7], flip(fin[8]), fin[9],
    )


def solution(mesh):
    row = P(None, ("blk", "head"), None)
    return jax.shard_map(
        body,
        mesh=mesh,
        in_specs=(row, row) + (P(),) * 4
        + (P("blk", "head"), P("head", "blk"), P("blk", "head"), P("blk", "head"), P("head", "blk"))
        + (P(),) * 10,
        out_specs=(row, row) + (P(),) * 10,
        check_vma=False,
    )
```

```python
from functools import partial

import jax
import jax.numpy as jnp
from jax import lax
from jax.experimental import pallas as pl
from jax.experimental.pallas import tpu as pltpu
from jax.sharding import PartitionSpec as P

MESH = pl.DeviceIdType.MESH
BF = jnp.bfloat16
F32 = jnp.float32
D = 2048
EXT = 128
CW = D + EXT
RANK = 16
WINDOW = 1024
EPS = 1e-05
THETA = 1000000.0
Y, CORES, Z, X = 4, 2, 4, 4
TOK = 64
SPAN = 512
SCALE = 128 ** (-0.5)
VMEM_BYTES = 66977792


def mm(a, b):
    return jnp.dot(a, b, preferred_element_type=F32)


def mm_nt(a, b):
    return lax.dot_general(a, b, (((1,), (1,)), ((), ())), preferred_element_type=F32)


def mm_tn(a, b):
    return lax.dot_general(a, b, (((0,), (0,)), ((), ())), preferred_element_type=F32)


class Place:
    def __init__(self):
        h = lax.axis_index("head")
        b = lax.axis_index("blk")
        self.h, self.b = h, b
        self.y, self.c = h // 2, h % 2
        self.z, self.x = b // 4, b % 4
        y, c, z, x = self.y, self.c, self.z, self.x
        self.yu, self.yd, self.yo = (y + 1) % 4, (y + 3) % 4, (y + 2) % 4
        self.xu, self.xd = (x + 1) % 4, (x + 3) % 4
        self.zu, self.zd = (z + 1) % 4, (z + 3) % 4
        self.sib = (y * 2 + (1 - c), b)
        self.yp, self.ym = (self.yu * 2 + c, b), (self.yd * 2 + c, b)
        self.xp, self.xm = (h, z * 4 + self.xu), (h, z * 4 + self.xd)
        self.zp, self.zm = (h, self.zu * 4 + x), (h, self.zd * 4 + x)
        self.next1, self.next2 = (h, (b + 1) % 16), (h, (b + 2) % 16)
        self.prev1, self.prev2 = (h, (b + 15) % 16), (h, (b + 14) % 16)

    def greet(self, peers):
        barrier = pltpu.get_barrier_semaphore()
        for peer in peers:
            pl.semaphore_signal(barrier, inc=1, device_id=peer, device_id_type=MESH)
        pl.semaphore_wait(barrier, len(peers))


class Net:
    def __init__(self, send, recv):
        self.send, self.recv, self.count, self.copies = send, recv, 0, []

    def push(self, src, dst, peer):
        i = self.count
        self.count += 1
        copy = pltpu.make_async_remote_copy(
            src_ref=src,
            dst_ref=dst,
            send_sem=self.send.at[i],
            recv_sem=self.recv.at[i],
            device_id=peer,
            device_id_type=MESH,
        )
        copy.start()
        self.copies.append(copy)
        return copy

    def settle(self, copies):
        for copy in copies:
            copy.wait_send()
            self.copies = [other for other in self.copies if other is not copy]

    def drain(self):
        self.settle(list(self.copies))


class Gather:
    def __init__(self, net, at, slot, extent):
        self.net, self.at, self.slot, self.half = net, at, slot, extent // 2
        own = slot(at.y, at.c)
        self.up = net.push(own, own, at.yp)
        self.down = net.push(own, own, at.ym)
        self.side = [net.push(own, own, at.sib)]

    def relay(self):
        at, net, half = self.at, self.net, self.half
        below = self.slot(at.yd, at.c)
        above = self.slot(at.yu, at.c)
        self.up.wait_recv()
        part = below.at[pl.ds(0, half)]
        self.far_a = net.push(part, part, at.yp)
        self.side.append(net.push(below, below, at.sib))
        self.down.wait_recv()
        part = above.at[pl.ds(half, half)]
        self.far_b = net.push(part, part, at.ym)
        self.side.append(net.push(above, above, at.sib))

    def last(self):
        at, net, half = self.at, self.net, self.half
        far = self.slot(at.yo, at.c)
        self.far_a.wait_recv()
        part = far.at[pl.ds(0, half)]
        self.side.append(net.push(part, part, at.sib))
        self.far_b.wait_recv()
        part = far.at[pl.ds(half, half)]
        self.side.append(net.push(part, part, at.sib))

    def done(self):
        for copy in self.side:
            copy.wait_recv()

    def settle(self):
        self.net.settle([self.up, self.down, self.far_a, self.far_b] + self.side)


class Fold:
    def __init__(self, net, at, full, full_in, vec, vec_in, out):
        self.net, self.at = net, at
        self.full, self.full_in, self.vec, self.vec_in, self.out = full, full_in, vec, vec_in, out

    def heads(self):
        at = self.at
        self.copies = []
        for k in range(1, 8):
            peer = (at.h + k) % 8
            self.copies.append(
                self.net.push(self.full.at[peer], self.full_in.at[k - 1], (peer, at.b))
            )

    def heads_sum(self):
        for copy in self.copies:
            copy.wait_recv()
        total = self.full[self.at.h].astype(F32)
        for k in range(7):
            total = total + self.full_in[k].astype(F32)
        return total

    def blocks(self):
        at = self.at
        self.copies = []
        for k in range(1, 16):
            peer = (at.b + k) % 16
            self.copies.append(
                self.net.push(self.vec.at[peer], self.vec_in.at[k - 1], (at.h, peer))
            )

    def blocks_sum(self):
        at = self.at
        for copy in self.copies:
            copy.wait_recv()
        total = self.vec[at.b].astype(F32)
        for k in range(15):
            total = total + self.vec_in[k].astype(F32)
        own = self.out.at[at.y, pl.ds(pl.multiple_of(at.c * 256 + at.b * 16, 16), 16)]
        own[...] = total.astype(BF)
        self.copies = []
        for k in range(1, 16):
            self.copies.append(self.net.push(own, own, (at.h, (at.b + k) % 16)))

    def blocks_done(self):
        for copy in self.copies:
            copy.wait_recv()

        def slot(y, c):
            return self.out.at[y, pl.ds(pl.multiple_of(c * 256, 256), 256)]

        self.gather = Gather(self.net, self.at, slot, 256)


class Scatter:
    def __init__(self, net, at, part, s, bufs):
        self.net, self.at, self.part, self.s = net, at, part, s
        self.sibr, self.ra, self.rb, self.fp, self.fm = bufs
        self.side = net.push(part.at[s, :, 1 - at.c], self.sibr.at[s], at.sib)

    def _merge(self, y):
        at, s = self.at, self.s
        self.part[s, y, at.c] = (
            self.part[s, y, at.c].astype(F32) + self.sibr[s, y].astype(F32)
        ).astype(BF)

    def merge(self):
        at, net, s = self.at, self.net, self.s
        self.side.wait_recv()
        self._merge(at.yo)
        far = self.part.at[s, at.yo, at.c]
        self.a = net.push(far.at[pl.ds(0, TOK // 2)], self.ra.at[s], at.yp)
        self.b = net.push(far.at[pl.ds(TOK // 2, TOK // 2)], self.rb.at[s], at.ym)
        self._merge(at.yu)
        self._merge(at.yd)

    def relay(self):
        at, net, s = self.at, self.net, self.s
        self.a.wait_recv()
        half = pl.ds(0, TOK // 2)
        self.part[s, at.yu, at.c, half] = (
            self.part[s, at.yu, at.c, half].astype(F32) + self.ra[s].astype(F32)
        ).astype(BF)
        self.up = net.push(self.part.at[s, at.yu, at.c], self.fp.at[s], at.yp)
        self.b.wait_recv()
        half = pl.ds(TOK // 2, TOK // 2)
        self.part[s, at.yd, at.c, half] = (
            self.part[s, at.yd, at.c, half].astype(F32) + self.rb[s].astype(F32)
        ).astype(BF)
        self.down = net.push(self.part.at[s, at.yd, at.c], self.fm.at[s], at.ym)

    def done(self):
        at, s = self.at, self.s
        self.up.wait_recv()
        self.down.wait_recv()
        self.net.settle([self.side, self.a, self.b, self.up, self.down])
        return (
            self.part[s, at.y, at.c].astype(F32) + self.sibr[s, at.y].astype(F32)
        ) + (self.fp[s].astype(F32) + self.fm[s].astype(F32))


class Weight:
    def __init__(self, net, at, ref, by_row):
        self.net, self.at, self.ref, self.by_row = net, at, ref, by_row
        self.rows, self.cols = ref.shape[1], ref.shape[2]
        self.state = [{}, {}]
        self.copies = []

    def sub(self, half, z, x, part):
        at = pl.ds(pl.multiple_of(x * 128, 128), 128)
        if self.by_row:
            width = self.cols // 2
            cols = pl.ds(half * width, width)
            if part is None:
                return self.ref.at[z, at, cols]
            return self.ref.at[z, pl.ds(pl.multiple_of(x * 128 + part * 64, 64), 64), cols]
        height = self.rows // 2
        if part is None:
            rows = pl.ds(half * height, height)
        else:
            rows = pl.ds(half * height + part * (height // 2), height // 2)
        return self.ref.at[z, rows, at]

    def block(self, half, index, part):
        if half == 0:
            if self.by_row:
                cols = pl.ds(0, self.cols // 2)
                rows = pl.ds(0, 512) if part is None else pl.ds(part * 256, 256)
                return self.ref.at[index, rows, cols]
            height = self.rows // 2
            rows = (
                pl.ds(0, height) if part is None else pl.ds(part * (height // 2), height // 2)
            )
            return self.ref.at[index, rows, pl.ds(0, 512)]
        zs = pl.ds(0, 4) if part is None else pl.ds(part * 2, 2)
        at = pl.ds(pl.multiple_of(index * 128, 128), 128)
        if self.by_row:
            return self.ref.at[zs, at, pl.ds(self.cols // 2, self.cols // 2)]
        return self.ref.at[zs, pl.ds(self.rows // 2, self.rows // 2), at]

    def _near(self, half, off, part):
        at = self.at
        if half == 0:
            return self.sub(0, at.z, (at.x + off) % 4, part)
        return self.sub(1, (at.z + off) % 4, at.x, part)

    def _far(self, half, off, part):
        at = self.at
        return self.block(half, ((at.z if half == 0 else at.x) + off) % 4, part)

    def _peers(self, half, first):
        at = self.at
        return (at.xp, at.xm) if (half == 0) == first else (at.zp, at.zm)

    def _round(self, k):
        for half in (0, 1):
            st = self.state[half]
            up, down = self._peers(half, k <= 2)
            if k == 1:
                ref = self._near(half, 0, None)
                st["u"], st["d"] = self.net.push(ref, ref, up), self.net.push(ref, ref, down)
            elif k == 2:
                st["u"].wait_recv()
                ref = self._near(half, 3, 0)
                st["fu"] = self.net.push(ref, ref, up)
                st["d"].wait_recv()
                ref = self._near(half, 1, 1)
                st["fd"] = self.net.push(ref, ref, down)
            elif k == 3:
                st["fu"].wait_recv()
                st["fd"].wait_recv()
                ref = self._far(half, 0, None)
                st["u"], st["d"] = self.net.push(ref, ref, up), self.net.push(ref, ref, down)
            elif k == 4:
                st["u"].wait_recv()
                ref = self._far(half, 3, 0)
                st["fu"] = self.net.push(ref, ref, up)
                st["d"].wait_recv()
                ref = self._far(half, 1, 1)
                st["fd"] = self.net.push(ref, ref, down)
            else:
                st["fu"].wait_recv()
                st["fd"].wait_recv()

    def step(self, k):
        first = len(self.net.copies)
        self._round(k)
        self.copies += self.net.copies[first:]

    def settle(self):
        self.net.settle(self.copies)


def rows_of(m):
    return pl.ds(pl.multiple_of(m * 256, 256), 256)


def cols_of(n):
    return pl.ds(pl.multiple_of(n * 512, 512), 512)


def heads_of(buf, s, m):
    return buf[s, pl.ds(m * 2, 2)].reshape(256, buf.shape[-1])


def rows_gather(net, at, buf, s):
    return Gather(net, at, lambda y, c: buf.at[s, y, c], TOK)


def rms(v, gain):
    return v * lax.rsqrt(jnp.mean(v * v, axis=-1, keepdims=True) + EPS) * gain


def rms_back(v, gain, grad):
    scale = lax.rsqrt(jnp.mean(v * v, axis=-1, keepdims=True) + EPS)
    scaled = gain * grad
    return scaled * scale - v * (
        jnp.mean(v * scaled, axis=-1, keepdims=True) * scale * scale * scale
    )


def put_part(part, s, m, z, value):
    part[s, pl.ds(m * 2, 2), :, :, cols_of(z)] = value.astype(BF).reshape(2, 2, TOK, 512)


def put_ext(part, s, pieces):
    part[s, :, :, :, D:] = jnp.zeros((4, 2, TOK, EXT), BF)
    for i, piece in enumerate(pieces):
        part[s, :, :, :, D + i * RANK : D + (i + 1) * RANK] = piece.astype(BF).reshape(
            4, 2, TOK, RANK
        )


def put_rows(buf, s, at, value, pieces):
    buf[s, at.y, at.c, :, :D] = value
    buf[s, at.y, at.c, :, D:] = jnp.zeros((TOK, EXT), BF)
    for i, piece in enumerate(pieces):
        buf[s, at.y, at.c, :, D + i * RANK : D + (i + 1) * RANK] = piece.astype(BF)


def grid_loop(m_count, n_count, body):
    def step(i, carry):
        body(i // n_count, i % n_count)
        return carry

    lax.fori_loop(0, m_count * n_count, step, 0)


def layer(
    index_ref, length_ref,
    tok, cot, again, fgain, inv,
    wq, wo, wg, wu, wd,
    qin, gin, uin, aout, dout, ain, din, qout, gout, uout,
    result_o, igrad_o, qi_o, qo_o, ai_o, ao_o, gi_o, go_o, ui_o, uo_o, di_o, do_o,
    w_q, w_o, w_g, w_u, w_d,
    nb, cb, part1, sib1, sib2, ra1, rb1, fp1, fm1, ra2, rb2, fp2, fm2,
    gate, up, hidden, qb, kvb, attn, lse, cosb, sinb, startb,
    midf, normed, midn, inner_a, mgrad, next_s, mid_s, cot_s, dkv, halo_in,
    a_b, d_b, q_b, g_b, u_b,
    full1, full1_in, vec1, vec1_in, full2, full2_in, vec2, vec2_in, stage8, stage2,
    send, recv, local,
):
    at = Place()
    net = Net(send, recv)
    pick = [index_ref[0, 0], index_ref[1, 0]]
    h, b = at.h, at.b

    here = pl.ds(pl.multiple_of(at.x * 128, 128), 128)
    loads = []

    def load(src, dst):
        copy = pltpu.make_async_copy(src, dst, local.at[len(loads)])
        copy.start()
        loads.append(copy)
        return copy

    load(wq, w_q.at[at.z, here, :])
    load(wo, w_o.at[at.z, :, here])
    load(wg, w_g.at[at.z, here, :])
    load(wu, w_u.at[at.z, here, :])
    load(wd, w_d.at[at.z, :, here])
    load(ain.at[:, :, pl.ds(pl.multiple_of(h * 256, 256), 256)], a_b)
    load(din.at[:, :, pl.ds(pl.multiple_of(h * 1024, 1024), 1024)], d_b)
    load(qout.at[:, :, pl.ds(pl.multiple_of(h * 512, 512), 512)], q_b)
    load(gout.at[:, :, pl.ds(pl.multiple_of(h * 1024, 1024), 1024)], g_b)
    load(uout.at[:, :, pl.ds(pl.multiple_of(h * 1024, 1024), 1024)], u_b)

    at.greet(
        [((h + k) % 8, b) for k in range(1, 8)] + [(h, (b + k) % 16) for k in range(1, 16)]
    )
    for copy in loads:
        copy.wait()
    W_Q = Weight(net, at, w_q, True)
    W_O = Weight(net, at, w_o, False)
    W_G = Weight(net, at, w_g, True)
    W_U = Weight(net, at, w_u, True)
    W_D = Weight(net, at, w_d, False)

    W_Q.step(1)
    W_O.step(1)

    g_n = []
    for s in (0, 1):
        n = rms(tok[s].astype(F32), again[...]).astype(BF)
        normed[s] = n
        put_rows(nb, s, at, n, [mm_nt(n, qin[pick[s]])])
        g_n.append(rows_gather(net, at, nb, s))
    W_Q.step(2)
    W_O.step(2)
    W_G.step(1)

    sign = jnp.where(lax.broadcasted_iota(jnp.int32, (1, 128), 1) < 64, -1.0, 1.0)

    def table(s, m):
        rows = pl.ds(pl.multiple_of(m * 64, 64), 64)
        pos = b * SPAN + m * 64 + lax.broadcasted_iota(jnp.int32, (64, 1), 0)
        start = jnp.zeros((64, 1), jnp.int32)
        end = 0
        for d in range(4):
            length = length_ref[s, d]
            end = end + length
            start = start + jnp.where(pos >= end, length, 0)
        startb[s, rows] = start
        angle = (pos - start).astype(F32) * inv[...]
        cosb[s, rows] = jnp.cos(angle)
        sinb[s, rows] = jnp.sin(angle) * sign

    grid_loop(2, 8, table)
    g_n[0].relay()
    g_n[1].relay()
    W_Q.step(3)
    W_G.step(2)

    for s in (0, 1):
        put_rows(cb, s, at, cot[s], [mm_nt(cot[s], dout[pick[s]])])
    g_n[0].last()
    g_n[1].last()
    W_Q.step(4)
    W_O.step(3)
    g_c = [rows_gather(net, at, cb, s) for s in (0, 1)]
    g_n[0].done()
    g_n[1].done()
    W_Q.step(5)
    W_G.step(3)

    halos = []
    for s in (0, 1):

        def qkv(m, unused, s=s):
            x = heads_of(nb, s, m)
            r = mm(x[:, :D], w_q[...].reshape(D, 512)) + mm(x[:, D : D + RANK], q_b[pick[s]])
            rows = rows_of(m)
            c, sn = cosb[s, rows], sinb[s, rows]

            def rot(v):
                return v * c + pltpu.roll(v, 64, 1) * sn

            for j in (0, 1):
                qb[s, j, rows] = (rot(r[:, j * 128 : (j + 1) * 128]) * SCALE).astype(BF)
            own = pl.ds(pl.multiple_of(1024 + m * 256, 256), 256)
            kvb[s, 0, own] = rot(r[:, 256:384]).astype(BF)
            kvb[s, 1, own] = r[:, 384:512].astype(BF)

        grid_loop(2, 1, qkv)
        own = kvb.at[s, :, pl.ds(1024, 512)]
        halos.append(net.push(own, kvb.at[s, :, pl.ds(512, 512)], at.next1))
        halos.append(net.push(own, kvb.at[s, :, pl.ds(0, 512)], at.next2))
    next_s[...] = nb[:, :, :, :, D:].reshape(2, SPAN, EXT)
    W_O.step(4)
    W_U.step(1)
    g_c[0].relay()
    g_c[1].relay()
    W_U.step(2)
    W_O.step(5)

    g_n[0].settle()
    g_n[1].settle()

    row = lax.broadcasted_iota(jnp.int32, (256, 1280), 0)
    col = lax.broadcasted_iota(jnp.int32, (256, 1280), 1)
    scat1 = []
    for s in (0, 1):
        halos[2 * s].wait_recv()
        halos[2 * s + 1].wait_recv()

        def attend(g, m, s=s):
            rows = rows_of(m)
            keys = pl.ds(pl.multiple_of(m * 256, 256), 1280)
            sc = mm_nt(qb[s, g, rows], kvb[s, 0, keys])
            low = startb[s, rows] - (b * SPAN - WINDOW + m * 256)
            gap = row - col + WINDOW
            ok = (gap >= 0) & (gap < WINDOW) & (col >= low)
            sc = jnp.where(ok, sc, -1e30)
            top = jnp.max(sc, axis=-1, keepdims=True)
            e = jnp.exp(sc - top)
            total = jnp.sum(e, axis=-1, keepdims=True)
            p = (e * (1.0 / total)).astype(BF)
            o = mm(p, kvb[s, 1, keys])
            attn[s, rows, pl.ds(pl.multiple_of(g * 128, 128), 128)] = o.astype(BF)
            lse[s, g, rows] = top + jnp.log(total)

        grid_loop(2, 2, attend)
        if s == 0:
            g_c[0].last()
            g_c[1].last()
            W_G.step(4)

        def out_proj(m, z, s=s):
            put_part(part1, s, m, z, mm(attn[s, rows_of(m)], w_o[z]))

        grid_loop(2, 4, out_proj)
        put_ext(part1, s, [mm_nt(attn[s], a_b[pick[s]])])
        scat1.append(Scatter(net, at, part1, s, (sib1, ra1, rb1, fp1, fm1)))
        if s == 0:
            W_U.step(3)
    g_c[0].done()
    g_c[1].done()
    scat1[0].merge()
    scat1[1].merge()
    scat1[0].relay()
    scat1[1].relay()
    W_G.step(5)
    W_D.step(1)

    g_m = []
    for s in (0, 1):
        t = scat1[s].done()
        inn = t[:, D : D + RANK]
        inner_a[s] = inn
        mid = tok[s].astype(F32) + t[:, :D] + mm(inn.astype(BF), aout[pick[s]])
        midf[s] = mid
        n = rms(mid, fgain[...]).astype(BF)
        midn[s] = n
        put_rows(nb, s, at, n, [mm_nt(n, gin[pick[s]]), mm_nt(n, uin[pick[s]])])
        g_m.append(rows_gather(net, at, nb, s))
    W_U.step(4)
    W_D.step(2)
    g_m[0].relay()
    g_m[1].relay()
    W_D.step(3)
    g_m[0].last()
    g_m[1].last()
    W_U.step(5)
    g_m[0].done()
    g_m[1].done()
    W_D.step(4)

    for s in (0, 1):

        def ffn(m, n, s=s):
            x = heads_of(nb, s, m)
            rows, cols = rows_of(m), cols_of(n)
            g = mm(x[:, :D], w_g[:, :, cols].reshape(D, 512))
            g = g + mm(x[:, D : D + RANK], g_b[pick[s], :, cols])
            u = mm(x[:, :D], w_u[:, :, cols].reshape(D, 512))
            u = u + mm(x[:, D + RANK : D + 2 * RANK], u_b[pick[s], :, cols])
            gate[s, rows, cols] = g.astype(BF)
            up[s, rows, cols] = u.astype(BF)
            hidden[s, rows, cols] = (g * jax.nn.sigmoid(g) * u).astype(BF)

        grid_loop(2, 2, ffn)
    W_D.step(5)
    mid_s[...] = nb[:, :, :, :, D:].reshape(2, SPAN, EXT)
    cot_s[...] = cb[:, :, :, :, D:].reshape(2, SPAN, EXT)
    for s in (0, 1):
        g_c[s].settle()
        g_m[s].settle()
    W_G.settle()
    W_U.settle()

    scat3 = []
    for s in (0, 1):

        def hid_back(m, n, s=s):
            x = heads_of(cb, s, m)
            rows, cols = rows_of(m), cols_of(n)
            hb = mm(x[:, D : D + RANK], d_b[pick[s], :, cols])
            for z in range(4):
                hb = hb + mm_nt(x[:, z * 512 : (z + 1) * 512], w_d[z, cols, :])
            g = gate[s, rows, cols].astype(F32)
            u = up[s, rows, cols].astype(F32)
            sg = jax.nn.sigmoid(g)
            gate[s, rows, cols] = (hb * u * sg * (1.0 + g * (1.0 - sg))).astype(BF)
            up[s, rows, cols] = (hb * g * sg).astype(BF)

        grid_loop(2, 2, hid_back)

        def mid_back(m, z, s=s):
            rows = rows_of(m)
            r = mm_nt(gate[s, rows], w_g[z]) + mm_nt(up[s, rows], w_u[z])
            put_part(part1, s, m, z, r)

        grid_loop(2, 4, mid_back)
        put_ext(part1, s, [mm_nt(gate[s], g_b[pick[s]]), mm_nt(up[s], u_b[pick[s]])])
        scat3.append(Scatter(net, at, part1, s, (sib1, ra1, rb1, fp1, fm1)))

    out1, out2 = w_g.at[:, :, pl.ds(0, 512)], w_u.at[:, :, pl.ds(0, 128)]
    fold1 = Fold(net, at, full1, full1_in, vec1, vec1_in, out1)
    fold2 = Fold(net, at, full2, full2_in, vec2, vec2_in, out2)
    scat2 = []
    for s in (0, 1):
        scat3[s].merge()

        def down(m, z, s=s):
            put_part(nb, s, m, z, mm(hidden[s, rows_of(m)], w_d[z]))

        grid_loop(2, 4, down)
        put_ext(nb, s, [mm_nt(hidden[s], d_b[pick[s]])])
        scat2.append(Scatter(net, at, nb, s, (sib2, ra2, rb2, fp2, fm2)))
    scat3[0].relay()
    scat3[1].relay()
    for s in (0, 1):
        terms = [
            mm_tn(mid_s[s], gate[s])[:RANK],
            mm_tn(mid_s[s], up[s])[RANK : 2 * RANK],
            mm_tn(cot_s[s], hidden[s])[:RANK],
        ]
        for i, term in enumerate(terms):
            for j in range(4):
                vec1[3 + 4 * i + j, :, s * 256 : (s + 1) * 256] = term[
                    :, j * 256 : (j + 1) * 256
                ].astype(BF)

    def slices(full, i, s, term):
        for j in range(8):
            full[j, i, :, s * 256 : (s + 1) * 256] = term[:, j * 256 : (j + 1) * 256].astype(BF)

    g_b2 = []
    for s in (0, 1):
        t = scat3[s].done()
        pg, pu = t[:, D : D + RANK].astype(BF), t[:, D + RANK : D + 2 * RANK].astype(BF)
        back = t[:, :D] + mm(pg, gin[pick[s]]) + mm(pu, uin[pick[s]])
        mg = cot[s].astype(F32) + rms_back(midf[s], fgain[...], back)
        mgrad[s] = mg
        bg = mg.astype(BF)
        put_rows(cb, s, at, bg, [mm_nt(bg, aout[pick[s]])])
        g_b2.append(rows_gather(net, at, cb, s))
        slices(full1, 0, s, mm_tn(pg, midn[s]))
        slices(full1, 1, s, mm_tn(pu, midn[s]))
        slices(full1, 2, s, mm_tn(inner_a[s].astype(BF), bg))
    fold1.heads()
    g_b2[0].relay()
    g_b2[1].relay()
    scat2[0].merge()
    g_b2[0].last()
    g_b2[1].last()
    scat2[1].merge()
    vec1[0:3] = fold1.heads_sum().astype(BF)
    g_b2[0].done()
    g_b2[1].done()

    def attn_back(s):
        def step(m, unused):
            x = heads_of(cb, s, m)
            r = mm(x[:, D : D + RANK], a_b[pick[s]])
            for z in range(4):
                r = r + mm_nt(x[:, z * 512 : (z + 1) * 512], w_o[z])
            hidden[s, rows_of(m), 512:768] = r.astype(BF)

        grid_loop(2, 1, step)
        e = cb[s, :, :, :, D:].reshape(SPAN, EXT)
        vec1[15, :, s * 256 : (s + 1) * 256] = mm_tn(e, attn[s])[:RANK].astype(BF)

    attn_back(0)
    attn_back(1)
    fold1.blocks()
    back_halos = []
    for s in (0, 1):
        dkv[...] = jnp.zeros(dkv.shape, F32)

        def attend_back(g, m, s=s):
            rows = rows_of(m)
            keys = pl.ds(pl.multiple_of(m * 256, 256), 1280)
            mine = pl.ds(pl.multiple_of(g * 128, 128), 128)
            q, k = qb[s, g, rows], kvb[s, 0, keys]
            do = hidden[s, rows, pl.ds(pl.multiple_of(512 + g * 128, 128), 128)]
            low = startb[s, rows] - (b * SPAN - WINDOW + m * 256)
            gap = row - col + WINDOW
            ok = (gap >= 0) & (gap < WINDOW) & (col >= low)
            p = jnp.where(ok, jnp.exp(mm_nt(q, k) - lse[s, g, rows]), 0.0)
            vg = mm_nt(do, kvb[s, 1, keys])
            delta = jnp.sum(p * vg, axis=-1, keepdims=True)
            sg = (p * (vg - delta)).astype(BF)
            dq = mm(sg, k) * SCALE
            hidden[s, rows, mine] = (
                dq * cosb[s, rows] - pltpu.roll(dq, 64, 1) * sinb[s, rows]
            ).astype(BF)
            dkv[0, keys] += mm_tn(sg, q)
            dkv[1, keys] += mm_tn(p.astype(BF), do)

        grid_loop(2, 2, attend_back)
        for hop in (0, 1, 2):
            for i in (0, 1):
                at_col = hop * 256 + i * 128
                gate[s, :, at_col : at_col + 128] = dkv[
                    i, (2 - hop) * SPAN : (3 - hop) * SPAN
                ].astype(BF)
            if hop == 0:
                continue
            back_halos.append(
                net.push(
                    gate.at[s, :, pl.ds(hop * 256, 256)],
                    halo_in.at[s, hop - 1],
                    at.prev1 if hop == 1 else at.prev2,
                )
            )
        if s == 0:
            scat2[0].relay()
            scat2[1].relay()
            fold1.blocks_sum()
    for s in (0, 1):
        t = scat2[s].done()
        inn = t[:, D : D + RANK].astype(BF)
        midf[s] = midf[s] + t[:, :D] + mm(inn, dout[pick[s]])
        slices(full2, 1, s, mm_tn(inn, cot[s]))
    fold1.blocks_done()

    scat4 = []
    for s in (0, 1):
        back_halos[2 * s].wait_recv()
        back_halos[2 * s + 1].wait_recv()

        def key_back(m, unused, s=s):
            rows = rows_of(m)
            dk, dv = [
                gate[s, rows, i * 128 : (i + 1) * 128].astype(F32)
                + halo_in[s, 0, rows, i * 128 : (i + 1) * 128].astype(F32)
                + halo_in[s, 1, rows, i * 128 : (i + 1) * 128].astype(F32)
                for i in (0, 1)
            ]
            hidden[s, rows, 256:384] = (
                dk * cosb[s, rows] - pltpu.roll(dk, 64, 1) * sinb[s, rows]
            ).astype(BF)
            hidden[s, rows, 384:512] = dv.astype(BF)

        grid_loop(2, 1, key_back)

        def qkv_back(m, z, s=s):
            put_part(part1, s, m, z, mm_nt(hidden[s, rows_of(m), :512], w_q[z]))

        grid_loop(2, 4, qkv_back)
        raw = hidden[s, :, :512]
        put_ext(part1, s, [mm_nt(raw, q_b[pick[s]])])
        scat4.append(Scatter(net, at, part1, s, (sib1, ra1, rb1, fp1, fm1)))
        term = mm_tn(next_s[s], raw)[:RANK]
        for j in range(4):
            vec2[s * 8 + 4 + j] = term[:, j * 128 : (j + 1) * 128].astype(BF)
        if s == 1:
            fold1.gather.relay()
        scat4[s].merge()
    scat4[0].relay()
    scat4[1].relay()
    fold1.gather.last()
    for s in (0, 1):
        t = scat4[s].done()
        p = t[:, D : D + RANK].astype(BF)
        back = t[:, :D] + mm(p, qin[pick[s]])
        mgrad[s] = mgrad[s] + rms_back(tok[s].astype(F32), again[...], back)
        slices(full2, 0, s, mm_tn(p, normed[s]))
    fold2.heads()
    writes = [
        pltpu.make_async_copy(midf, result_o, local.at[0]),
        pltpu.make_async_copy(mgrad, igrad_o, local.at[1]),
    ]
    for copy in writes:
        copy.start()

    swap = pick[0] == 1

    def found(buf, j, i, width):
        row0 = (j % 2) * 256 + i * RANK
        return buf[j // 2, row0 : row0 + RANK, :width]

    def emit(stage, out, sem, parts):
        for cols, (first, second) in parts:
            first, second = first.astype(F32), second.astype(F32)
            stage[0, :, cols] = jnp.where(swap, second, first)
            stage[1, :, cols] = jnp.where(swap, first, second)
        copy = pltpu.make_async_copy(stage, out, local.at[sem])
        copy.start()
        return copy

    fold1.gather.done()
    wide = [go_o, uo_o, di_o]
    for i in range(3):
        parts = []
        for j in range(8):
            for k in range(4):
                block = found(w_g, j, 3 + 4 * i + k, 512)
                parts.append((pl.ds(j * 1024 + k * 256, 256), (block[:, :256], block[:, 256:])))
        copy = emit(stage8, wide[i], 2, parts)
        copy.wait()
    small = []
    for i, (index, out) in enumerate([(0, gi_o), (1, ui_o), (2, ao_o), (15, ai_o)]):
        parts = []
        for j in range(8):
            block = found(w_g, j, index, 512)
            parts.append((pl.ds(j * 256, 256), (block[:, :256], block[:, 256:])))
        small.append(emit(stage2.at[i], out, 3 + i, parts))

    total = fold2.heads_sum()
    for i in (0, 1):
        for s in (0, 1):
            for j in (0, 1):
                vec2[s * 8 + 2 * i + j] = total[i, :, s * 256 + j * 128 : s * 256 + (j + 1) * 128].astype(BF)
    fold2.blocks()
    fold2.blocks_sum()
    fold2.blocks_done()
    fold2.gather.relay()
    fold2.gather.last()
    fold2.gather.done()
    for i, out in enumerate([qi_o, do_o]):
        parts = []
        for j in range(8):
            for k in range(2):
                first = found(w_u, j, 2 * i + k, 128)
                second = found(w_u, j, 8 + 2 * i + k, 128)
                parts.append((pl.ds(j * 256 + k * 128, 128), (first, second)))
        small[i].wait()
        small[i] = emit(stage2.at[i], out, 3 + i, parts)
    parts = []
    for j in range(8):
        for k in range(4):
            first = found(w_u, j, 4 + k, 128)
            second = found(w_u, j, 12 + k, 128)
            parts.append((pl.ds(j * 512 + k * 128, 128), (first, second)))
    writes.append(emit(stage8.at[:, :, pl.ds(0, 4096)], qo_o, 2, parts))
    net.drain()
    for copy in writes + small:
        copy.wait()


def call_layer(args):
    vm = lambda *shape, t=BF: pltpu.VMEM(shape, t)
    rs = lambda: [vm(2, TOK // 2, CW), vm(2, TOK // 2, CW), vm(2, TOK, CW), vm(2, TOK, CW)]
    narrow, wide = ((2, RANK, D), F32), ((2, RANK, 8192), F32)
    outs = [
        ((2, TOK, D), F32), ((2, TOK, D), F32), narrow, ((2, RANK, 4096), F32), narrow, narrow,
        narrow, wide, narrow, wide, wide, narrow,
    ]
    scratch = (
        [vm(4, 512, 512), vm(4, 256, 512), vm(4, 512, 1024), vm(4, 512, 1024), vm(4, 1024, 512)]
        + [vm(2, 4, 2, TOK, CW)] * 3
        + [vm(2, 4, TOK, CW), vm(2, 4, TOK, CW)]
        + rs() + rs()
        + [vm(2, SPAN, 1024)] * 3
        + [vm(2, 2, SPAN, 128), vm(2, 2, 1536, 128), vm(2, SPAN, 256), vm(2, 2, SPAN, 1, t=F32)]
        + [vm(2, SPAN, 128, t=F32)] * 2
        + [vm(2, SPAN, 1, t=jnp.int32)]
        + [vm(2, TOK, D, t=F32), vm(2, TOK, D), vm(2, TOK, D), vm(2, TOK, RANK, t=F32)]
        + [vm(2, TOK, D, t=F32)] + [vm(2, SPAN, EXT)] * 3
        + [vm(2, 1536, 128, t=F32), vm(2, 2, SPAN, 256)]
        + [vm(2, RANK, 256), vm(2, RANK, 1024), vm(2, RANK, 512), vm(2, RANK, 1024), vm(2, RANK, 1024)]
        + [vm(8, 3, RANK, 512), vm(7, 3, RANK, 512), vm(16, RANK, 512), vm(15, RANK, 512)]
        + [vm(8, 2, RANK, 512), vm(7, 2, RANK, 512), vm(16, RANK, 128), vm(15, RANK, 128)]
        + [vm(2, RANK, 8192, t=F32), vm(4, 2, RANK, D, t=F32)]
        + [pltpu.SemaphoreType.DMA((320,)), pltpu.SemaphoreType.DMA((320,)), pltpu.SemaphoreType.DMA((10,))]
    )
    smem = pl.BlockSpec(memory_space=pltpu.SMEM)
    vmem = pl.BlockSpec(memory_space=pltpu.VMEM)
    hbm = pl.BlockSpec(memory_space=pl.ANY)
    return pl.pallas_call(
        layer,
        out_shape=[jax.ShapeDtypeStruct(shape, kind) for shape, kind in outs],
        in_specs=[smem] * 2 + [vmem] * 5 + [hbm] * 5 + [vmem] * 5 + [hbm] * 5,
        out_specs=[hbm] * len(outs),
        scratch_shapes=scratch,
        compiler_params=pltpu.CompilerParams(
            collective_id=0, has_side_effects=True, vmem_limit_bytes=VMEM_BYTES
        ),
    )(*args)


def body(
    tokens, cotangent, doc_lengths, adapter_index, attn_gain, ffn_gain,
    w_qkv, w_out, w_gate, w_up, w_down,
    qkv_in, qkv_out, attn_in, attn_out, gate_in, gate_out, up_in, up_out, down_in, down_out,
):
    flip = lambda g: jnp.swapaxes(g, 1, 2)
    half = jnp.arange(64, dtype=F32)
    inverse = THETA ** (-(half * 2.0 / 128))
    inv = jnp.concatenate([inverse, inverse])[None]
    result, igrad, qi, qo, ai, ao, gi, go, ui, uo, di, do = call_layer((
        adapter_index, doc_lengths, tokens, cotangent, attn_gain[None], ffn_gain[None], inv,
        w_qkv, w_out, w_gate, w_up, w_down,
        flip(qkv_in), flip(gate_in), flip(up_in), attn_out, down_out, flip(attn_in), flip(down_in),
        qkv_out, gate_out, up_out,
    ))
    return (
        result, igrad, flip(qi), qo, flip(ai), ao, flip(gi), go, flip(ui), uo, flip(di), do
    )


def solution(mesh):
    row = P(None, ("blk", "head"), None)
    return jax.shard_map(
        body,
        mesh=mesh,
        in_specs=(row, row) + (P(),) * 4
        + (P("blk", "head"), P("head", "blk"), P("blk", "head"), P("blk", "head"), P("head", "blk"))
        + (P(),) * 10,
        out_specs=(row, row) + (P(),) * 10,
        check_vma=False,
    )
```

```python
from functools import partial

import jax
import jax.numpy as jnp
import numpy as np
from jax import lax
from jax.experimental import pallas as pl
from jax.experimental.pallas import tpu as pltpu
from jax.sharding import PartitionSpec as P

MESH = pl.DeviceIdType.MESH
BF = jnp.bfloat16
F32 = jnp.float32
D = 2048
EXT = 128
CW = D + EXT
RANK = 16
WINDOW = 1024
EPS = 1e-05
THETA = 1000000.0
Y, CORES, Z, X = 4, 2, 4, 4
TOK = 64
SPAN = 512
SCALE = 128 ** (-0.5)
VMEM_BYTES = 66977792
N_SEMS = 180


def mm(a, b):
    return jnp.dot(a, b, preferred_element_type=F32)


def mm_nt(a, b):
    return lax.dot_general(a, b, (((1,), (1,)), ((), ())), preferred_element_type=F32)


def mm_tn(a, b):
    return lax.dot_general(a, b, (((0,), (0,)), ((), ())), preferred_element_type=F32)


class Place:
    def __init__(self):
        h = lax.axis_index("head")
        b = lax.axis_index("blk")
        self.h, self.b = h, b
        self.y, self.c = h // 2, h % 2
        self.z, self.x = b // 4, b % 4
        y, c, z, x = self.y, self.c, self.z, self.x
        self.yu, self.yd, self.yo = (y + 1) % 4, (y + 3) % 4, (y + 2) % 4
        self.xu, self.xd = (x + 1) % 4, (x + 3) % 4
        self.zu, self.zd = (z + 1) % 4, (z + 3) % 4
        self.sib = (y * 2 + (1 - c), b)
        self.yp, self.ym = (self.yu * 2 + c, b), (self.yd * 2 + c, b)
        self.xp, self.xm = (h, z * 4 + self.xu), (h, z * 4 + self.xd)
        self.zp, self.zm = (h, self.zu * 4 + x), (h, self.zd * 4 + x)
        self.next1, self.next2 = (h, (b + 1) % 16), (h, (b + 2) % 16)
        self.prev1, self.prev2 = (h, (b + 15) % 16), (h, (b + 14) % 16)

    def greet(self, peers):
        barrier = pltpu.get_barrier_semaphore()
        for peer in peers:
            pl.semaphore_signal(barrier, inc=1, device_id=peer, device_id_type=MESH)
        pl.semaphore_wait(barrier, len(peers))


class Net:
    def __init__(self, send, recv):
        self.send, self.recv, self.count, self.copies = send, recv, 0, []

    def ids(self, n):
        first = self.count
        self.count += n
        return list(range(first, first + n))

    def make(self, src, dst, peer, i):
        return pltpu.make_async_remote_copy(
            src_ref=src,
            dst_ref=dst,
            send_sem=self.send.at[i],
            recv_sem=self.recv.at[i],
            device_id=peer,
            device_id_type=MESH,
        )

    def push(self, src, dst, peer, i):
        copy = self.make(src, dst, peer, i)
        copy.start()
        self.copies.append(copy)
        return copy

    def spread(self, pairs, whole, i):
        for src, dst, peer in pairs:
            self.make(src, dst, peer, i).start()
        copy = self.make(whole, whole, pairs[0][2], i)
        self.copies.append(copy)
        return copy

    def settle(self, copies):
        for copy in copies:
            copy.wait_send()
            self.copies = [other for other in self.copies if other is not copy]

    def drain(self):
        self.settle(list(self.copies))


class Gather:
    def __init__(self, net, at, slot, extent, ids):
        self.net, self.at, self.slot, self.half, self.ids = net, at, slot, extent // 2, ids
        own = slot(at.y, at.c)
        self.up = net.push(own, own, at.yp, ids[0])
        self.down = net.push(own, own, at.ym, ids[1])
        self.side = [net.push(own, own, at.sib, ids[2])]

    def relay(self):
        at, net, half, ids = self.at, self.net, self.half, self.ids
        below = self.slot(at.yd, at.c)
        above = self.slot(at.yu, at.c)
        self.up.wait_recv()
        part = below.at[pl.ds(0, half)]
        self.far_a = net.push(part, part, at.yp, ids[3])
        self.side.append(net.push(below, below, at.sib, ids[4]))
        self.down.wait_recv()
        part = above.at[pl.ds(half, half)]
        self.far_b = net.push(part, part, at.ym, ids[5])
        self.side.append(net.push(above, above, at.sib, ids[6]))

    def last(self):
        at, net, half, ids = self.at, self.net, self.half, self.ids
        far = self.slot(at.yo, at.c)
        self.far_a.wait_recv()
        part = far.at[pl.ds(0, half)]
        self.side.append(net.push(part, part, at.sib, ids[7]))
        self.far_b.wait_recv()
        part = far.at[pl.ds(half, half)]
        self.side.append(net.push(part, part, at.sib, ids[8]))

    def done(self):
        for copy in self.side:
            copy.wait_recv()

    def settle(self):
        self.net.settle([self.up, self.down, self.far_a, self.far_b] + self.side)


class Fold:
    def __init__(self, net, at, full, full_in, vec, vec_in, out, near):
        self.net, self.at = net, at
        self.full, self.full_in, self.vec, self.vec_in, self.out = full, full_in, vec, vec_in, out
        self.ids, self.near = net.ids(2), near

    def heads(self):
        at = self.at
        pairs = []
        for k in range(1, 8):
            peer = (at.h + k) % 8
            pairs.append((self.full.at[peer], self.full_in.at[k - 1], (peer, at.b)))
        self.copy = self.net.spread(pairs, self.full_in, self.ids[0])

    def heads_sum(self):
        self.copy.wait_recv()
        total = self.full[self.at.h].astype(F32)
        for k in range(7):
            total = total + self.full_in[k].astype(F32)
        return total

    def blocks(self):
        at = self.at
        pairs = []
        for k in range(1, 16):
            peer = (at.b + k) % 16
            pairs.append((self.vec.at[peer], self.vec_in.at[k - 1], (at.h, peer)))
        self.copy = self.net.spread(pairs, self.vec_in, self.ids[1])

    def blocks_sum(self):
        at = self.at
        self.copy.wait_recv()
        total = self.vec[at.b].astype(F32)
        for k in range(15):
            total = total + self.vec_in[k].astype(F32)
        own = self.out.at[at.z, pl.ds(pl.multiple_of(at.x * 128 + at.h * 16, 16), 16)]
        own[...] = total.astype(BF)
        self.copies = [
            self.net.push(own, own, ((at.h + k) % 8, at.b), self.near[k - 1]) for k in range(1, 8)
        ]

    def near_done(self):
        for copy in self.copies:
            copy.wait_recv()
        self.net.settle(self.copies)

    def far(self, ids):
        at = self.at
        own = self.out.at[at.z, pl.ds(pl.multiple_of(at.x * 128, 128), 128)]
        self.copies = [
            self.net.push(own, own, (at.h, (at.b + k) % 16), ids[k - 1]) for k in range(1, 16)
        ]

    def far_done(self):
        for copy in self.copies:
            copy.wait_recv()


class Scatter:
    def __init__(self, net, at, part, s, bufs, ids):
        self.net, self.at, self.part, self.s, self.ids = net, at, part, s, ids
        self.sibr, self.ra, self.rb, self.fp, self.fm = bufs
        self.side = net.push(part.at[s, :, 1 - at.c], self.sibr.at[s], at.sib, ids[0])

    def _merge(self, y):
        at, s = self.at, self.s
        self.part[s, y, at.c] = (
            self.part[s, y, at.c].astype(F32) + self.sibr[s, y].astype(F32)
        ).astype(BF)

    def merge(self):
        at, net, s = self.at, self.net, self.s
        self.side.wait_recv()
        self._merge(at.yo)
        far = self.part.at[s, at.yo, at.c]
        self.a = net.push(far.at[pl.ds(0, TOK // 2)], self.ra.at[s], at.yp, self.ids[1])
        self.b = net.push(far.at[pl.ds(TOK // 2, TOK // 2)], self.rb.at[s], at.ym, self.ids[2])
        self._merge(at.yu)
        self._merge(at.yd)

    def relay(self):
        at, net, s = self.at, self.net, self.s
        self.a.wait_recv()
        half = pl.ds(0, TOK // 2)
        self.part[s, at.yu, at.c, half] = (
            self.part[s, at.yu, at.c, half].astype(F32) + self.ra[s].astype(F32)
        ).astype(BF)
        self.up = net.push(self.part.at[s, at.yu, at.c], self.fp.at[s], at.yp, self.ids[3])
        self.b.wait_recv()
        half = pl.ds(TOK // 2, TOK // 2)
        self.part[s, at.yd, at.c, half] = (
            self.part[s, at.yd, at.c, half].astype(F32) + self.rb[s].astype(F32)
        ).astype(BF)
        self.down = net.push(self.part.at[s, at.yd, at.c], self.fm.at[s], at.ym, self.ids[4])

    def done(self):
        at, s = self.at, self.s
        self.up.wait_recv()
        self.down.wait_recv()
        self.net.settle([self.side, self.a, self.b, self.up, self.down])
        return (
            self.part[s, at.y, at.c].astype(F32) + self.sibr[s, at.y].astype(F32)
        ) + (self.fp[s].astype(F32) + self.fm[s].astype(F32))


class Weight:
    def __init__(self, net, at, ref, by_row, ids):
        self.net, self.at, self.ref, self.by_row, self.ids = net, at, ref, by_row, ids
        self.rows, self.cols = ref.shape[1], ref.shape[2]
        self.state = [{}, {}]
        self.copies = []

    def sub(self, half, z, x, part):
        at = pl.ds(pl.multiple_of(x * 128, 128), 128)
        if self.by_row:
            width = self.cols // 2
            cols = pl.ds(half * width, width)
            if part is None:
                return self.ref.at[z, at, cols]
            return self.ref.at[z, pl.ds(pl.multiple_of(x * 128 + part * 64, 64), 64), cols]
        height = self.rows // 2
        if part is None:
            rows = pl.ds(half * height, height)
        else:
            rows = pl.ds(half * height + part * (height // 2), height // 2)
        return self.ref.at[z, rows, at]

    def block(self, half, index, part):
        if half == 0:
            if self.by_row:
                cols = pl.ds(0, self.cols // 2)
                rows = pl.ds(0, 512) if part is None else pl.ds(part * 256, 256)
                return self.ref.at[index, rows, cols]
            height = self.rows // 2
            rows = (
                pl.ds(0, height) if part is None else pl.ds(part * (height // 2), height // 2)
            )
            return self.ref.at[index, rows, pl.ds(0, 512)]
        zs = pl.ds(0, 4) if part is None else pl.ds(part * 2, 2)
        at = pl.ds(pl.multiple_of(index * 128, 128), 128)
        if self.by_row:
            return self.ref.at[zs, at, pl.ds(self.cols // 2, self.cols // 2)]
        return self.ref.at[zs, pl.ds(self.rows // 2, self.rows // 2), at]

    def _near(self, half, off, part):
        at = self.at
        if half == 0:
            return self.sub(0, at.z, (at.x + off) % 4, part)
        return self.sub(1, (at.z + off) % 4, at.x, part)

    def _far(self, half, off, part):
        at = self.at
        return self.block(half, ((at.z if half == 0 else at.x) + off) % 4, part)

    def _peers(self, half, first):
        at = self.at
        return (at.xp, at.xm) if (half == 0) == first else (at.zp, at.zm)

    def _push(self, ref, peer, half, k, way):
        return self.net.push(ref, ref, peer, self.ids[half * 8 + (k - 1) * 2 + way])

    def _round(self, k):
        for half in (0, 1):
            st = self.state[half]
            near = self._near if k <= 2 else self._far
            up, down = self._peers(half, k <= 2)
            if k > 1:
                st[0].wait_recv()
                st[1].wait_recv()
            if k in (1, 3):
                ref = near(half, 0, None)
                st[0] = self._push(ref, up, half, k, 0)
                st[1] = self._push(ref, down, half, k, 1)
            elif k in (2, 4):
                st[0] = self._push(near(half, 3, 0), up, half, k, 0)
                st[1] = self._push(near(half, 1, 1), down, half, k, 1)

    def step(self, k):
        first = len(self.net.copies)
        self._round(k)
        self.copies += self.net.copies[first:]

    def settle(self):
        self.net.settle(self.copies)


def rows_of(m):
    return pl.ds(pl.multiple_of(m * 256, 256), 256)


def cols_of(n):
    return pl.ds(pl.multiple_of(n * 512, 512), 512)


def heads_of(buf, s, m):
    return buf[s, pl.ds(m * 2, 2)].reshape(256, buf.shape[-1])


def rows_gather(net, at, buf, s, ids):
    return Gather(net, at, lambda y, c: buf.at[s, y, c], TOK, ids)


def rms(v, gain):
    return v * lax.rsqrt(jnp.mean(v * v, axis=-1, keepdims=True) + EPS) * gain


def rms_back(v, gain, grad):
    scale = lax.rsqrt(jnp.mean(v * v, axis=-1, keepdims=True) + EPS)
    scaled = gain * grad
    return scaled * scale - v * (
        jnp.mean(v * scaled, axis=-1, keepdims=True) * scale * scale * scale
    )


def put_part(part, s, m, z, value):
    part[s, pl.ds(m * 2, 2), :, :, cols_of(z)] = value.astype(BF).reshape(2, 2, TOK, 512)


def put_ext(part, s, pieces):
    part[s, :, :, :, D:] = jnp.zeros((4, 2, TOK, EXT), BF)
    for i, piece in enumerate(pieces):
        part[s, :, :, :, D + i * RANK : D + (i + 1) * RANK] = piece.astype(BF).reshape(
            4, 2, TOK, RANK
        )


def put_rows(buf, s, at, value, pieces):
    buf[s, at.y, at.c, :, :D] = value
    buf[s, at.y, at.c, :, D:] = jnp.zeros((TOK, EXT), BF)
    for i, piece in enumerate(pieces):
        buf[s, at.y, at.c, :, D + i * RANK : D + (i + 1) * RANK] = piece.astype(BF)


def grid_loop(m_count, n_count, body):
    def step(i, carry):
        body(i // n_count, i % n_count)
        return carry

    lax.fori_loop(0, m_count * n_count, step, 0)


def layer(
    index_ref, length_ref,
    tok, cot, again, fgain, inv,
    wq, wo, wg, wu, wd,
    qin, gin, uin, aout, dout, ain, din, qout, gout, uout,
    result_o, igrad_o, sums1_o, sums2_o,
    w_q, w_o, w_g, w_u, w_d,
    nb, cb, part1, sib1, sib2, ra1, rb1, fp1, fm1, ra2, rb2, fp2, fm2,
    gate, up, hidden, qb, kvb, attn, lse, cosb, sinb, startb,
    midf, normed, midn, inner_a, mgrad, next_s, mid_s, cot_s, dkv, halo_in,
    a_b, d_b, q_b, g_b, u_b,
    full1, full1_in, vec1, vec1_in, full2, full2_in, vec2, vec2_in, px, px_in,
    send, recv, local,
):
    at = Place()
    net = Net(send, recv)
    pick = [index_ref[0], index_ref[1]]
    h, b = at.h, at.b
    both = (0, 1)

    here = pl.ds(pl.multiple_of(at.x * 128, 128), 128)
    loads = []

    def load(src, dst):
        copy = pltpu.make_async_copy(src, dst, local.at[len(loads)])
        copy.start()
        loads.append(copy)

    load(wq, w_q.at[at.z, here, :])
    load(wo, w_o.at[at.z, :, here])
    load(wg, w_g.at[at.z, here, :])
    load(wu, w_u.at[at.z, here, :])
    load(wd, w_d.at[at.z, :, here])
    load(qout.at[:, :, pl.ds(pl.multiple_of(h * 512, 512), 512)], q_b)
    load(ain.at[:, :, pl.ds(pl.multiple_of(h * 256, 256), 256)], a_b)
    load(din.at[:, :, pl.ds(pl.multiple_of(h * 1024, 1024), 1024)], d_b)
    load(gout.at[:, :, pl.ds(pl.multiple_of(h * 1024, 1024), 1024)], g_b)
    load(uout.at[:, :, pl.ds(pl.multiple_of(h * 1024, 1024), 1024)], u_b)
    at.greet(
        [((h + k) % 8, b) for k in range(1, 8)] + [(h, (b + k) % 16) for k in range(1, 16)]
    )

    q_ids = net.ids(16)
    W_Q = Weight(net, at, w_q, True, q_ids)
    W_O = Weight(net, at, w_o, False, net.ids(16))
    W_G = Weight(net, at, w_g, True, net.ids(16))
    W_U = Weight(net, at, w_u, True, net.ids(16))
    W_D = Weight(net, at, w_d, False, net.ids(16))
    n_ids = [net.ids(9), net.ids(9)]
    c_ids = [net.ids(9), net.ids(9)]
    s_ids = [net.ids(5), net.ids(5)]
    t_ids = [net.ids(5), net.ids(5)]
    near_ids = net.ids(7)
    halo_ids = net.ids(8)
    px_ids = net.ids(2)
    out1, out2 = w_g.at[:, :, pl.ds(0, 512)], w_u.at[:, :, pl.ds(0, 128)]
    fold1 = Fold(net, at, full1, full1_in, vec1, vec1_in, out1, near_ids)
    fold2 = Fold(net, at, full2, full2_in, vec2, vec2_in, out2, near_ids)
    set1, set2 = (sib1, ra1, rb1, fp1, fm1), (sib2, ra2, rb2, fp2, fm2)

    def norm_in(s):
        n = rms(tok[s].astype(F32), again[...]).astype(BF)
        normed[s] = n
        put_rows(nb, s, at, n, [mm_nt(n, qin[pick[s]])])

    sign = jnp.where(lax.broadcasted_iota(jnp.int32, (1, 128), 1) < 64, -1.0, 1.0)

    def table(s, m):
        rows = pl.ds(pl.multiple_of(m * 64, 64), 64)
        pos = b * SPAN + m * 64 + lax.broadcasted_iota(jnp.int32, (64, 1), 0)
        start = jnp.zeros((64, 1), jnp.int32)
        end = 0
        for d in range(4):
            length = length_ref[s, d]
            end = end + length
            start = start + jnp.where(pos >= end, length, 0)
        startb[s, rows] = start
        angle = (pos - start).astype(F32) * inv[...]
        cosb[s, rows] = jnp.cos(angle)
        sinb[s, rows] = jnp.sin(angle) * sign

    def cot_in(s):
        put_rows(cb, s, at, cot[s], [mm_nt(cot[s], dout[pick[s]])])

    def qkv(s):
        def step(m, unused):
            x = heads_of(nb, s, m)
            r = mm(x[:, :D], w_q[...].reshape(D, 512)) + mm(x[:, D : D + RANK], q_b[pick[s]])
            rows = rows_of(m)
            c, sn = cosb[s, rows], sinb[s, rows]

            def rot(v):
                return v * c + pltpu.roll(v, 64, 1) * sn

            for j in both:
                qb[s, j, rows] = (rot(r[:, j * 128 : (j + 1) * 128]) * SCALE).astype(BF)
            own = pl.ds(pl.multiple_of(1024 + m * 256, 256), 256)
            kvb[s, 0, own] = rot(r[:, 256:384]).astype(BF)
            kvb[s, 1, own] = r[:, 384:512].astype(BF)

        grid_loop(2, 1, step)
        next_s[s] = nb[s, :, :, :, D:].reshape(SPAN, EXT)

    def halo(s):
        own = kvb.at[s, :, pl.ds(1024, 512)]
        return [
            net.push(own, kvb.at[s, :, pl.ds(512, 512)], at.next1, halo_ids[2 * s]),
            net.push(own, kvb.at[s, :, pl.ds(0, 512)], at.next2, halo_ids[2 * s + 1]),
        ]

    row = lax.broadcasted_iota(jnp.int32, (256, 1280), 0)
    col = lax.broadcasted_iota(jnp.int32, (256, 1280), 1)

    def allowed(s, m):
        low = startb[s, rows_of(m)] - (b * SPAN - WINDOW + m * 256)
        gap = row - col + WINDOW
        return (gap >= 0) & (gap < WINDOW) & (col >= low)

    def keys_of(m):
        return pl.ds(pl.multiple_of(m * 256, 256), 1280)

    def attend(s, g):
        def step(m, unused):
            rows, keys = rows_of(m), keys_of(m)
            sc = mm_nt(qb[s, g, rows], kvb[s, 0, keys])
            sc = jnp.where(allowed(s, m), sc, -1e30)
            top = jnp.max(sc, axis=-1, keepdims=True)
            e = jnp.exp(sc - top)
            total = jnp.sum(e, axis=-1, keepdims=True)
            p = (e * (1.0 / total)).astype(BF)
            o = mm(p, kvb[s, 1, keys])
            attn[s, rows, g * 128 : (g + 1) * 128] = o.astype(BF)
            lse[s, g, rows] = top + jnp.log(total)

        grid_loop(2, 1, step)

    def out_proj(s):
        grid_loop(
            2, 4, lambda m, z: put_part(part1, s, m, z, mm(attn[s, rows_of(m)], w_o[z]))
        )
        put_ext(part1, s, [mm_nt(attn[s], a_b[pick[s]])])
        return Scatter(net, at, part1, s, set1, s_ids[s])

    def middle(s, t):
        inn = t[:, D : D + RANK]
        inner_a[s] = inn
        mid = tok[s].astype(F32) + t[:, :D] + mm(inn.astype(BF), aout[pick[s]])
        midf[s] = mid
        n = rms(mid, fgain[...]).astype(BF)
        midn[s] = n
        put_rows(nb, s, at, n, [mm_nt(n, gin[pick[s]]), mm_nt(n, uin[pick[s]])])
        return rows_gather(net, at, nb, s, n_ids[s])

    def ffn(s):
        def step(m, n):
            x = heads_of(nb, s, m)
            rows, cols = rows_of(m), cols_of(n)
            g = mm(x[:, :D], w_g[:, :, cols].reshape(D, 512))
            g = g + mm(x[:, D : D + RANK], g_b[pick[s], :, cols])
            u = mm(x[:, :D], w_u[:, :, cols].reshape(D, 512))
            u = u + mm(x[:, D + RANK : D + 2 * RANK], u_b[pick[s], :, cols])
            gate[s, rows, cols] = g.astype(BF)
            up[s, rows, cols] = u.astype(BF)
            hidden[s, rows, cols] = (g * jax.nn.sigmoid(g) * u).astype(BF)

        grid_loop(2, 2, step)
        mid_s[s] = nb[s, :, :, :, D:].reshape(SPAN, EXT)

    def hid_back(s):
        def step(m, n):
            x = heads_of(cb, s, m)
            rows, cols = rows_of(m), cols_of(n)
            hb = mm(x[:, D : D + RANK], d_b[pick[s], :, cols])
            for z in range(4):
                hb = hb + mm_nt(x[:, z * 512 : (z + 1) * 512], w_d[z, cols, :])
            g = gate[s, rows, cols].astype(F32)
            u = up[s, rows, cols].astype(F32)
            sg = jax.nn.sigmoid(g)
            gate[s, rows, cols] = (hb * u * sg * (1.0 + g * (1.0 - sg))).astype(BF)
            up[s, rows, cols] = (hb * g * sg).astype(BF)

        grid_loop(2, 2, step)
        cot_s[s] = cb[s, :, :, :, D:].reshape(SPAN, EXT)

    def mid_back(s):
        def step(m, z):
            rows = rows_of(m)
            put_part(part1, s, m, z, mm_nt(gate[s, rows], w_g[z]) + mm_nt(up[s, rows], w_u[z]))

        grid_loop(2, 4, step)
        put_ext(part1, s, [mm_nt(gate[s], g_b[pick[s]]), mm_nt(up[s], u_b[pick[s]])])
        return Scatter(net, at, part1, s, set1, s_ids[s])

    def down(s):
        grid_loop(2, 4, lambda m, z: put_part(nb, s, m, z, mm(hidden[s, rows_of(m)], w_d[z])))
        put_ext(nb, s, [mm_nt(hidden[s], d_b[pick[s]])])

    def wide_terms(s):
        terms = [
            mm_tn(mid_s[s], gate[s])[:RANK],
            mm_tn(mid_s[s], up[s])[RANK : 2 * RANK],
            mm_tn(cot_s[s], hidden[s])[:RANK],
        ]
        for i, term in enumerate(terms):
            for j in range(4):
                vec1[3 + 4 * i + j, :, s * 256 : (s + 1) * 256] = term[
                    :, j * 256 : (j + 1) * 256
                ].astype(BF)

    def slices(full, i, s, term):
        for j in range(8):
            full[j, i, :, s * 256 : (s + 1) * 256] = term[:, j * 256 : (j + 1) * 256].astype(BF)

    def middle_back(s, t):
        pg, pu = t[:, D : D + RANK].astype(BF), t[:, D + RANK : D + 2 * RANK].astype(BF)
        back = t[:, :D] + mm(pg, gin[pick[s]]) + mm(pu, uin[pick[s]])
        mg = cot[s].astype(F32) + rms_back(midf[s], fgain[...], back)
        mgrad[s] = mg
        bg = mg.astype(BF)
        put_rows(cb, s, at, bg, [mm_nt(bg, aout[pick[s]])])
        gather = rows_gather(net, at, cb, s, n_ids[s])
        slices(full1, 0, s, mm_tn(pg, midn[s]))
        slices(full1, 1, s, mm_tn(pu, midn[s]))
        slices(full1, 2, s, mm_tn(inner_a[s].astype(BF), bg))
        return gather

    def attn_back(s):
        def step(m, unused):
            x = heads_of(cb, s, m)
            r = mm(x[:, D : D + RANK], a_b[pick[s]])
            for z in range(4):
                r = r + mm_nt(x[:, z * 512 : (z + 1) * 512], w_o[z])
            hidden[s, rows_of(m), 512:768] = r.astype(BF)

        grid_loop(2, 1, step)
        e = cb[s, :, :, :, D:].reshape(SPAN, EXT)
        vec1[15, :, s * 256 : (s + 1) * 256] = mm_tn(e, attn[s])[:RANK].astype(BF)

    def attend_back(s, g):
        if g == 0:
            dkv[...] = jnp.zeros(dkv.shape, F32)

        def step(m, unused):
            rows, keys = rows_of(m), keys_of(m)
            q, k = qb[s, g, rows], kvb[s, 0, keys]
            do = hidden[s, rows, 512 + g * 128 : 640 + g * 128]
            p = jnp.where(allowed(s, m), jnp.exp(mm_nt(q, k) - lse[s, g, rows]), 0.0)
            vg = mm_nt(do, kvb[s, 1, keys])
            delta = jnp.sum(p * vg, axis=-1, keepdims=True)
            sg = (p * (vg - delta)).astype(BF)
            dq = mm(sg, k) * SCALE
            hidden[s, rows, g * 128 : (g + 1) * 128] = (
                dq * cosb[s, rows] - pltpu.roll(dq, 64, 1) * sinb[s, rows]
            ).astype(BF)
            dkv[0, keys] += mm_tn(sg, q)
            dkv[1, keys] += mm_tn(p.astype(BF), do)

        grid_loop(2, 1, step)

    def halo_back(s):
        copies = []
        for hop in (2, 1, 0):
            for i in both:
                at_col = hop * 256 + i * 128
                gate[s, :, at_col : at_col + 128] = dkv[
                    i, (2 - hop) * SPAN : (3 - hop) * SPAN
                ].astype(BF)
            if hop > 0:
                copies.append(
                    net.push(
                        gate.at[s, :, pl.ds(hop * 256, 256)],
                        halo_in.at[s, hop - 1],
                        at.prev1 if hop == 1 else at.prev2,
                        halo_ids[4 + 2 * s + hop - 1],
                    )
                )
        return copies

    def qkv_back(s):
        def keys(m, unused):
            rows = rows_of(m)
            dk, dv = [
                gate[s, rows, i * 128 : (i + 1) * 128].astype(F32)
                + halo_in[s, 0, rows, i * 128 : (i + 1) * 128].astype(F32)
                + halo_in[s, 1, rows, i * 128 : (i + 1) * 128].astype(F32)
                for i in both
            ]
            hidden[s, rows, 256:384] = (
                dk * cosb[s, rows] - pltpu.roll(dk, 64, 1) * sinb[s, rows]
            ).astype(BF)
            hidden[s, rows, 384:512] = dv.astype(BF)

        grid_loop(2, 1, keys)
        raw = hidden[s, :, :512]
        px[s] = jnp.zeros(px.shape[1:], BF)
        px[s, :, :, :RANK] = mm_nt(raw, q_b[pick[s]]).astype(BF).reshape(8, TOK, RANK)
        pairs = []
        for k in range(1, 8):
            peer = (h + k) % 8
            pairs.append((px.at[s, peer], px_in.at[s, k - 1], (peer, b)))
        exchange = net.spread(pairs, px_in.at[s], px_ids[s])
        grid_loop(
            2, 4, lambda m, z: put_part(part1, s, m, z, mm_nt(hidden[s, rows_of(m), :512], w_q[z]))
        )
        scatter = Scatter(net, at, part1, s, set1, s_ids[s])
        term = mm_tn(next_s[s], raw)[:RANK]
        for j in range(4):
            vec2[s * 8 + 4 + j] = term[:, j * 128 : (j + 1) * 128].astype(BF)
        return scatter, exchange

    def finish_result(s, t):
        inn = t[:, D : D + RANK].astype(BF)
        midf[s] = midf[s] + t[:, :D] + mm(inn, dout[pick[s]])
        slices(full2, 1, s, mm_tn(inn, cot[s]))

    def p_sum(s, exchange):
        exchange.wait_recv()
        total = px[s, h].astype(F32)
        for k in range(7):
            total = total + px_in[s, k].astype(F32)
        p = total[:, :RANK].astype(BF)
        slices(full2, 0, s, mm_tn(p, normed[s]))
        return p

    def finish_grad(s, t, p):
        back = t[:, :D] + mm(p, qin[pick[s]])
        mgrad[s] = mgrad[s] + rms_back(tok[s].astype(F32), again[...], back)

    loads[0].wait()
    loads[1].wait()
    W_Q.step(1)
    W_O.step(1)
    norm_in(0)
    n0 = rows_gather(net, at, nb, 0, n_ids[0])
    for copy in loads[2:5]:
        copy.wait()
    W_G.step(1)
    W_Q.step(2)
    W_O.step(2)
    norm_in(1)
    grid_loop(2, 8, table)
    W_Q.step(3)
    n0.relay()
    n1 = rows_gather(net, at, nb, 1, n_ids[1])
    W_G.step(2)
    W_U.step(1)
    W_O.step(3)
    cot_in(0)
    cot_in(1)
    n0.last()
    n1.relay()
    c0 = rows_gather(net, at, cb, 0, c_ids[0])
    W_Q.step(4)
    W_G.step(3)
    for copy in loads[5:]:
        copy.wait()
    n0.done()
    W_Q.step(5)
    qkv(0)
    halo0 = halo(0)
    W_O.step(4)
    W_U.step(2)
    W_D.step(1)
    n1.last()
    c0.relay()
    c1 = rows_gather(net, at, cb, 1, c_ids[1])
    n1.done()
    qkv(1)
    halo1 = halo(1)
    W_U.step(3)
    W_D.step(2)
    n0.settle()
    n1.settle()
    c0.last()
    W_O.step(5)
    W_G.step(4)
    for copy in halo0:
        copy.wait_recv()
    attend(0, 0)
    c1.relay()
    attend(0, 1)
    s0 = out_proj(0)
    c1.last()
    for copy in halo1:
        copy.wait_recv()
    attend(1, 0)
    s0.merge()
    attend(1, 1)
    s1 = out_proj(1)
    s0.relay()
    W_D.step(3)
    s1.merge()
    m0 = middle(0, s0.done())
    s1.relay()
    W_U.step(4)
    m0.relay()
    c0.done()
    c1.done()
    m1 = middle(1, s1.done())
    W_G.step(5)
    m0.last()
    m1.relay()
    W_D.step(4)
    m0.done()
    m1.last()
    W_U.step(5)
    ffn(0)
    m1.done()
    ffn(1)
    W_D.step(5)
    for item in (c0, c1, m0, m1, W_Q, W_G, W_U):
        item.settle()
    hid_back(0)
    s0 = mid_back(0)
    hid_back(1)
    s0.merge()
    s1 = mid_back(1)
    s0.relay()
    down(0)
    s1.merge()
    down(1)
    b0 = middle_back(0, s0.done())
    s1.relay()
    wide_terms(0)
    wide_terms(1)
    b0.relay()
    b1 = middle_back(1, s1.done())
    fold1.heads()
    b0.last()
    r0 = Scatter(net, at, nb, 0, set2, t_ids[0])
    r1 = Scatter(net, at, nb, 1, set2, t_ids[1])
    b0.done()
    attn_back(0)
    attend_back(0, 0)
    b1.relay()
    attend_back(0, 1)
    back0 = halo_back(0)
    b1.last()
    vec1[0:3] = fold1.heads_sum().astype(BF)
    b1.done()
    attn_back(1)
    fold1.blocks()
    r0.merge()
    r1.merge()
    attend_back(1, 0)
    fold1.blocks_sum()
    r0.relay()
    attend_back(1, 1)
    back1 = halo_back(1)
    b0.settle()
    b1.settle()
    for copy in back0:
        copy.wait_recv()
    s0, x0 = qkv_back(0)
    r1.relay()
    fold1.near_done()
    spread = Weight(net, at, out1, True, q_ids)
    spread.step(1)
    s0.merge()
    finish_result(0, r0.done())
    for copy in back1:
        copy.wait_recv()
    s1, x1 = qkv_back(1)
    spread.step(2)
    s0.relay()
    s1.merge()
    finish_result(1, r1.done())
    p0 = p_sum(0, x0)
    p1 = p_sum(1, x1)
    fold2.heads()
    spread.step(3)
    s1.relay()
    total = fold2.heads_sum()
    for i in both:
        for s in both:
            for j in both:
                vec2[s * 8 + 2 * i + j] = total[
                    i, :, s * 256 + j * 128 : s * 256 + (j + 1) * 128
                ].astype(BF)
    fold2.blocks()
    finish_grad(0, s0.done(), p0)
    spread.step(4)
    fold2.blocks_sum()
    finish_grad(1, s1.done(), p1)
    fold2.near_done()
    fold2.far((c_ids[0] + c_ids[1])[:15])
    spread.step(5)
    writes = [
        pltpu.make_async_copy(midf, result_o, local.at[0]),
        pltpu.make_async_copy(mgrad, igrad_o, local.at[1]),
        pltpu.make_async_copy(out1, sums1_o, local.at[2]),
    ]
    for copy in writes:
        copy.start()
    fold2.far_done()
    writes.append(pltpu.make_async_copy(out2, sums2_o, local.at[3]))
    writes[3].start()
    net.drain()
    for copy in writes:
        copy.wait()


def call_layer(args):
    vm = lambda *shape, t=BF: pltpu.VMEM(shape, t)
    rs = lambda: [vm(2, TOK // 2, CW), vm(2, TOK // 2, CW), vm(2, TOK, CW), vm(2, TOK, CW)]
    outs = [((2, TOK, D), F32), ((2, TOK, D), F32), ((4, 512, 512), BF), ((4, 512, 128), BF)]
    scratch = (
        [vm(4, 512, 512), vm(4, 256, 512), vm(4, 512, 1024), vm(4, 512, 1024), vm(4, 1024, 512)]
        + [vm(2, 4, 2, TOK, CW)] * 3
        + [vm(2, 4, TOK, D + EXT), vm(2, 4, TOK, D + EXT)]
        + rs() + rs()
        + [vm(2, SPAN, 1024)] * 3
        + [vm(2, 2, SPAN, 128), vm(2, 2, 1536, 128), vm(2, SPAN, 256), vm(2, 2, SPAN, 1, t=F32)]
        + [vm(2, SPAN, 128, t=F32)] * 2
        + [vm(2, SPAN, 1, t=jnp.int32)]
        + [vm(2, TOK, D, t=F32), vm(2, TOK, D), vm(2, TOK, D), vm(2, TOK, RANK, t=F32)]
        + [vm(2, TOK, D, t=F32)] + [vm(2, SPAN, EXT)] * 3
        + [vm(2, 1536, 128, t=F32), vm(2, 2, SPAN, 256)]
        + [vm(2, RANK, 256), vm(2, RANK, 1024), vm(2, RANK, 512), vm(2, RANK, 1024), vm(2, RANK, 1024)]
        + [vm(8, 3, RANK, 512), vm(7, 3, RANK, 512), vm(16, RANK, 512), vm(15, RANK, 512)]
        + [vm(8, 2, RANK, 512), vm(7, 2, RANK, 512), vm(16, RANK, 128), vm(15, RANK, 128)]
        + [vm(2, 8, TOK, EXT), vm(2, 7, TOK, EXT)]
        + [pltpu.SemaphoreType.DMA((N_SEMS,)), pltpu.SemaphoreType.DMA((N_SEMS,)), pltpu.SemaphoreType.DMA((10,))]
    )
    smem = pl.BlockSpec(memory_space=pltpu.SMEM)
    vmem = pl.BlockSpec(memory_space=pltpu.VMEM)
    hbm = pl.BlockSpec(memory_space=pl.ANY)
    return pl.pallas_call(
        layer,
        out_shape=[jax.ShapeDtypeStruct(shape, kind) for shape, kind in outs],
        in_specs=[smem] * 2 + [vmem] * 5 + [hbm] * 5 + [vmem] * 5 + [hbm] * 5,
        out_specs=[hbm] * len(outs),
        scratch_shapes=scratch,
        compiler_params=pltpu.CompilerParams(
            collective_id=0, has_side_effects=True, vmem_limit_bytes=VMEM_BYTES
        ),
    )(*args)


def unpack(
    index_ref, result, igrad, sums1, sums2,
    result_o, igrad_o, qi_o, qo_o, ai_o, ao_o, gi_o, go_o, ui_o, uo_o, di_o, do_o, sem,
):
    copies = [
        pltpu.make_async_copy(result, result_o, sem.at[0]),
        pltpu.make_async_copy(igrad, igrad_o, sem.at[1]),
    ]
    for copy in copies:
        copy.start()
    swap = index_ref[0] == 1

    def emit(out, cols, first, second):
        first, second = first.astype(F32), second.astype(F32)
        out[0, :, cols] = jnp.where(swap, second, first)
        out[1, :, cols] = jnp.where(swap, first, second)

    def found(ref, j, head, width):
        row0 = (j % 4) * 128 + head * RANK
        return ref[j // 4, row0 : row0 + RANK, :width]

    for head in range(8):
        for j, out in ((0, gi_o), (1, ui_o), (2, ao_o), (15, ai_o)):
            block = found(sums1, j, head, 512)
            emit(out, pl.ds(head * 256, 256), block[:, :256], block[:, 256:])
        for i, out in enumerate([go_o, uo_o, di_o]):
            for k in range(4):
                block = found(sums1, 3 + 4 * i + k, head, 512)
                emit(out, pl.ds(head * 1024 + k * 256, 256), block[:, :256], block[:, 256:])
        for j, out, width in (
            (0, qi_o, 256), (1, qi_o, 256), (2, do_o, 256), (3, do_o, 256),
            (4, qo_o, 512), (5, qo_o, 512), (6, qo_o, 512), (7, qo_o, 512),
        ):
            cols = pl.ds(head * width + (j % (width // 128)) * 128, 128)
            emit(out, cols, found(sums2, j, head, 128), found(sums2, 8 + j, head, 128))
    for copy in copies:
        copy.wait()


def call_unpack(index, arrays):
    narrow, wide = (2, RANK, D), (2, RANK, 8192)
    outs = [
        (2, TOK, D), (2, TOK, D), narrow, (2, RANK, 4096), narrow, narrow,
        narrow, wide, narrow, wide, wide, narrow,
    ]
    smem = pl.BlockSpec(memory_space=pltpu.SMEM)
    vmem = pl.BlockSpec(memory_space=pltpu.VMEM)
    hbm = pl.BlockSpec(memory_space=pl.ANY)
    return pl.pallas_call(
        unpack,
        out_shape=[jax.ShapeDtypeStruct(shape, F32) for shape in outs],
        in_specs=[smem] + [vmem] * 4,
        out_specs=[hbm, hbm] + [vmem] * 10,
        scratch_shapes=[pltpu.SemaphoreType.DMA((2,))],
        compiler_params=pltpu.CompilerParams(vmem_limit_bytes=VMEM_BYTES),
    )(index, *arrays)


def body(
    tokens, cotangent, doc_lengths, adapter_index, attn_gain, ffn_gain,
    w_qkv, w_out, w_gate, w_up, w_down,
    qkv_in, qkv_out, attn_in, attn_out, gate_in, gate_out, up_in, up_out, down_in, down_out,
):
    flip = lambda g: jnp.swapaxes(g, 1, 2)
    half = np.arange(64, dtype=np.float32) * np.float32(2.0 / 128)
    inverse = np.power(np.float32(THETA), -half).astype(np.float32)
    inv = jnp.asarray(np.concatenate([inverse, inverse])[None])
    index = adapter_index.reshape(2)
    arrays = call_layer((
        index, doc_lengths, tokens, cotangent, attn_gain[None], ffn_gain[None], inv,
        w_qkv, w_out, w_gate, w_up, w_down,
        flip(qkv_in), flip(gate_in), flip(up_in), attn_out, down_out, flip(attn_in), flip(down_in),
        qkv_out, gate_out, up_out,
    ))
    result, igrad, qi, qo, ai, ao, gi, go, ui, uo, di, do = call_unpack(index, arrays)
    return (
        result, igrad, flip(qi), qo, flip(ai), ao, flip(gi), go, flip(ui), uo, flip(di), do
    )


def solution(mesh):
    row = P(None, ("blk", "head"), None)
    return jax.shard_map(
        body,
        mesh=mesh,
        in_specs=(row, row) + (P(),) * 4
        + (P("blk", "head"), P("head", "blk"), P("blk", "head"), P("blk", "head"), P("head", "blk"))
        + (P(),) * 10,
        out_specs=(row, row) + (P(),) * 10,
        check_vma=False,
    )
```

```python
from functools import partial

import jax
import jax.numpy as jnp
import numpy as np
from jax import lax
from jax.experimental import pallas as pl
from jax.experimental.pallas import tpu as pltpu
from jax.sharding import PartitionSpec as P

MESH = pl.DeviceIdType.MESH
BF = jnp.bfloat16
F32 = jnp.float32
D = 2048
EXT = 128
CW = D + EXT
RANK = 16
WINDOW = 1024
EPS = 1e-05
THETA = 1000000.0
Y, CORES, Z, X = 4, 2, 4, 4
TOK = 64
SPAN = 512
SCALE = 128 ** (-0.5)
VMEM_BYTES = 66977792
N_SEMS = 159


def mm(a, b):
    return jnp.dot(a, b, preferred_element_type=F32)


def mm_nt(a, b):
    return lax.dot_general(a, b, (((1,), (1,)), ((), ())), preferred_element_type=F32)


def mm_tn(a, b):
    return lax.dot_general(a, b, (((0,), (0,)), ((), ())), preferred_element_type=F32)


class Place:
    def __init__(self):
        h = lax.axis_index("head")
        b = lax.axis_index("blk")
        self.h, self.b = h, b
        self.y, self.c = h // 2, h % 2
        self.z, self.x = b // 4, b % 4
        y, c, z, x = self.y, self.c, self.z, self.x
        self.yu, self.yd, self.yo = (y + 1) % 4, (y + 3) % 4, (y + 2) % 4
        self.xu, self.xd = (x + 1) % 4, (x + 3) % 4
        self.zu, self.zd = (z + 1) % 4, (z + 3) % 4
        self.sib = (y * 2 + (1 - c), b)
        self.yp, self.ym = (self.yu * 2 + c, b), (self.yd * 2 + c, b)
        self.xp, self.xm = (h, z * 4 + self.xu), (h, z * 4 + self.xd)
        self.zp, self.zm = (h, self.zu * 4 + x), (h, self.zd * 4 + x)
        self.next1, self.next2 = (h, (b + 1) % 16), (h, (b + 2) % 16)
        self.prev1, self.prev2 = (h, (b + 15) % 16), (h, (b + 14) % 16)

    def greet(self, peers):
        barrier = pltpu.get_barrier_semaphore()
        for peer in peers:
            pl.semaphore_signal(barrier, inc=1, device_id=peer, device_id_type=MESH)
        pl.semaphore_wait(barrier, len(peers))


class Net:
    def __init__(self, send, recv):
        self.send, self.recv, self.count, self.copies = send, recv, 0, []

    def ids(self, n):
        first = self.count
        self.count += n
        return list(range(first, first + n))

    def make(self, src, dst, peer, i):
        return pltpu.make_async_remote_copy(
            src_ref=src,
            dst_ref=dst,
            send_sem=self.send.at[i],
            recv_sem=self.recv.at[i],
            device_id=peer,
            device_id_type=MESH,
        )

    def push(self, src, dst, peer, i):
        copy = self.make(src, dst, peer, i)
        copy.start()
        self.copies.append(copy)
        return copy

    def spread(self, pairs, whole, i):
        for src, dst, peer in pairs:
            self.make(src, dst, peer, i).start()
        copy = self.make(whole, whole, pairs[0][2], i)
        self.copies.append(copy)
        return copy

    def settle(self, copies):
        for copy in copies:
            copy.wait_send()
            self.copies = [other for other in self.copies if other is not copy]

    def drain(self):
        self.settle(list(self.copies))


class Gather:
    def __init__(self, net, at, slot, extent, ids):
        self.net, self.at, self.slot, self.half, self.ids = net, at, slot, extent // 2, ids
        own = slot(at.y, at.c)
        self.up = net.push(own, own, at.yp, ids[0])
        self.down = net.push(own, own, at.ym, ids[1])
        self.side = [net.push(own, own, at.sib, ids[2])]

    def relay(self):
        at, net, half, ids = self.at, self.net, self.half, self.ids
        below = self.slot(at.yd, at.c)
        above = self.slot(at.yu, at.c)
        self.up.wait_recv()
        part = below.at[pl.ds(0, half)]
        self.far_a = net.push(part, part, at.yp, ids[3])
        self.side.append(net.push(below, below, at.sib, ids[4]))
        self.down.wait_recv()
        part = above.at[pl.ds(half, half)]
        self.far_b = net.push(part, part, at.ym, ids[5])
        self.side.append(net.push(above, above, at.sib, ids[6]))

    def last(self):
        at, net, half, ids = self.at, self.net, self.half, self.ids
        far = self.slot(at.yo, at.c)
        self.far_a.wait_recv()
        part = far.at[pl.ds(0, half)]
        self.side.append(net.push(part, part, at.sib, ids[7]))
        self.far_b.wait_recv()
        part = far.at[pl.ds(half, half)]
        self.side.append(net.push(part, part, at.sib, ids[8]))

    def done(self):
        for copy in self.side:
            copy.wait_recv()

    def settle(self):
        self.net.settle([self.up, self.down, self.far_a, self.far_b] + self.side)


class Fold:
    def __init__(self, net, at, full, full_in, vec, vec_in, out, near):
        self.net, self.at = net, at
        self.full, self.full_in, self.vec, self.vec_in, self.out = full, full_in, vec, vec_in, out
        self.ids, self.near = net.ids(2), near

    def heads(self):
        at = self.at
        pairs = []
        for k in range(1, 8):
            peer = (at.h + k) % 8
            pairs.append((self.full.at[peer], self.full_in.at[k - 1], (peer, at.b)))
        self.copy = self.net.spread(pairs, self.full_in, self.ids[0])

    def heads_sum(self):
        self.copy.wait_recv()
        total = self.full[self.at.h].astype(F32)
        for k in range(7):
            total = total + self.full_in[k].astype(F32)
        return total

    def blocks(self):
        at = self.at
        pairs = []
        for k in range(1, 16):
            peer = (at.b + k) % 16
            pairs.append((self.vec.at[peer], self.vec_in.at[k - 1], (at.h, peer)))
        self.copy = self.net.spread(pairs, self.vec_in, self.ids[1])

    def blocks_sum(self):
        at = self.at
        self.copy.wait_recv()
        total = self.vec[at.b].astype(F32)
        for k in range(15):
            total = total + self.vec_in[k].astype(F32)
        row = at.c * 256 + at.x * 64 + at.y * 16
        own = self.out.at[at.z, pl.ds(pl.multiple_of(row, 16), 16)]
        own[...] = total.astype(BF)
        self.copies = [
            self.net.push(own, own, (((at.y + k) % 4) * 2 + at.c, at.b), self.near[k - 1])
            for k in range(1, 4)
        ]

    def near_done(self):
        for copy in self.copies:
            copy.wait_recv()
        self.net.settle(self.copies)

    def far(self, ids):
        at = self.at
        own = self.out.at[at.z, pl.ds(pl.multiple_of(at.c * 256 + at.x * 64, 64), 64)]
        self.copies = [
            self.net.push(own, own, (at.h, (at.b + k) % 16), ids[k - 1]) for k in range(1, 16)
        ]

    def across(self, i):
        at = self.at
        for copy in self.copies:
            copy.wait_recv()
        own = self.out.at[:, pl.ds(pl.multiple_of(at.c * 256, 256), 256)]
        self.copies = [self.net.push(own, own, at.sib, i)]

    def done(self):
        self.copies[0].wait_recv()


class Scatter:
    def __init__(self, net, at, part, s, bufs, ids, width):
        self.net, self.at, self.ids, self.width = net, at, ids, width
        cols = pl.ds(0, width)
        self.part = part.at[s, :, :, :, cols]
        self.sibr, self.ra, self.rb, self.fp, self.fm = [
            buf.at[s, :, :, cols] if i == 0 else buf.at[s, :, cols] for i, buf in enumerate(bufs)
        ]
        self.side = []

    def send(self, m):
        ys = pl.ds(m * 2, 2)
        self.side.append(
            self.net.push(
                self.part.at[ys, 1 - self.at.c],
                self.sibr.at[ys],
                self.at.sib,
                self.ids[0 if not self.side else 5],
            )
        )

    def _merge(self, y):
        c = self.at.c
        self.part[y, c] = (self.part[y, c].astype(F32) + self.sibr[y].astype(F32)).astype(BF)

    def merge(self):
        at, net = self.at, self.net
        self.side[0].wait_recv()
        self._merge(at.yo)
        far = self.part.at[at.yo, at.c]
        self.a = net.push(far.at[pl.ds(0, TOK // 2)], self.ra, at.yp, self.ids[1])
        self.b = net.push(far.at[pl.ds(TOK // 2, TOK // 2)], self.rb, at.ym, self.ids[2])
        self.side[1].wait_recv()
        self._merge(at.yu)
        self._merge(at.yd)

    def relay(self):
        at, net = self.at, self.net
        self.a.wait_recv()
        half = pl.ds(0, TOK // 2)
        self.part[at.yu, at.c, half] = (
            self.part[at.yu, at.c, half].astype(F32) + self.ra[...].astype(F32)
        ).astype(BF)
        self.up = net.push(self.part.at[at.yu, at.c], self.fp, at.yp, self.ids[3])
        self.b.wait_recv()
        half = pl.ds(TOK // 2, TOK // 2)
        self.part[at.yd, at.c, half] = (
            self.part[at.yd, at.c, half].astype(F32) + self.rb[...].astype(F32)
        ).astype(BF)
        self.down = net.push(self.part.at[at.yd, at.c], self.fm, at.ym, self.ids[4])

    def done(self):
        at = self.at
        self.up.wait_recv()
        self.down.wait_recv()
        self.net.settle(self.side + [self.a, self.b, self.up, self.down])
        return (self.part[at.y, at.c].astype(F32) + self.sibr[at.y].astype(F32)) + (
            self.fp[...].astype(F32) + self.fm[...].astype(F32)
        )


class Weight:
    def __init__(self, net, at, ref, by_row, ids, cut=None):
        self.net, self.at, self.ref, self.by_row, self.ids = net, at, ref, by_row, ids
        self.rows, self.cols = ref.shape[1], ref.shape[2]
        self.state = [{}, {}]
        size = self.cols if by_row else self.rows
        cut = cut or size // 2
        self.spans = [(0, cut), (cut, size - cut)]
        self.copies = []

    def sub(self, half, z, x, part):
        first, size = self.spans[half]
        at = pl.ds(pl.multiple_of(x * 128, 128), 128)
        if self.by_row:
            cols = pl.ds(first, size)
            if part is None:
                return self.ref.at[z, at, cols]
            return self.ref.at[z, pl.ds(pl.multiple_of(x * 128 + part * 64, 64), 64), cols]
        if part is None:
            rows = pl.ds(first, size)
        else:
            rows = pl.ds(first + part * (size // 2), size // 2)
        return self.ref.at[z, rows, at]

    def block(self, half, index, part):
        first, size = self.spans[half]

        def cut(start, extent):
            if part is None:
                return pl.ds(start, extent)
            low = extent * 3 // 8
            return pl.ds(start, low) if part == 0 else pl.ds(start + low, extent - low)

        if half == 0:
            if self.by_row:
                return self.ref.at[index, cut(0, 512), pl.ds(first, size)]
            return self.ref.at[index, cut(first, size), pl.ds(0, 512)]
        if not self.by_row:
            at = pl.ds(pl.multiple_of(index * 128, 128), 128)
            return self.ref.at[pl.ds(0, 4), cut(first, size), at]
        start, extent = index * 128, 128
        if part is not None:
            start, extent = index * 128 + part * 48, 48 + 32 * part
        return self.ref.at[pl.ds(0, 4), pl.ds(pl.multiple_of(start, 16), extent), pl.ds(first, size)]

    def _near(self, half, off, part):
        at = self.at
        if half == 0:
            return self.sub(0, at.z, (at.x + off) % 4, part)
        return self.sub(1, (at.z + off) % 4, at.x, part)

    def _far(self, half, off, part):
        at = self.at
        return self.block(half, ((at.z if half == 0 else at.x) + off) % 4, part)

    def _peers(self, half, first):
        at = self.at
        return (at.xp, at.xm) if (half == 0) == first else (at.zp, at.zm)

    def _push(self, ref, peer, half, k, way):
        return self.net.push(ref, ref, peer, self.ids[half * 8 + (k - 1) * 2 + way])

    def _round(self, k, halves, ways):
        for half in halves:
            st = self.state[half]
            near = self._near if k <= 2 else self._far
            up, down = self._peers(half, k <= 2)
            if k > 1 and st.get("at") != k:
                st[0].wait_recv()
                st[1].wait_recv()
            st["at"] = k
            if k in (1, 3):
                ref = near(half, 0, None)
                for way in ways:
                    st[way] = self._push(ref, (up, down)[way], half, k, way)
            elif k in (2, 4):
                st[0] = self._push(near(half, 3, 0), up, half, k, 0)
                st[1] = self._push(near(half, 1, 1), down, half, k, 1)

    def step(self, k, halves=(0, 1), ways=(0, 1)):
        first = len(self.net.copies)
        self._round(k, halves, ways)
        self.copies += self.net.copies[first:]

    def settle(self):
        self.net.settle(self.copies)


def rows_of(m):
    return pl.ds(pl.multiple_of(m * 256, 256), 256)


def cols_of(n):
    return pl.ds(pl.multiple_of(n * 512, 512), 512)


def heads_of(buf, s, m):
    return buf[s, pl.ds(m * 2, 2), :, :, :D].reshape(256, D)


def rows_gather(net, at, buf, s, ids):
    return Gather(net, at, lambda y, c: buf.at[s, y, c, :, pl.ds(0, D)], TOK, ids)


def rms(v, gain):
    return v * lax.rsqrt(jnp.mean(v * v, axis=-1, keepdims=True) + EPS) * gain


def rms_back(v, gain, grad):
    scale = lax.rsqrt(jnp.mean(v * v, axis=-1, keepdims=True) + EPS)
    scaled = gain * grad
    return scaled * scale - v * (
        jnp.mean(v * scaled, axis=-1, keepdims=True) * scale * scale * scale
    )


def put_part(part, s, m, z, value):
    part[s, pl.ds(m * 2, 2), :, :, cols_of(z)] = value.astype(BF).reshape(2, 2, TOK, 512)


def put_ext(part, s, pieces):
    part[s, :, :, :, D:] = jnp.zeros((4, 2, TOK, EXT), BF)
    for i, piece in enumerate(pieces):
        part[s, :, :, :, D + i * RANK : D + (i + 1) * RANK] = piece.astype(BF).reshape(
            4, 2, TOK, RANK
        )


def put_rows(buf, s, at, value):
    buf[s, at.y, at.c, :, :D] = value


def grid_loop(m_count, n_count, body):
    def step(i, carry):
        body(i // n_count, i % n_count)
        return carry

    lax.fori_loop(0, m_count * n_count, step, 0)


def layer(
    index_ref, length_ref,
    tok, cot, again, fgain, inv,
    wq, wo, wg, wu, wd,
    qin, gin, uin, aout, dout, ain, din, qout, gout, uout,
    result_o, igrad_o, sums1_o, sums2_o,
    w_q, w_o, w_g, w_u, w_d,
    nb, cb, part1, sib1, sib2, ra1, rb1, fp1, fm1, ra2, rb2, fp2, fm2,
    gate, up, hidden, qb, kvb, attn, lse, cosb, sinb, startb,
    midf, normed, midn, inner_a, mgrad, next_s, mid_s, cot_s, dkv, halo_in,
    a_b, d_b, q_b, g_b, u_b,
    full1, full1_in, vec1, vec1_in, full2, full2_in, vec2, vec2_in, px, px_in,
    send, recv, local,
):
    at = Place()
    net = Net(send, recv)
    pick = [index_ref[0], index_ref[1]]
    h, b = at.h, at.b
    both = (0, 1)

    here = pl.ds(pl.multiple_of(at.x * 128, 128), 128)
    loads = []

    def load(src, dst):
        copy = pltpu.make_async_copy(src, dst, local.at[len(loads)])
        copy.start()
        loads.append(copy)

    load(wq, w_q.at[at.z, here, :])
    load(wo, w_o.at[at.z, :, here])
    load(wg, w_g.at[at.z, here, :])
    load(wu, w_u.at[at.z, here, :])
    load(wd, w_d.at[at.z, :, here])
    load(qout.at[:, :, pl.ds(pl.multiple_of(h * 512, 512), 512)], q_b)
    load(ain.at[:, :, pl.ds(pl.multiple_of(h * 256, 256), 256)], a_b)
    load(din.at[:, :, pl.ds(pl.multiple_of(h * 1024, 1024), 1024)], d_b)
    load(gout.at[:, :, pl.ds(pl.multiple_of(h * 1024, 1024), 1024)], g_b)
    load(uout.at[:, :, pl.ds(pl.multiple_of(h * 1024, 1024), 1024)], u_b)
    at.greet(
        [((h + k) % 8, b) for k in range(1, 8)] + [(h, (b + k) % 16) for k in range(1, 16)]
    )

    q_ids = net.ids(16)
    W_Q = Weight(net, at, w_q, True, q_ids)
    W_O = Weight(net, at, w_o, False, net.ids(16))
    W_G = Weight(net, at, w_g, True, net.ids(16))
    W_U = Weight(net, at, w_u, True, net.ids(16))
    W_D = Weight(net, at, w_d, False, net.ids(16))
    n_ids = [net.ids(9), net.ids(9)]
    c_ids = [net.ids(9), net.ids(9)]
    s_ids = [net.ids(6), net.ids(6)]
    t_ids = [net.ids(6), net.ids(6)]
    near_ids = net.ids(3)
    across_ids = net.ids(2)
    first_m = at.yo // 2
    halves = (first_m, 1 - first_m)
    halo_ids = net.ids(8)
    px_ids = net.ids(2)
    out1, out2 = w_g.at[:, :, pl.ds(0, 512)], w_u.at[:, :, pl.ds(0, 128)]
    fold1 = Fold(net, at, full1, full1_in, vec1, vec1_in, out1, near_ids)
    fold2 = Fold(net, at, full2, full2_in, vec2, vec2_in, out2, near_ids)
    set1, set2 = (sib1, ra1, rb1, fp1, fm1), (sib2, ra2, rb2, fp2, fm2)

    def norm_in(s):
        n = rms(tok[s].astype(F32), again[...]).astype(BF)
        normed[s] = n
        put_rows(nb, s, at, n)

    sign = jnp.where(lax.broadcasted_iota(jnp.int32, (1, 128), 1) < 64, -1.0, 1.0)

    def table(s, m):
        rows = pl.ds(pl.multiple_of(m * 64, 64), 64)
        pos = b * SPAN + m * 64 + lax.broadcasted_iota(jnp.int32, (64, 1), 0)
        start = jnp.zeros((64, 1), jnp.int32)
        end = 0
        for d in range(4):
            length = length_ref[s, d]
            end = end + length
            start = start + jnp.where(pos >= end, length, 0)
        startb[s, rows] = start
        angle = (pos - start).astype(F32) * inv[...]
        cosb[s, rows] = jnp.cos(angle)
        sinb[s, rows] = jnp.sin(angle) * sign

    def cot_in(s):
        put_rows(cb, s, at, cot[s])

    def qkv(s):
        def step(m, unused):
            x = heads_of(nb, s, m)
            rows = rows_of(m)
            inner = mm_nt(x, qin[pick[s]]).astype(BF)
            next_s[s, rows] = inner
            r = mm(x, w_q[...].reshape(D, 512)) + mm(inner, q_b[pick[s]])
            c, sn = cosb[s, rows], sinb[s, rows]

            def rot(v):
                return v * c + pltpu.roll(v, 64, 1) * sn

            for j in both:
                qb[s, j, rows] = (rot(r[:, j * 128 : (j + 1) * 128]) * SCALE).astype(BF)
            own = pl.ds(pl.multiple_of(1024 + m * 256, 256), 256)
            kvb[s, 0, own] = rot(r[:, 256:384]).astype(BF)
            kvb[s, 1, own] = r[:, 384:512].astype(BF)

        grid_loop(2, 1, step)

    def halo(s):
        own = kvb.at[s, :, pl.ds(1024, 512)]
        return [
            net.push(own, kvb.at[s, :, pl.ds(512, 512)], at.next1, halo_ids[2 * s]),
            net.push(own, kvb.at[s, :, pl.ds(0, 512)], at.next2, halo_ids[2 * s + 1]),
        ]

    row = lax.broadcasted_iota(jnp.int32, (256, 1280), 0)
    col = lax.broadcasted_iota(jnp.int32, (256, 1280), 1)

    def allowed(s, m):
        low = startb[s, rows_of(m)] - (b * SPAN - WINDOW + m * 256)
        gap = row - col + WINDOW
        return (gap >= 0) & (gap < WINDOW) & (col >= low)

    def keys_of(m):
        return pl.ds(pl.multiple_of(m * 256, 256), 1280)

    def attend(s, g):
        def step(m, unused):
            rows, keys = rows_of(m), keys_of(m)
            sc = mm_nt(qb[s, g, rows], kvb[s, 0, keys])
            sc = jnp.where(allowed(s, m), sc, -1e30)
            top = jnp.max(sc, axis=-1, keepdims=True)
            e = jnp.exp(sc - top)
            total = jnp.sum(e, axis=-1, keepdims=True)
            p = (e * (1.0 / total)).astype(BF)
            o = mm(p, kvb[s, 1, keys])
            attn[s, rows, g * 128 : (g + 1) * 128] = o.astype(BF)
            lse[s, g, rows] = top + jnp.log(total)

        grid_loop(2, 1, step)

    def out_proj(s):
        put_ext(part1, s, [mm_nt(attn[s], a_b[pick[s]])])
        scatter = Scatter(net, at, part1, s, set1, s_ids[s], CW)
        for m in halves:
            grid_loop(
                1, 4, lambda unused, z: put_part(part1, s, m, z, mm(attn[s, rows_of(m)], w_o[z]))
            )
            scatter.send(m)
        return scatter

    def middle(s, t):
        inn = t[:, D : D + RANK]
        inner_a[s] = inn
        mid = tok[s].astype(F32) + t[:, :D] + mm(inn.astype(BF), aout[pick[s]])
        midf[s] = mid
        n = rms(mid, fgain[...]).astype(BF)
        midn[s] = n
        put_rows(nb, s, at, n)
        return rows_gather(net, at, nb, s, n_ids[s])

    def ffn(s):
        def inner(m, unused):
            x = heads_of(nb, s, m)
            mid_s[s, rows_of(m), :RANK] = mm_nt(x, gin[pick[s]]).astype(BF)
            mid_s[s, rows_of(m), RANK:] = mm_nt(x, uin[pick[s]]).astype(BF)

        grid_loop(2, 1, inner)

        def step(m, n):
            x = heads_of(nb, s, m)
            rows, cols = rows_of(m), cols_of(n)
            g = mm(x, w_g[:, :, cols].reshape(D, 512))
            g = g + mm(mid_s[s, rows, :RANK], g_b[pick[s], :, cols])
            u = mm(x, w_u[:, :, cols].reshape(D, 512))
            u = u + mm(mid_s[s, rows, RANK:], u_b[pick[s], :, cols])
            gate[s, rows, cols] = g.astype(BF)
            up[s, rows, cols] = u.astype(BF)
            hidden[s, rows, cols] = (g * jax.nn.sigmoid(g) * u).astype(BF)

        grid_loop(2, 2, step)

    def hid_back(s, m):
        def step(unused, n):
            x = heads_of(cb, s, m)
            rows, cols = rows_of(m), cols_of(n)
            hb = mm(cot_s[s, rows], d_b[pick[s], :, cols])
            for z in range(4):
                hb = hb + mm_nt(x[:, z * 512 : (z + 1) * 512], w_d[z, cols, :])
            g = gate[s, rows, cols].astype(F32)
            u = up[s, rows, cols].astype(F32)
            sg = jax.nn.sigmoid(g)
            gate[s, rows, cols] = (hb * u * sg * (1.0 + g * (1.0 - sg))).astype(BF)
            up[s, rows, cols] = (hb * g * sg).astype(BF)

        grid_loop(1, 2, step)

    def cot_inner(s):
        def step(m, unused):
            cot_s[s, rows_of(m)] = mm_nt(heads_of(cb, s, m), dout[pick[s]]).astype(BF)

        grid_loop(2, 1, step)

    def mid_scatter(s):
        put_ext(part1, s, [mm_nt(gate[s], g_b[pick[s]]), mm_nt(up[s], u_b[pick[s]])])
        return Scatter(net, at, part1, s, set1, s_ids[s], CW)

    def mid_back(s, m, scatter):
        def step(unused, z):
            rows = rows_of(m)
            put_part(part1, s, m, z, mm_nt(gate[s, rows], w_g[z]) + mm_nt(up[s, rows], w_u[z]))

        grid_loop(1, 4, step)
        scatter.send(m)

    def down(s, m):
        grid_loop(
            1, 4, lambda unused, z: put_part(nb, s, m, z, mm(hidden[s, rows_of(m)], w_d[z]))
        )

    def down_scatter(s):
        put_ext(nb, s, [mm_nt(hidden[s], d_b[pick[s]])])
        scatter = Scatter(net, at, nb, s, set2, t_ids[s], CW)
        for m in halves:
            scatter.send(m)
        return scatter

    def wide_terms(s):
        terms = [
            mm_tn(mid_s[s, :, :RANK], gate[s]),
            mm_tn(mid_s[s, :, RANK:], up[s]),
            mm_tn(cot_s[s], hidden[s]),
        ]
        for i, term in enumerate(terms):
            for j in range(4):
                vec1[3 + 4 * i + j, :, s * 256 : (s + 1) * 256] = term[
                    :, j * 256 : (j + 1) * 256
                ].astype(BF)

    def slices(full, i, s, term):
        for j in range(8):
            full[j, i, :, s * 256 : (s + 1) * 256] = term[:, j * 256 : (j + 1) * 256].astype(BF)

    def middle_back(s, t):
        pg, pu = t[:, D : D + RANK].astype(BF), t[:, D + RANK : D + 2 * RANK].astype(BF)
        back = t[:, :D] + mm(pg, gin[pick[s]]) + mm(pu, uin[pick[s]])
        mg = cot[s].astype(F32) + rms_back(midf[s], fgain[...], back)
        mgrad[s] = mg
        bg = mg.astype(BF)
        put_rows(cb, s, at, bg)
        gather = rows_gather(net, at, cb, s, n_ids[s])
        slices(full1, 0, s, mm_tn(pg, midn[s]))
        slices(full1, 1, s, mm_tn(pu, midn[s]))
        slices(full1, 2, s, mm_tn(inner_a[s].astype(BF), bg))
        return gather

    def attn_back(s):
        def step(m, unused):
            x = heads_of(cb, s, m)
            inner = mm_nt(x, aout[pick[s]]).astype(BF)
            cot_s[s, rows_of(m)] = inner
            r = mm(inner, a_b[pick[s]])
            for z in range(4):
                r = r + mm_nt(x[:, z * 512 : (z + 1) * 512], w_o[z])
            hidden[s, rows_of(m), 512:768] = r.astype(BF)

        grid_loop(2, 1, step)
        vec1[15, :, s * 256 : (s + 1) * 256] = mm_tn(cot_s[s], attn[s]).astype(BF)

    def attend_back(s, g):
        if g == 0:
            dkv[...] = jnp.zeros(dkv.shape, F32)

        def step(m, unused):
            rows, keys = rows_of(m), keys_of(m)
            q, k = qb[s, g, rows], kvb[s, 0, keys]
            do = hidden[s, rows, 512 + g * 128 : 640 + g * 128]
            p = jnp.where(allowed(s, m), jnp.exp(mm_nt(q, k) - lse[s, g, rows]), 0.0)
            vg = mm_nt(do, kvb[s, 1, keys])
            delta = jnp.sum(p * vg, axis=-1, keepdims=True)
            sg = (p * (vg - delta)).astype(BF)
            dq = mm(sg, k) * SCALE
            hidden[s, rows, g * 128 : (g + 1) * 128] = (
                dq * cosb[s, rows] - pltpu.roll(dq, 64, 1) * sinb[s, rows]
            ).astype(BF)
            dkv[0, keys] += mm_tn(sg, q)
            dkv[1, keys] += mm_tn(p.astype(BF), do)

        grid_loop(2, 1, step)

    def halo_back(s):
        copies = []
        for hop in (2, 1, 0):
            for i in both:
                at_col = hop * 256 + i * 128
                gate[s, :, at_col : at_col + 128] = dkv[
                    i, (2 - hop) * SPAN : (3 - hop) * SPAN
                ].astype(BF)
            if hop > 0:
                copies.append(
                    net.push(
                        gate.at[s, :, pl.ds(hop * 256, 256)],
                        halo_in.at[s, hop - 1],
                        at.prev1 if hop == 1 else at.prev2,
                        halo_ids[4 + 2 * s + hop - 1],
                    )
                )
        return copies

    def key_back(s):
        def keys(m, unused):
            rows = rows_of(m)
            dk, dv = [
                gate[s, rows, i * 128 : (i + 1) * 128].astype(F32)
                + halo_in[s, 0, rows, i * 128 : (i + 1) * 128].astype(F32)
                + halo_in[s, 1, rows, i * 128 : (i + 1) * 128].astype(F32)
                for i in both
            ]
            hidden[s, rows, 256:384] = (
                dk * cosb[s, rows] - pltpu.roll(dk, 64, 1) * sinb[s, rows]
            ).astype(BF)
            hidden[s, rows, 384:512] = dv.astype(BF)

        grid_loop(2, 1, keys)

    def p_send(s):
        raw = hidden[s, :, :512]
        px[s] = jnp.zeros(px.shape[1:], BF)
        px[s, :, :, :RANK] = mm_nt(raw, q_b[pick[s]]).astype(BF).reshape(8, TOK, RANK)
        pairs = []
        for k in range(1, 8):
            peer = (h + k) % 8
            pairs.append((px.at[s, peer], px_in.at[s, k - 1], (peer, b)))
        return net.spread(pairs, px_in.at[s], px_ids[s])

    def qkv_back(s, m, scatter):
        grid_loop(
            1, 4,
            lambda unused, z: put_part(part1, s, m, z, mm_nt(hidden[s, rows_of(m), :512], w_q[z])),
        )
        scatter.send(m)

    def qkv_terms(s):
        term = mm_tn(next_s[s], hidden[s, :, :512])
        for j in range(4):
            vec2[s * 8 + 4 + j] = term[:, j * 128 : (j + 1) * 128].astype(BF)

    def finish_result(s, t):
        inn = t[:, D : D + RANK].astype(BF)
        midf[s] = midf[s] + t[:, :D] + mm(inn, dout[pick[s]])
        slices(full2, 1, s, mm_tn(inn, cot[s]))

    def p_sum(s, exchange):
        exchange.wait_recv()
        total = px[s, h].astype(F32)
        for k in range(7):
            total = total + px_in[s, k].astype(F32)
        p = total[:, :RANK].astype(BF)
        slices(full2, 0, s, mm_tn(p, normed[s]))
        return p

    def finish_grad(s, t, p):
        back = t + mm(p, qin[pick[s]])
        mgrad[s] = mgrad[s] + rms_back(tok[s].astype(F32), again[...], back)

    loads[0].wait()
    loads[1].wait()
    W_Q.step(1)
    norm_in(0)
    n0 = rows_gather(net, at, nb, 0, n_ids[0])
    for copy in loads[2:5]:
        copy.wait()
    W_Q.step(2)
    norm_in(1)
    grid_loop(2, 8, table)
    W_Q.step(3)
    W_O.step(1)
    n0.relay()
    n1 = rows_gather(net, at, nb, 1, n_ids[1])
    W_G.step(1)
    W_O.step(2)
    cot_in(0)
    cot_in(1)
    n0.last()
    n1.relay()
    c0 = rows_gather(net, at, cb, 0, c_ids[0])
    W_Q.step(4)
    W_O.step(3)
    W_G.step(2)
    W_U.step(1)
    for copy in loads[5:]:
        copy.wait()
    n0.done()
    W_Q.step(5)
    qkv(0)
    halo0 = halo(0)
    W_O.step(4)
    W_U.step(2)
    W_D.step(1)
    n1.last()
    c0.relay()
    c1 = rows_gather(net, at, cb, 1, c_ids[1])
    n1.done()
    qkv(1)
    halo1 = halo(1)
    W_D.step(2)
    n0.settle()
    n1.settle()
    c0.last()
    W_O.step(5)
    for copy in halo0:
        copy.wait_recv()
    W_G.step(3)
    attend(0, 0)
    c1.relay()
    attend(0, 1)
    s0 = out_proj(0)
    c1.last()
    s0.merge()
    for copy in halo1:
        copy.wait_recv()
    W_U.step(3)
    attend(1, 0)
    s0.relay()
    W_D.step(3)
    attend(1, 1)
    s1 = out_proj(1)
    W_G.step(4)
    s1.merge()
    m0 = middle(0, s0.done())
    s1.relay()
    W_U.step(4)
    c0.done()
    c1.done()
    cot_inner(0)
    m0.relay()
    cot_inner(1)
    W_D.step(4)
    m1 = middle(1, s1.done())
    m0.last()
    m0.done()
    m1.relay()
    W_G.step(5)
    W_U.step(5)
    ffn(0)
    W_D.step(5)
    hid_back(0, 0)
    m1.last()
    hid_back(0, 1)
    for item in (c0, c1, m0, m1, W_Q, W_G, W_U):
        item.settle()
    s0 = mid_scatter(0)
    for m in halves:
        mid_back(0, m, s0)
    m1.done()
    s0.merge()
    ffn(1)
    s0.relay()
    hid_back(1, 0)
    hid_back(1, 1)
    s1 = mid_scatter(1)
    mid_back(1, halves[0], s1)
    b0 = middle_back(0, s0.done())
    mid_back(1, halves[1], s1)
    down(0, 0)
    s1.merge()
    down(0, 1)
    r0 = down_scatter(0)
    b0.relay()
    down(1, 0)
    wide_terms(0)
    down(1, 1)
    s1.relay()
    b0.last()
    b0.done()
    attn_back(0)
    b1 = middle_back(1, s1.done())
    fold1.heads()
    attend_back(0, 0)
    attend_back(0, 1)
    back0 = halo_back(0)
    r1 = down_scatter(1)
    wide_terms(1)
    b1.relay()
    r0.merge()
    b1.last()
    vec1[0:3] = fold1.heads_sum().astype(BF)
    b1.done()
    attn_back(1)
    fold1.blocks()
    attend_back(1, 0)
    r0.relay()
    r1.merge()
    attend_back(1, 1)
    back1 = halo_back(1)
    fold1.blocks_sum()
    b0.settle()
    b1.settle()
    r1.relay()
    for copy in back0:
        copy.wait_recv()
    key_back(0)
    x0 = p_send(0)
    s0 = Scatter(net, at, part1, 0, set1, s_ids[0], D)
    for m in halves:
        qkv_back(0, m, s0)
    s0.merge()
    fold1.near_done()
    fold1.far((n_ids[0] + n_ids[1])[:15])
    qkv_terms(0)
    finish_result(0, r0.done())
    finish_result(1, r1.done())
    p0 = p_sum(0, x0)
    for copy in back1:
        copy.wait_recv()
    key_back(1)
    x1 = p_send(1)
    s0.relay()
    s1 = Scatter(net, at, part1, 1, set1, s_ids[1], D)
    qkv_back(1, halves[0], s1)
    p1 = p_sum(1, x1)
    fold2.heads()
    qkv_back(1, halves[1], s1)
    qkv_terms(1)
    s1.merge()
    total = fold2.heads_sum()
    for i in both:
        for s in both:
            for j in both:
                vec2[s * 8 + 2 * i + j] = total[
                    i, :, s * 256 + j * 128 : s * 256 + (j + 1) * 128
                ].astype(BF)
    fold2.blocks()
    s1.relay()
    finish_grad(0, s0.done(), p0)
    fold1.across(across_ids[0])
    fold2.blocks_sum()
    fold2.near_done()
    fold2.far((c_ids[0] + c_ids[1])[:15])
    finish_grad(1, s1.done(), p1)
    fold2.across(across_ids[1])
    writes = [
        pltpu.make_async_copy(midf, result_o, local.at[0]),
        pltpu.make_async_copy(mgrad, igrad_o, local.at[1]),
        pltpu.make_async_copy(out1, sums1_o, local.at[2]),
        pltpu.make_async_copy(out2, sums2_o, local.at[3]),
    ]
    writes[0].start()
    writes[1].start()
    fold1.done()
    writes[2].start()
    fold2.done()
    writes[3].start()
    net.drain()
    assert net.count == N_SEMS
    for copy in writes:
        copy.wait()


def call_layer(args):
    vm = lambda *shape, t=BF: pltpu.VMEM(shape, t)
    rs = lambda: [vm(2, TOK // 2, CW), vm(2, TOK // 2, CW), vm(2, TOK, CW), vm(2, TOK, CW)]
    outs = [((2, TOK, D), F32), ((2, TOK, D), F32), ((4, 512, 512), BF), ((4, 512, 128), BF)]
    scratch = (
        [vm(4, 512, 512), vm(4, 256, 512), vm(4, 512, 1024), vm(4, 512, 1024), vm(4, 1024, 512)]
        + [vm(2, 4, 2, TOK, CW)] * 3
        + [vm(2, 4, TOK, D + EXT), vm(2, 4, TOK, D + EXT)]
        + rs() + rs()
        + [vm(2, SPAN, 1024)] * 3
        + [vm(2, 2, SPAN, 128), vm(2, 2, 1536, 128), vm(2, SPAN, 256), vm(2, 2, SPAN, 1, t=F32)]
        + [vm(2, SPAN, 128, t=F32)] * 2
        + [vm(2, SPAN, 1, t=jnp.int32)]
        + [vm(2, TOK, D, t=F32), vm(2, TOK, D), vm(2, TOK, D), vm(2, TOK, RANK, t=F32)]
        + [vm(2, TOK, D, t=F32)] + [vm(2, SPAN, RANK), vm(2, SPAN, 2 * RANK), vm(2, SPAN, RANK)]
        + [vm(2, 1536, 128, t=F32), vm(2, 2, SPAN, 256)]
        + [vm(2, RANK, 256), vm(2, RANK, 1024), vm(2, RANK, 512), vm(2, RANK, 1024), vm(2, RANK, 1024)]
        + [vm(8, 3, RANK, 512), vm(7, 3, RANK, 512), vm(16, RANK, 512), vm(15, RANK, 512)]
        + [vm(8, 2, RANK, 512), vm(7, 2, RANK, 512), vm(16, RANK, 128), vm(15, RANK, 128)]
        + [vm(2, 8, TOK, EXT), vm(2, 7, TOK, EXT)]
        + [pltpu.SemaphoreType.DMA((N_SEMS,)), pltpu.SemaphoreType.DMA((N_SEMS,)), pltpu.SemaphoreType.DMA((10,))]
    )
    smem = pl.BlockSpec(memory_space=pltpu.SMEM)
    vmem = pl.BlockSpec(memory_space=pltpu.VMEM)
    hbm = pl.BlockSpec(memory_space=pl.ANY)
    return pl.pallas_call(
        layer,
        out_shape=[jax.ShapeDtypeStruct(shape, kind) for shape, kind in outs],
        in_specs=[smem] * 2 + [vmem] * 5 + [hbm] * 5 + [vmem] * 5 + [hbm] * 5,
        out_specs=[hbm] * len(outs),
        scratch_shapes=scratch,
        compiler_params=pltpu.CompilerParams(
            collective_id=0, has_side_effects=True, vmem_limit_bytes=VMEM_BYTES
        ),
    )(*args)


def unpack(
    index_ref, result, igrad, sums1, sums2,
    result_o, igrad_o, qi_o, qo_o, ai_o, ao_o, gi_o, go_o, ui_o, uo_o, di_o, do_o, sem,
):
    copies = [
        pltpu.make_async_copy(result, result_o, sem.at[0]),
        pltpu.make_async_copy(igrad, igrad_o, sem.at[1]),
    ]
    for copy in copies:
        copy.start()
    swap = index_ref[0] == 1

    def emit(out, cols, first, second):
        first, second = first.astype(F32), second.astype(F32)
        out[0, :, cols] = jnp.where(swap, second, first)
        out[1, :, cols] = jnp.where(swap, first, second)

    def found(ref, j, head, width):
        row0 = (head % 2) * 256 + (j % 4) * 64 + (head // 2) * RANK
        return ref[j // 4, row0 : row0 + RANK, :width]

    for head in range(8):
        for j, out in ((0, gi_o), (1, ui_o), (2, ao_o), (15, ai_o)):
            block = found(sums1, j, head, 512)
            emit(out, pl.ds(head * 256, 256), block[:, :256], block[:, 256:])
        for i, out in enumerate([go_o, uo_o, di_o]):
            for k in range(4):
                block = found(sums1, 3 + 4 * i + k, head, 512)
                emit(out, pl.ds(head * 1024 + k * 256, 256), block[:, :256], block[:, 256:])
        for j, out, width in (
            (0, qi_o, 256), (1, qi_o, 256), (2, do_o, 256), (3, do_o, 256),
            (4, qo_o, 512), (5, qo_o, 512), (6, qo_o, 512), (7, qo_o, 512),
        ):
            cols = pl.ds(head * width + (j % (width // 128)) * 128, 128)
            emit(out, cols, found(sums2, j, head, 128), found(sums2, 8 + j, head, 128))
    for copy in copies:
        copy.wait()


def call_unpack(index, arrays):
    narrow, wide = (2, RANK, D), (2, RANK, 8192)
    outs = [
        (2, TOK, D), (2, TOK, D), narrow, (2, RANK, 4096), narrow, narrow,
        narrow, wide, narrow, wide, wide, narrow,
    ]
    smem = pl.BlockSpec(memory_space=pltpu.SMEM)
    vmem = pl.BlockSpec(memory_space=pltpu.VMEM)
    hbm = pl.BlockSpec(memory_space=pl.ANY)
    return pl.pallas_call(
        unpack,
        out_shape=[jax.ShapeDtypeStruct(shape, F32) for shape in outs],
        in_specs=[smem] + [vmem] * 4,
        out_specs=[hbm, hbm] + [vmem] * 10,
        scratch_shapes=[pltpu.SemaphoreType.DMA((2,))],
        compiler_params=pltpu.CompilerParams(vmem_limit_bytes=VMEM_BYTES),
    )(index, *arrays)


def body(
    tokens, cotangent, doc_lengths, adapter_index, attn_gain, ffn_gain,
    w_qkv, w_out, w_gate, w_up, w_down,
    qkv_in, qkv_out, attn_in, attn_out, gate_in, gate_out, up_in, up_out, down_in, down_out,
):
    flip = lambda g: jnp.swapaxes(g, 1, 2)
    half = np.arange(64, dtype=np.float32) * np.float32(2.0 / 128)
    inverse = np.power(np.float32(THETA), -half).astype(np.float32)
    inv = jnp.asarray(np.concatenate([inverse, inverse])[None])
    index = adapter_index.reshape(2)
    arrays = call_layer((
        index, doc_lengths, tokens, cotangent, attn_gain[None], ffn_gain[None], inv,
        w_qkv, w_out, w_gate, w_up, w_down,
        flip(qkv_in), flip(gate_in), flip(up_in), attn_out, down_out, flip(attn_in), flip(down_in),
        qkv_out, gate_out, up_out,
    ))
    result, igrad, qi, qo, ai, ao, gi, go, ui, uo, di, do = call_unpack(index, arrays)
    return (
        result, igrad, flip(qi), qo, flip(ai), ao, flip(gi), go, flip(ui), uo, flip(di), do
    )


def solution(mesh):
    row = P(None, ("blk", "head"), None)
    return jax.shard_map(
        body,
        mesh=mesh,
        in_specs=(row, row) + (P(),) * 4
        + (P("blk", "head"), P("head", "blk"), P("blk", "head"), P("blk", "head"), P("head", "blk"))
        + (P(),) * 10,
        out_specs=(row, row) + (P(),) * 10,
        check_vma=False,
    )
```

```python
from functools import partial

import jax
import jax.numpy as jnp
import numpy as np
from jax import lax
from jax.experimental import pallas as pl
from jax.experimental.pallas import tpu as pltpu
from jax.sharding import PartitionSpec as P

MESH = pl.DeviceIdType.MESH
BF = jnp.bfloat16
F32 = jnp.float32
D = 2048
EXT = 128
CW = D + EXT
RANK = 16
WINDOW = 1024
EPS = 1e-05
THETA = 1000000.0
Y, CORES, Z, X = 4, 2, 4, 4
TOK = 64
SPAN = 512
SCALE = 128 ** (-0.5)
VMEM_BYTES = 66977792
N_SEMS = 159


def mm(a, b):
    return jnp.dot(a, b, preferred_element_type=F32)


def mm_nt(a, b):
    return lax.dot_general(a, b, (((1,), (1,)), ((), ())), preferred_element_type=F32)


def mm_tn(a, b):
    return lax.dot_general(a, b, (((0,), (0,)), ((), ())), preferred_element_type=F32)


class Place:
    def __init__(self):
        h = lax.axis_index("head")
        b = lax.axis_index("blk")
        self.h, self.b = h, b
        self.y, self.c = h // 2, h % 2
        self.z, self.x = b // 4, b % 4
        y, c, z, x = self.y, self.c, self.z, self.x
        self.yu, self.yd, self.yo = (y + 1) % 4, (y + 3) % 4, (y + 2) % 4
        self.xu, self.xd = (x + 1) % 4, (x + 3) % 4
        self.zu, self.zd = (z + 1) % 4, (z + 3) % 4
        self.sib = (y * 2 + (1 - c), b)
        self.yp, self.ym = (self.yu * 2 + c, b), (self.yd * 2 + c, b)
        self.xp, self.xm = (h, z * 4 + self.xu), (h, z * 4 + self.xd)
        self.zp, self.zm = (h, self.zu * 4 + x), (h, self.zd * 4 + x)
        self.next1, self.next2 = (h, (b + 1) % 16), (h, (b + 2) % 16)
        self.prev1, self.prev2 = (h, (b + 15) % 16), (h, (b + 14) % 16)

    def greet(self, peers):
        barrier = pltpu.get_barrier_semaphore()
        for peer in peers:
            pl.semaphore_signal(barrier, inc=1, device_id=peer, device_id_type=MESH)
        pl.semaphore_wait(barrier, len(peers))


class Net:
    def __init__(self, send, recv):
        self.send, self.recv, self.count, self.copies = send, recv, 0, []

    def ids(self, n):
        first = self.count
        self.count += n
        return list(range(first, first + n))

    def make(self, src, dst, peer, i):
        out = i // 16 if i < 80 else i - 75
        return pltpu.make_async_remote_copy(
            src_ref=src,
            dst_ref=dst,
            send_sem=self.send.at[out],
            recv_sem=self.recv.at[i],
            device_id=peer,
            device_id_type=MESH,
        )

    def push(self, src, dst, peer, i):
        copy = self.make(src, dst, peer, i)
        copy.start()
        self.copies.append(copy)
        return copy

    def spread(self, pairs, whole, i):
        for src, dst, peer in pairs:
            self.make(src, dst, peer, i).start()
        copy = self.make(whole, whole, pairs[0][2], i)
        self.copies.append(copy)
        return copy

    def settle(self, copies):
        for copy in copies:
            copy.wait_send()
            self.copies = [other for other in self.copies if other is not copy]

    def drain(self):
        self.settle(list(self.copies))


class Gather:
    def __init__(self, net, at, slot, extent, ids):
        self.net, self.at, self.slot, self.half, self.ids = net, at, slot, extent // 2, ids
        own = slot(at.y, at.c)
        self.up = net.push(own, own, at.yp, ids[0])
        self.down = net.push(own, own, at.ym, ids[1])
        self.side = [net.push(own, own, at.sib, ids[2])]

    def relay(self):
        at, net, half, ids = self.at, self.net, self.half, self.ids
        below = self.slot(at.yd, at.c)
        above = self.slot(at.yu, at.c)
        self.up.wait_recv()
        part = below.at[pl.ds(0, half)]
        self.far_a = net.push(part, part, at.yp, ids[3])
        self.side.append(net.push(below, below, at.sib, ids[4]))
        self.down.wait_recv()
        part = above.at[pl.ds(half, half)]
        self.far_b = net.push(part, part, at.ym, ids[5])
        self.side.append(net.push(above, above, at.sib, ids[6]))

    def last(self):
        at, net, half, ids = self.at, self.net, self.half, self.ids
        far = self.slot(at.yo, at.c)
        self.far_a.wait_recv()
        part = far.at[pl.ds(0, half)]
        self.side.append(net.push(part, part, at.sib, ids[7]))
        self.far_b.wait_recv()
        part = far.at[pl.ds(half, half)]
        self.side.append(net.push(part, part, at.sib, ids[8]))

    def done(self):
        for copy in self.side:
            copy.wait_recv()

    def settle(self):
        self.net.settle([self.up, self.down, self.far_a, self.far_b] + self.side)


class Fold:
    def __init__(self, net, at, full, full_in, vec, vec_in, out, near):
        self.net, self.at = net, at
        self.full, self.full_in, self.vec, self.vec_in, self.out = full, full_in, vec, vec_in, out
        self.ids, self.near = net.ids(2), near

    def heads(self):
        at = self.at
        pairs = []
        for k in range(1, 8):
            peer = (at.h + k) % 8
            pairs.append((self.full.at[peer], self.full_in.at[k - 1], (peer, at.b)))
        self.copy = self.net.spread(pairs, self.full_in, self.ids[0])

    def heads_sum(self):
        self.copy.wait_recv()
        total = self.full[self.at.h].astype(F32)
        for k in range(7):
            total = total + self.full_in[k].astype(F32)
        return total

    def blocks(self):
        at = self.at
        pairs = []
        for k in range(1, 16):
            peer = (at.b + k) % 16
            pairs.append((self.vec.at[peer], self.vec_in.at[k - 1], (at.h, peer)))
        self.copy = self.net.spread(pairs, self.vec_in, self.ids[1])

    def blocks_sum(self):
        at = self.at
        self.copy.wait_recv()
        total = self.vec[at.b].astype(F32)
        for k in range(15):
            total = total + self.vec_in[k].astype(F32)
        row = at.c * 256 + at.x * 64 + at.y * 16
        own = self.out.at[at.z, pl.ds(pl.multiple_of(row, 16), 16)]
        own[...] = total.astype(BF)
        self.copies = [
            self.net.push(own, own, (((at.y + k) % 4) * 2 + at.c, at.b), self.near[k - 1])
            for k in range(1, 4)
        ]

    def near_done(self):
        for copy in self.copies:
            copy.wait_recv()
        self.net.settle(self.copies)

    def far(self, ids):
        at = self.at
        own = self.out.at[at.z, pl.ds(pl.multiple_of(at.c * 256 + at.x * 64, 64), 64)]
        self.copies = [
            self.net.push(own, own, (at.h, (at.b + k) % 16), ids[k - 1]) for k in range(1, 16)
        ]

    def far_done(self):
        for copy in self.copies:
            copy.wait_recv()

    def across(self, i):
        at = self.at
        own = self.out.at[:, pl.ds(pl.multiple_of(at.c * 256, 256), 256)]
        self.copies = [self.net.push(own, own, at.sib, i)]

    def done(self):
        self.copies[0].wait_recv()


class Scatter:
    def __init__(self, net, at, part, s, bufs, ids, width):
        self.net, self.at, self.ids, self.width = net, at, ids, width
        cols = pl.ds(0, width)
        self.part = part.at[s, :, :, :, cols]
        self.sibr, self.ra, self.rb, self.fp, self.fm = [
            buf.at[s, :, :, cols] if i == 0 else buf.at[s, :, cols] for i, buf in enumerate(bufs)
        ]
        self.side = []

    def send(self, m):
        ys = pl.ds(m * 2, 2)
        self.side.append(
            self.net.push(
                self.part.at[ys, 1 - self.at.c],
                self.sibr.at[ys],
                self.at.sib,
                self.ids[0 if not self.side else 5],
            )
        )

    def _merge(self, y):
        c = self.at.c
        self.part[y, c] = (self.part[y, c].astype(F32) + self.sibr[y].astype(F32)).astype(BF)

    def merge(self):
        at, net = self.at, self.net
        self.side[0].wait_recv()
        self._merge(at.yo)
        far = self.part.at[at.yo, at.c]
        self.a = net.push(far.at[pl.ds(0, TOK // 2)], self.ra, at.yp, self.ids[1])
        self.b = net.push(far.at[pl.ds(TOK // 2, TOK // 2)], self.rb, at.ym, self.ids[2])
        self.side[1].wait_recv()
        self._merge(at.yu)
        self._merge(at.yd)

    def relay(self):
        at, net = self.at, self.net
        self.a.wait_recv()
        half = pl.ds(0, TOK // 2)
        self.part[at.yu, at.c, half] = (
            self.part[at.yu, at.c, half].astype(F32) + self.ra[...].astype(F32)
        ).astype(BF)
        self.up = net.push(self.part.at[at.yu, at.c], self.fp, at.yp, self.ids[3])
        self.b.wait_recv()
        half = pl.ds(TOK // 2, TOK // 2)
        self.part[at.yd, at.c, half] = (
            self.part[at.yd, at.c, half].astype(F32) + self.rb[...].astype(F32)
        ).astype(BF)
        self.down = net.push(self.part.at[at.yd, at.c], self.fm, at.ym, self.ids[4])

    def done(self):
        at = self.at
        self.up.wait_recv()
        self.down.wait_recv()
        self.net.settle(self.side + [self.a, self.b, self.up, self.down])
        return (self.part[at.y, at.c].astype(F32) + self.sibr[at.y].astype(F32)) + (
            self.fp[...].astype(F32) + self.fm[...].astype(F32)
        )


class Weight:
    def __init__(self, net, at, ref, by_row, ids, base=0, unit=128):
        self.net, self.at, self.ref, self.by_row, self.ids = net, at, ref, by_row, ids
        self.rows, self.cols = ref.shape[1], ref.shape[2]
        self.state = [{}, {}]
        size = self.cols if by_row else self.rows
        self.spans = [(0, size // 2), (size // 2, size // 2)]
        self.base, self.unit = base, unit

    def sub(self, half, z, x, part):
        first, size = self.spans[half]
        if self.by_row:
            rows = self.unit if part is None else self.unit // 2
            start = self.base + x * self.unit + (part or 0) * rows
            return self.ref.at[z, pl.ds(pl.multiple_of(start, 16), rows), pl.ds(first, size)]
        at = pl.ds(pl.multiple_of(x * 128, 128), 128)
        if part is None:
            rows = pl.ds(first, size)
        else:
            rows = pl.ds(first + part * (size // 2), size // 2)
        return self.ref.at[z, rows, at]

    def block(self, half, index, part):
        first, size = self.spans[half]

        def cut(start, extent):
            if part is None:
                return pl.ds(start, extent)
            low = extent * 3 // 8
            return pl.ds(start, low) if part == 0 else pl.ds(start + low, extent - low)

        if half == 0:
            if self.by_row:
                return self.ref.at[index, cut(self.base, 4 * self.unit), pl.ds(first, size)]
            return self.ref.at[index, cut(first, size), pl.ds(0, 512)]
        if not self.by_row:
            at = pl.ds(pl.multiple_of(index * 128, 128), 128)
            return self.ref.at[pl.ds(0, 4), cut(first, size), at]
        low = 48 if self.unit == 128 else 32
        start, extent = self.base + index * self.unit, self.unit
        if part is not None:
            start, extent = start + part * low, (self.unit - low) if part else low
        return self.ref.at[pl.ds(0, 4), pl.ds(pl.multiple_of(start, 16), extent), pl.ds(first, size)]

    def _near(self, half, off, part):
        at = self.at
        if half == 0:
            return self.sub(0, at.z, (at.x + off) % 4, part)
        return self.sub(1, (at.z + off) % 4, at.x, part)

    def _far(self, half, off, part):
        at = self.at
        return self.block(half, ((at.z if half == 0 else at.x) + off) % 4, part)

    def _peers(self, half, first):
        at = self.at
        return (at.xp, at.xm) if (half == 0) == first else (at.zp, at.zm)

    def _push(self, ref, peer, half, k, way):
        copy = self.net.make(ref, ref, peer, self.ids[half * 8 + (k - 1) * 2 + way])
        copy.start()
        return copy

    def _round(self, k, halves, ways):
        for half in halves:
            st = self.state[half]
            near = self._near if k <= 2 else self._far
            up, down = self._peers(half, k <= 2)
            if k > 1 and st.get("at") != k:
                st[0].wait_recv()
                st[1].wait_recv()
            st["at"] = k
            if k in (1, 3):
                ref = near(half, 0, None)
                for way in ways:
                    st[way] = self._push(ref, (up, down)[way], half, k, way)
            elif k in (2, 4):
                st[0] = self._push(near(half, 3, 0), up, half, k, 0)
                st[1] = self._push(near(half, 1, 1), down, half, k, 1)

    def step(self, k, halves=(0, 1), ways=(0, 1)):
        self._round(k, halves, ways)

    def settle(self):
        sent = self.ref.at[:, pl.ds(0, (4 * self.unit if self.by_row else self.rows) * 15 // 16)]
        self.net.make(sent, sent, self.at.xp, self.ids[0]).wait_send()


def rows_of(m):
    return pl.ds(pl.multiple_of(m * 256, 256), 256)


def cols_of(n):
    return pl.ds(pl.multiple_of(n * 512, 512), 512)


def heads_of(buf, s, m):
    return buf[s, pl.ds(m * 2, 2), :, :, :D].reshape(256, D)


def rows_gather(net, at, buf, s, ids):
    return Gather(net, at, lambda y, c: buf.at[s, y, c, :, pl.ds(0, D)], TOK, ids)


def rms(v, gain):
    return v * lax.rsqrt(jnp.mean(v * v, axis=-1, keepdims=True) + EPS) * gain


def rms_back(v, gain, grad):
    scale = lax.rsqrt(jnp.mean(v * v, axis=-1, keepdims=True) + EPS)
    scaled = gain * grad
    return scaled * scale - v * (
        jnp.mean(v * scaled, axis=-1, keepdims=True) * scale * scale * scale
    )


def put_part(part, s, m, z, value):
    part[s, pl.ds(m * 2, 2), :, :, cols_of(z)] = value.astype(BF).reshape(2, 2, TOK, 512)


def put_ext(part, s, pieces):
    part[s, :, :, :, D:] = jnp.zeros((4, 2, TOK, EXT), BF)
    for i, piece in enumerate(pieces):
        part[s, :, :, :, D + i * RANK : D + (i + 1) * RANK] = piece.astype(BF).reshape(
            4, 2, TOK, RANK
        )


def put_rows(buf, s, at, value):
    buf[s, at.y, at.c, :, :D] = value


def grid_loop(m_count, n_count, body):
    def step(i, carry):
        body(i // n_count, i % n_count)
        return carry

    lax.fori_loop(0, m_count * n_count, step, 0)


def layer(
    index_ref, length_ref,
    tok, cot, again, fgain, inv,
    wq, wo, wg, wu, wd,
    qin, gin, uin, aout, dout, ain, din, qout, gout, uout,
    result_o, igrad_o, sums1_o, sums2_o,
    w_q, w_o, w_g, w_u, w_d,
    nb, cb, part1, sib1, sib2, ra1, rb1, fp1, fm1, ra2, rb2, fp2, fm2,
    gate, up, hidden, qb, kvb, attn, lse, cosb, sinb, startb,
    midf, normed, midn, inner_a, mgrad, next_s, mid_s, cot_s, dkv, halo_in,
    a_b, d_b, q_b, g_b, u_b,
    full1, full1_in, vec1, vec1_in, full2, full2_in, vec2, vec2_in, px, px_in,
    send, recv, local,
):
    at = Place()
    net = Net(send, recv)
    pick = [index_ref[0], index_ref[1]]
    h, b = at.h, at.b
    both = (0, 1)

    here = pl.ds(pl.multiple_of(at.x * 128, 128), 128)
    loads = []

    def load(src, dst):
        copy = pltpu.make_async_copy(src, dst, local.at[len(loads)])
        copy.start()
        loads.append(copy)

    load(wq, w_q.at[at.z, here, :])
    load(wo, w_o.at[at.z, :, here])
    load(wg, w_g.at[at.z, here, :])
    load(wu, w_u.at[at.z, here, :])
    load(wd, w_d.at[at.z, :, here])
    load(qout.at[:, :, pl.ds(pl.multiple_of(h * 512, 512), 512)], q_b)
    load(ain.at[:, :, pl.ds(pl.multiple_of(h * 256, 256), 256)], a_b)
    load(din.at[:, :, pl.ds(pl.multiple_of(h * 1024, 1024), 1024)], d_b)
    load(gout.at[:, :, pl.ds(pl.multiple_of(h * 1024, 1024), 1024)], g_b)
    load(uout.at[:, :, pl.ds(pl.multiple_of(h * 1024, 1024), 1024)], u_b)
    at.greet(
        [((h + k) % 8, b) for k in range(1, 8)] + [(h, (b + k) % 16) for k in range(1, 16)]
    )

    q_ids = net.ids(16)
    W_Q = Weight(net, at, w_q, True, q_ids)
    W_O = Weight(net, at, w_o, False, net.ids(16))
    W_G = Weight(net, at, w_g, True, net.ids(16))
    W_U = Weight(net, at, w_u, True, net.ids(16))
    W_D = Weight(net, at, w_d, False, net.ids(16))
    n_ids = [net.ids(9), net.ids(9)]
    c_ids = [net.ids(9), net.ids(9)]
    s_ids = [net.ids(6), net.ids(6)]
    t_ids = [net.ids(6), net.ids(6)]
    near_ids = net.ids(3)
    across_ids = net.ids(2)
    first_m = at.yo // 2
    halves = (first_m, 1 - first_m)
    halo_ids = net.ids(8)
    px_ids = net.ids(2)
    out1, out2 = w_g.at[:, :, pl.ds(0, 512)], w_u.at[:, :, pl.ds(0, 128)]
    fold1 = Fold(net, at, full1, full1_in, vec1, vec1_in, out1, near_ids)
    fold2 = Fold(net, at, full2, full2_in, vec2, vec2_in, out2, near_ids)
    set1, set2 = (sib1, ra1, rb1, fp1, fm1), (sib2, ra2, rb2, fp2, fm2)

    def norm_in(s):
        n = rms(tok[s].astype(F32), again[...]).astype(BF)
        normed[s] = n
        put_rows(nb, s, at, n)

    sign = jnp.where(lax.broadcasted_iota(jnp.int32, (1, 128), 1) < 64, -1.0, 1.0)

    def table(s, m):
        rows = pl.ds(pl.multiple_of(m * 64, 64), 64)
        pos = b * SPAN + m * 64 + lax.broadcasted_iota(jnp.int32, (64, 1), 0)
        start = jnp.zeros((64, 1), jnp.int32)
        end = 0
        for d in range(4):
            length = length_ref[s, d]
            end = end + length
            start = start + jnp.where(pos >= end, length, 0)
        startb[s, rows] = start
        angle = (pos - start).astype(F32) * inv[...]
        cosb[s, rows] = jnp.cos(angle)
        sinb[s, rows] = jnp.sin(angle) * sign

    def cot_in(s):
        put_rows(cb, s, at, cot[s])

    def qkv(s):
        def step(m, unused):
            x = heads_of(nb, s, m)
            rows = rows_of(m)
            inner = mm_nt(x, qin[pick[s]]).astype(BF)
            next_s[s, rows] = inner
            r = mm(x, w_q[:, :, 256:].reshape(D, 256)) + mm(inner, q_b[pick[s], :, 256:])
            c, sn = cosb[s, rows], sinb[s, rows]

            def rot(v):
                return v * c + pltpu.roll(v, 64, 1) * sn

            own = pl.ds(pl.multiple_of(1024 + m * 256, 256), 256)
            kvb[s, 0, own] = rot(r[:, :128]).astype(BF)
            kvb[s, 1, own] = r[:, 128:].astype(BF)

        grid_loop(2, 1, step)

    def queries(s):
        def step(m, unused):
            x = heads_of(nb, s, m)
            rows = rows_of(m)
            r = mm(x, w_q[:, :, :256].reshape(D, 256))
            r = r + mm(next_s[s, rows], q_b[pick[s], :, :256])
            c, sn = cosb[s, rows], sinb[s, rows]
            for j in both:
                v = r[:, j * 128 : (j + 1) * 128]
                v = v * c + pltpu.roll(v, 64, 1) * sn
                qb[s, j, rows] = (v * SCALE).astype(BF)

        grid_loop(2, 1, step)

    def halo(s):
        own = kvb.at[s, :, pl.ds(1024, 512)]
        return [
            net.push(own, kvb.at[s, :, pl.ds(512, 512)], at.next1, halo_ids[2 * s]),
            net.push(own, kvb.at[s, :, pl.ds(0, 512)], at.next2, halo_ids[2 * s + 1]),
        ]

    row = lax.broadcasted_iota(jnp.int32, (256, 1280), 0)
    col = lax.broadcasted_iota(jnp.int32, (256, 1280), 1)

    def allowed(s, m):
        low = startb[s, rows_of(m)] - (b * SPAN - WINDOW + m * 256)
        gap = row - col + WINDOW
        return (gap >= 0) & (gap < WINDOW) & (col >= low)

    def keys_of(m):
        return pl.ds(pl.multiple_of(m * 256, 256), 1280)

    def attend(s, g):
        def step(m, unused):
            rows, keys = rows_of(m), keys_of(m)
            sc = mm_nt(qb[s, g, rows], kvb[s, 0, keys])
            sc = jnp.where(allowed(s, m), sc, -1e30)
            top = jnp.max(sc, axis=-1, keepdims=True)
            e = jnp.exp(sc - top)
            total = jnp.sum(e, axis=-1, keepdims=True)
            p = (e * (1.0 / total)).astype(BF)
            o = mm(p, kvb[s, 1, keys])
            attn[s, rows, g * 128 : (g + 1) * 128] = o.astype(BF)
            lse[s, g, rows] = top + jnp.log(total)

        grid_loop(2, 1, step)

    def out_proj(s):
        put_ext(part1, s, [mm_nt(attn[s], a_b[pick[s]])])
        scatter = Scatter(net, at, part1, s, set1, s_ids[s], CW)
        for m in halves:
            grid_loop(
                1, 4, lambda unused, z: put_part(part1, s, m, z, mm(attn[s, rows_of(m)], w_o[z]))
            )
            scatter.send(m)
        return scatter

    def middle(s, t):
        inn = t[:, D : D + RANK]
        inner_a[s] = inn
        mid = tok[s].astype(F32) + t[:, :D] + mm(inn.astype(BF), aout[pick[s]])
        midf[s] = mid
        n = rms(mid, fgain[...]).astype(BF)
        midn[s] = n
        put_rows(nb, s, at, n)
        return rows_gather(net, at, nb, s, n_ids[s])

    def ffn(s):
        def inner(m, unused):
            x = heads_of(nb, s, m)
            mid_s[s, rows_of(m), :RANK] = mm_nt(x, gin[pick[s]]).astype(BF)
            mid_s[s, rows_of(m), RANK:] = mm_nt(x, uin[pick[s]]).astype(BF)

        grid_loop(2, 1, inner)

        def step(m, n):
            x = heads_of(nb, s, m)
            rows, cols = rows_of(m), cols_of(n)
            g = mm(x, w_g[:, :, cols].reshape(D, 512))
            g = g + mm(mid_s[s, rows, :RANK], g_b[pick[s], :, cols])
            u = mm(x, w_u[:, :, cols].reshape(D, 512))
            u = u + mm(mid_s[s, rows, RANK:], u_b[pick[s], :, cols])
            gate[s, rows, cols] = g.astype(BF)
            up[s, rows, cols] = u.astype(BF)
            hidden[s, rows, cols] = (g * jax.nn.sigmoid(g) * u).astype(BF)

        grid_loop(2, 2, step)

    def hid_back(s, m):
        def step(unused, n):
            x = heads_of(cb, s, m)
            rows, cols = rows_of(m), cols_of(n)
            hb = mm(cot_s[s, rows], d_b[pick[s], :, cols])
            for z in range(4):
                hb = hb + mm_nt(x[:, z * 512 : (z + 1) * 512], w_d[z, cols, :])
            g = gate[s, rows, cols].astype(F32)
            u = up[s, rows, cols].astype(F32)
            sg = jax.nn.sigmoid(g)
            gate[s, rows, cols] = (hb * u * sg * (1.0 + g * (1.0 - sg))).astype(BF)
            up[s, rows, cols] = (hb * g * sg).astype(BF)

        grid_loop(1, 2, step)

    def cot_inner(s):
        def step(m, unused):
            cot_s[s, rows_of(m)] = mm_nt(heads_of(cb, s, m), dout[pick[s]]).astype(BF)

        grid_loop(2, 1, step)

    def mid_scatter(s):
        put_ext(part1, s, [mm_nt(gate[s], g_b[pick[s]]), mm_nt(up[s], u_b[pick[s]])])
        return Scatter(net, at, part1, s, set1, s_ids[s], CW)

    def mid_back(s, m, scatter):
        def step(unused, z):
            rows = rows_of(m)
            put_part(part1, s, m, z, mm_nt(gate[s, rows], w_g[z]) + mm_nt(up[s, rows], w_u[z]))

        grid_loop(1, 4, step)
        scatter.send(m)

    def down(s, m):
        grid_loop(
            1, 4, lambda unused, z: put_part(nb, s, m, z, mm(hidden[s, rows_of(m)], w_d[z]))
        )

    def down_scatter(s):
        put_ext(nb, s, [mm_nt(hidden[s], d_b[pick[s]])])
        scatter = Scatter(net, at, nb, s, set2, t_ids[s], CW)
        for m in halves:
            scatter.send(m)
        return scatter

    def wide_terms(s):
        terms = [
            mm_tn(mid_s[s, :, :RANK], gate[s]),
            mm_tn(mid_s[s, :, RANK:], up[s]),
            mm_tn(cot_s[s], hidden[s]),
        ]
        for i, term in enumerate(terms):
            for j in range(4):
                vec1[3 + 4 * i + j, :, s * 256 : (s + 1) * 256] = term[
                    :, j * 256 : (j + 1) * 256
                ].astype(BF)

    def slices(full, i, s, term):
        for j in range(8):
            full[j, i, :, s * 256 : (s + 1) * 256] = term[:, j * 256 : (j + 1) * 256].astype(BF)

    def middle_back(s, t):
        pg, pu = t[:, D : D + RANK].astype(BF), t[:, D + RANK : D + 2 * RANK].astype(BF)
        back = t[:, :D] + mm(pg, gin[pick[s]]) + mm(pu, uin[pick[s]])
        mg = cot[s].astype(F32) + rms_back(midf[s], fgain[...], back)
        mgrad[s] = mg
        bg = mg.astype(BF)
        put_rows(cb, s, at, bg)
        gather = rows_gather(net, at, cb, s, n_ids[s])
        slices(full1, 0, s, mm_tn(pg, midn[s]))
        slices(full1, 1, s, mm_tn(pu, midn[s]))
        slices(full1, 2, s, mm_tn(inner_a[s].astype(BF), bg))
        return gather

    def attn_back(s):
        def step(m, unused):
            x = heads_of(cb, s, m)
            inner = mm_nt(x, aout[pick[s]]).astype(BF)
            cot_s[s, rows_of(m)] = inner
            r = mm(inner, a_b[pick[s]])
            for z in range(4):
                r = r + mm_nt(x[:, z * 512 : (z + 1) * 512], w_o[z])
            hidden[s, rows_of(m), 512:768] = r.astype(BF)

        grid_loop(2, 1, step)
        vec1[15, :, s * 256 : (s + 1) * 256] = mm_tn(cot_s[s], attn[s]).astype(BF)

    def attend_back(s, g):
        if g == 0:
            dkv[...] = jnp.zeros(dkv.shape, F32)

        def step(m, unused):
            rows, keys = rows_of(m), keys_of(m)
            q, k = qb[s, g, rows], kvb[s, 0, keys]
            do = hidden[s, rows, 512 + g * 128 : 640 + g * 128]
            p = jnp.where(allowed(s, m), jnp.exp(mm_nt(q, k) - lse[s, g, rows]), 0.0)
            vg = mm_nt(do, kvb[s, 1, keys])
            delta = jnp.sum(p * vg, axis=-1, keepdims=True)
            sg = (p * (vg - delta)).astype(BF)
            dq = mm(sg, k) * SCALE
            hidden[s, rows, g * 128 : (g + 1) * 128] = (
                dq * cosb[s, rows] - pltpu.roll(dq, 64, 1) * sinb[s, rows]
            ).astype(BF)
            dkv[0, keys] += mm_tn(sg, q)
            dkv[1, keys] += mm_tn(p.astype(BF), do)

        grid_loop(2, 1, step)

    def halo_back(s):
        copies = []
        for hop in (2, 1, 0):
            for i in both:
                at_col = hop * 256 + i * 128
                gate[s, :, at_col : at_col + 128] = dkv[
                    i, (2 - hop) * SPAN : (3 - hop) * SPAN
                ].astype(BF)
            if hop > 0:
                copies.append(
                    net.push(
                        gate.at[s, :, pl.ds(hop * 256, 256)],
                        halo_in.at[s, hop - 1],
                        at.prev1 if hop == 1 else at.prev2,
                        halo_ids[4 + 2 * s + hop - 1],
                    )
                )
        return copies

    def key_back(s):
        def keys(m, unused):
            rows = rows_of(m)
            dk, dv = [
                gate[s, rows, i * 128 : (i + 1) * 128].astype(F32)
                + halo_in[s, 0, rows, i * 128 : (i + 1) * 128].astype(F32)
                + halo_in[s, 1, rows, i * 128 : (i + 1) * 128].astype(F32)
                for i in both
            ]
            hidden[s, rows, 256:384] = (
                dk * cosb[s, rows] - pltpu.roll(dk, 64, 1) * sinb[s, rows]
            ).astype(BF)
            hidden[s, rows, 384:512] = dv.astype(BF)

        grid_loop(2, 1, keys)

    def p_send(s):
        raw = hidden[s, :, :512]
        px[s] = jnp.zeros(px.shape[1:], BF)
        px[s, :, :, :RANK] = mm_nt(raw, q_b[pick[s]]).astype(BF).reshape(8, TOK, RANK)
        pairs = []
        for k in range(1, 8):
            peer = (h + k) % 8
            pairs.append((px.at[s, peer], px_in.at[s, k - 1], (peer, b)))
        return net.spread(pairs, px_in.at[s], px_ids[s])

    def qkv_back(s, m, scatter):
        grid_loop(
            1, 4,
            lambda unused, z: put_part(part1, s, m, z, mm_nt(hidden[s, rows_of(m), :512], w_q[z])),
        )
        scatter.send(m)

    def qkv_terms(s):
        term = mm_tn(next_s[s], hidden[s, :, :512])
        for j in range(4):
            vec2[s * 8 + 4 + j] = term[:, j * 128 : (j + 1) * 128].astype(BF)

    def finish_result(s, t):
        inn = t[:, D : D + RANK].astype(BF)
        midf[s] = midf[s] + t[:, :D] + mm(inn, dout[pick[s]])
        slices(full2, 1, s, mm_tn(inn, cot[s]))

    def p_sum(s, exchange):
        exchange.wait_recv()
        total = px[s, h].astype(F32)
        for k in range(7):
            total = total + px_in[s, k].astype(F32)
        p = total[:, :RANK].astype(BF)
        slices(full2, 0, s, mm_tn(p, normed[s]))
        return p

    def finish_grad(s, t, p):
        back = t + mm(p, qin[pick[s]])
        mgrad[s] = mgrad[s] + rms_back(tok[s].astype(F32), again[...], back)

    loads[0].wait()
    loads[1].wait()
    W_Q.step(1)
    norm_in(0)
    n0 = rows_gather(net, at, nb, 0, n_ids[0])
    for copy in loads[2:5]:
        copy.wait()
    W_Q.step(2)
    norm_in(1)
    grid_loop(2, 8, table)
    W_Q.step(3)
    W_O.step(1)
    n0.relay()
    n1 = rows_gather(net, at, nb, 1, n_ids[1])
    W_G.step(1)
    W_O.step(2)
    cot_in(0)
    cot_in(1)
    n0.last()
    n1.relay()
    c0 = rows_gather(net, at, cb, 0, c_ids[0])
    W_Q.step(4)
    W_O.step(3)
    W_G.step(2)
    W_U.step(1)
    for copy in loads[5:]:
        copy.wait()
    n0.done()
    W_Q.step(5)
    qkv(0)
    halo0 = halo(0)
    queries(0)
    W_O.step(4)
    W_U.step(2)
    W_D.step(1)
    n1.last()
    c0.relay()
    c1 = rows_gather(net, at, cb, 1, c_ids[1])
    n1.done()
    qkv(1)
    halo1 = halo(1)
    queries(1)
    W_D.step(2)
    W_G.step(3, (0,))
    n0.settle()
    n1.settle()
    c0.last()
    W_O.step(5)
    for copy in halo0:
        copy.wait_recv()
    W_G.step(3, (1,))
    W_U.step(3, (0,))
    attend(0, 0)
    c1.relay()
    attend(0, 1)
    s0 = out_proj(0)
    c1.last()
    s0.merge()
    for copy in halo1:
        copy.wait_recv()
    W_U.step(3, (1,))
    W_D.step(3, (0,))
    attend(1, 0)
    s0.relay()
    W_D.step(3, (1,))
    attend(1, 1)
    s1 = out_proj(1)
    W_G.step(4)
    s1.merge()
    m0 = middle(0, s0.done())
    s1.relay()
    W_U.step(4)
    c0.done()
    c1.done()
    cot_inner(0)
    m0.relay()
    cot_inner(1)
    W_D.step(4)
    m1 = middle(1, s1.done())
    m0.last()
    m0.done()
    m1.relay()
    W_G.step(5)
    W_U.step(5)
    ffn(0)
    W_D.step(5)
    hid_back(0, 0)
    m1.last()
    hid_back(0, 1)
    for item in (c0, c1, m0, m1, W_Q, W_G, W_U):
        item.settle()
    s0 = mid_scatter(0)
    for m in halves:
        mid_back(0, m, s0)
    m1.done()
    s0.merge()
    ffn(1)
    s0.relay()
    hid_back(1, 0)
    hid_back(1, 1)
    s1 = mid_scatter(1)
    mid_back(1, halves[0], s1)
    b0 = middle_back(0, s0.done())
    mid_back(1, halves[1], s1)
    down(0, 0)
    s1.merge()
    down(0, 1)
    r0 = down_scatter(0)
    b0.relay()
    down(1, 0)
    wide_terms(0)
    down(1, 1)
    s1.relay()
    b0.last()
    b0.done()
    attn_back(0)
    b1 = middle_back(1, s1.done())
    fold1.heads()
    attend_back(0, 0)
    attend_back(0, 1)
    back0 = halo_back(0)
    r1 = down_scatter(1)
    wide_terms(1)
    b1.relay()
    r0.merge()
    b1.last()
    vec1[0:3] = fold1.heads_sum().astype(BF)
    b1.done()
    attn_back(1)
    fold1.blocks()
    attend_back(1, 0)
    r0.relay()
    r1.merge()
    attend_back(1, 1)
    back1 = halo_back(1)
    fold1.blocks_sum()
    b0.settle()
    b1.settle()
    r1.relay()
    for copy in back0:
        copy.wait_recv()
    key_back(0)
    x0 = p_send(0)
    s0 = Scatter(net, at, part1, 0, set1, s_ids[0], D)
    for m in halves:
        qkv_back(0, m, s0)
    s0.merge()
    fold1.near_done()
    spread = Weight(net, at, out1, True, q_ids, at.c * 256, 64)
    spread.step(1)
    qkv_terms(0)
    finish_result(0, r0.done())
    finish_result(1, r1.done())
    p0 = p_sum(0, x0)
    spread.step(2)
    for copy in back1:
        copy.wait_recv()
    key_back(1)
    x1 = p_send(1)
    s0.relay()
    spread.step(3)
    s1 = Scatter(net, at, part1, 1, set1, s_ids[1], D)
    qkv_back(1, halves[0], s1)
    p1 = p_sum(1, x1)
    fold2.heads()
    spread.step(4)
    qkv_back(1, halves[1], s1)
    qkv_terms(1)
    s1.merge()
    total = fold2.heads_sum()
    for i in both:
        for s in both:
            for j in both:
                vec2[s * 8 + 2 * i + j] = total[
                    i, :, s * 256 + j * 128 : s * 256 + (j + 1) * 128
                ].astype(BF)
    fold2.blocks()
    s1.relay()
    finish_grad(0, s0.done(), p0)
    spread.step(5)
    fold1.across(across_ids[0])
    fold2.blocks_sum()
    fold2.near_done()
    fold2.far((c_ids[0] + c_ids[1])[:15])
    finish_grad(1, s1.done(), p1)
    fold2.far_done()
    fold2.across(across_ids[1])
    writes = [
        pltpu.make_async_copy(midf, result_o, local.at[0]),
        pltpu.make_async_copy(mgrad, igrad_o, local.at[1]),
        pltpu.make_async_copy(out1, sums1_o, local.at[2]),
        pltpu.make_async_copy(out2, sums2_o, local.at[3]),
    ]
    writes[0].start()
    writes[1].start()
    fold1.done()
    writes[2].start()
    fold2.done()
    writes[3].start()
    net.drain()
    for item in (W_O, W_D, spread):
        item.settle()
    assert net.count == N_SEMS
    for copy in writes:
        copy.wait()


def call_layer(args):
    vm = lambda *shape, t=BF: pltpu.VMEM(shape, t)
    rs = lambda: [vm(2, TOK // 2, CW), vm(2, TOK // 2, CW), vm(2, TOK, CW), vm(2, TOK, CW)]
    outs = [((2, TOK, D), F32), ((2, TOK, D), F32), ((4, 512, 512), BF), ((4, 512, 128), BF)]
    scratch = (
        [vm(4, 512, 512), vm(4, 256, 512), vm(4, 512, 1024), vm(4, 512, 1024), vm(4, 1024, 512)]
        + [vm(2, 4, 2, TOK, CW)] * 3
        + [vm(2, 4, TOK, D + EXT), vm(2, 4, TOK, D + EXT)]
        + rs() + rs()
        + [vm(2, SPAN, 1024)] * 3
        + [vm(2, 2, SPAN, 128), vm(2, 2, 1536, 128), vm(2, SPAN, 256), vm(2, 2, SPAN, 1, t=F32)]
        + [vm(2, SPAN, 128, t=F32)] * 2
        + [vm(2, SPAN, 1, t=jnp.int32)]
        + [vm(2, TOK, D, t=F32), vm(2, TOK, D), vm(2, TOK, D), vm(2, TOK, RANK, t=F32)]
        + [vm(2, TOK, D, t=F32)] + [vm(2, SPAN, RANK), vm(2, SPAN, 2 * RANK), vm(2, SPAN, RANK)]
        + [vm(2, 1536, 128, t=F32), vm(2, 2, SPAN, 256)]
        + [vm(2, RANK, 256), vm(2, RANK, 1024), vm(2, RANK, 512), vm(2, RANK, 1024), vm(2, RANK, 1024)]
        + [vm(8, 3, RANK, 512), vm(7, 3, RANK, 512), vm(16, RANK, 512), vm(15, RANK, 512)]
        + [vm(8, 2, RANK, 512), vm(7, 2, RANK, 512), vm(16, RANK, 128), vm(15, RANK, 128)]
        + [vm(2, 8, TOK, EXT), vm(2, 7, TOK, EXT)]
        + [pltpu.SemaphoreType.DMA((N_SEMS - 75,)), pltpu.SemaphoreType.DMA((N_SEMS,)), pltpu.SemaphoreType.DMA((10,))]
    )
    smem = pl.BlockSpec(memory_space=pltpu.SMEM)
    vmem = pl.BlockSpec(memory_space=pltpu.VMEM)
    hbm = pl.BlockSpec(memory_space=pl.ANY)
    return pl.pallas_call(
        layer,
        out_shape=[jax.ShapeDtypeStruct(shape, kind) for shape, kind in outs],
        in_specs=[smem] * 2 + [vmem] * 5 + [hbm] * 5 + [vmem] * 5 + [hbm] * 5,
        out_specs=[hbm] * len(outs),
        scratch_shapes=scratch,
        compiler_params=pltpu.CompilerParams(
            collective_id=0, has_side_effects=True, vmem_limit_bytes=VMEM_BYTES
        ),
    )(*args)


def unpack(
    index_ref, result, igrad, sums1, sums2,
    result_o, igrad_o, qi_o, qo_o, ai_o, ao_o, gi_o, go_o, ui_o, uo_o, di_o, do_o,
    held, first_in, second_in, narrow, middling, wide, sem,
):
    loads = [
        pltpu.make_async_copy(sums1, first_in, sem.at[0]),
        pltpu.make_async_copy(sums2, second_in, sem.at[1]),
        pltpu.make_async_copy(result, held.at[0], sem.at[2]),
        pltpu.make_async_copy(igrad, held.at[1], sem.at[3]),
    ]
    for copy in loads:
        copy.start()
    swap = index_ref[0] == 1
    stores = []

    def store(src, dst):
        copy = pltpu.make_async_copy(src, dst, sem.at[4 + len(stores)])
        copy.start()
        stores.append(copy)

    def emit(out, cols, first, second):
        first, second = first.astype(F32), second.astype(F32)
        out[0, :, cols] = jnp.where(swap, second, first)
        out[1, :, cols] = jnp.where(swap, first, second)

    def found(ref, j, head, width):
        row0 = (head % 2) * 256 + (j % 4) * 64 + (head // 2) * RANK
        return ref[j // 4, row0 : row0 + RANK, :width]

    loads[0].wait()
    for i, out in enumerate([go_o, uo_o, di_o]):
        for head in range(8):
            for k in range(4):
                block = found(first_in, 3 + 4 * i + k, head, 512)
                cols = pl.ds(head * 1024 + k * 256, 256)
                emit(wide.at[i], cols, block[:, :256], block[:, 256:])
        store(wide.at[i], out)
    loads[2].wait()
    store(held.at[0], result_o)
    loads[3].wait()
    store(held.at[1], igrad_o)
    for i, (j, out) in enumerate([(0, gi_o), (1, ui_o), (2, ao_o), (15, ai_o)]):
        for head in range(8):
            block = found(first_in, j, head, 512)
            emit(narrow.at[i], pl.ds(head * 256, 256), block[:, :256], block[:, 256:])
        store(narrow.at[i], out)
    loads[1].wait()
    for i, (j, out) in enumerate([(0, qi_o), (2, do_o)]):
        for head in range(8):
            for k in range(2):
                cols = pl.ds(head * 256 + k * 128, 128)
                first, second = [found(second_in, j + k + 8 * n, head, 128) for n in (0, 1)]
                emit(narrow.at[4 + i], cols, first, second)
        store(narrow.at[4 + i], out)
    for head in range(8):
        for k in range(4):
            cols = pl.ds(head * 512 + k * 128, 128)
            first, second = [found(second_in, 4 + k + 8 * n, head, 128) for n in (0, 1)]
            emit(middling, cols, first, second)
    store(middling, qo_o)
    for copy in stores:
        copy.wait()


def call_unpack(index, arrays):
    narrow, wide = (2, RANK, D), (2, RANK, 8192)
    outs = [
        (2, TOK, D), (2, TOK, D), narrow, (2, RANK, 4096), narrow, narrow,
        narrow, wide, narrow, wide, wide, narrow,
    ]
    smem = pl.BlockSpec(memory_space=pltpu.SMEM)
    hbm = pl.BlockSpec(memory_space=pl.ANY)
    return pl.pallas_call(
        unpack,
        out_shape=[jax.ShapeDtypeStruct(shape, F32) for shape in outs],
        in_specs=[smem] + [hbm] * 4,
        out_specs=[hbm] * 12,
        scratch_shapes=[
            pltpu.VMEM((2, 2, TOK, D), F32), pltpu.VMEM((4, 512, 512), BF),
            pltpu.VMEM((4, 512, 128), BF), pltpu.VMEM((6,) + narrow, F32),
            pltpu.VMEM((2, RANK, 4096), F32), pltpu.VMEM((3,) + wide, F32),
            pltpu.SemaphoreType.DMA((16,)),
        ],
        compiler_params=pltpu.CompilerParams(vmem_limit_bytes=VMEM_BYTES),
    )(index, *arrays)


def body(
    tokens, cotangent, doc_lengths, adapter_index, attn_gain, ffn_gain,
    w_qkv, w_out, w_gate, w_up, w_down,
    qkv_in, qkv_out, attn_in, attn_out, gate_in, gate_out, up_in, up_out, down_in, down_out,
):
    flip = lambda g: jnp.swapaxes(g, 1, 2)
    half = np.arange(64, dtype=np.float32) * np.float32(2.0 / 128)
    inverse = np.power(np.float32(THETA), -half).astype(np.float32)
    inv = jnp.asarray(np.concatenate([inverse, inverse])[None])
    index = adapter_index.reshape(2)
    arrays = call_layer((
        index, doc_lengths, tokens, cotangent, attn_gain[None], ffn_gain[None], inv,
        w_qkv, w_out, w_gate, w_up, w_down,
        flip(qkv_in), flip(gate_in), flip(up_in), attn_out, down_out, flip(attn_in), flip(down_in),
        qkv_out, gate_out, up_out,
    ))
    result, igrad, qi, qo, ai, ao, gi, go, ui, uo, di, do = call_unpack(index, arrays)
    return (
        result, igrad, flip(qi), qo, flip(ai), ao, flip(gi), go, flip(ui), uo, flip(di), do
    )


def solution(mesh):
    row = P(None, ("blk", "head"), None)
    return jax.shard_map(
        body,
        mesh=mesh,
        in_specs=(row, row) + (P(),) * 4
        + (P("blk", "head"), P("head", "blk"), P("blk", "head"), P("blk", "head"), P("head", "blk"))
        + (P(),) * 10,
        out_specs=(row, row) + (P(),) * 10,
        check_vma=False,
    )
```
